128 devices in a mesh: seq: 32 (over y, z, core), head: 4 (over x).
Axes of the slice: x: 4, y: 4, z: 4, core: 2. Of those that a mesh axis runs over, the one named last changes fastest.
Arguments:
- tokens: bfloat16 [32768, 2048], P(('seq', 'head')), may hold values from -6 to 6
- in_weight: bfloat16 [2048, 16, 160], P(None, 'head'), may hold values from -0.125 to 0.125
- conv_kernel: float32 [3, 16, 160], P(None, 'head'), may hold values from -2.4 to 2.4
- grad_out: bfloat16 [32768, 2048], P('seq', 'head'), may hold values from -6 to 6
Outputs:
- attended: bfloat16 [32768, 2048], P('seq', 'head')
- grad_input: bfloat16 [32768, 2048], P(('seq', 'head'))
- grad_weight: float32 [2048, 16, 160], P('seq', 'head')
The draws below stay inside these ranges and needn't reach their ends.
All inputs are finite; a program needn't handle non-finite values.
Results may differ from the reference program's by a relative error of at most 0.009.
Values may be sent and summed in bfloat16 or wider, within the bound.
A program may use at most 192 MiB of HBM per device.

```python
import math
import jax
import jax.numpy as jnp
from jax import lax

D = 2048
H = 16
F = 16
E = 128
BLK = 256
FEAT = 273
CHAN = 160
L = 32768


def shard_levels(own_key, shape, shards, least, largest):
    factor_of = 1.0
    for axis_at, blocks in shards:
        steps = jax.random.uniform(jax.random.fold_in(jax.random.fold_in(own_key, 6), axis_at), (blocks,), jnp.float32, least / len(shards), largest / len(shards))
        factor_of = factor_of * jnp.repeat(jnp.exp(steps), shape[axis_at] // blocks).reshape((-1,) + (1,) * (len(shape) - 1 - axis_at))
    return factor_of


def centred(own_key, extent, deviation, reach, shards=(), kind=jnp.bfloat16):
    result = deviation * jax.random.normal(own_key, extent, jnp.float32)
    if shards:
        result = result * shard_levels(own_key, extent, shards, -0.22, 0.18)
    return jnp.clip(result, -reach, reach).astype(kind)


def setup_inputs(seed: int = 0) -> dict:
    key_of = jax.random.split(jax.random.key(seed), 5)
    tokens = centred(key_of[0], (L, D), 1.0, 6.0, ((0, 128),))
    in_weight = centred(key_of[1], (D, H, CHAN), D ** -0.5, 0.125, ((1, 4),))
    conv_kernel = centred(key_of[2], (3, H, CHAN), 0.6, 2.4, ((1, 4),), jnp.float32)
    grad_out = centred(key_of[3], (L, H * E), 1.0, 6.0, ((0, 32), (1, 4)))
    return {"tokens": tokens, "in_weight": in_weight, "conv_kernel": conv_kernel, "grad_out": grad_out}


exact_mode = lax.Precision.HIGHEST

def rounded(array):
    return lax.optimization_barrier(array.astype(jnp.bfloat16))

def features(vector):
    leading = vector.shape[:-1]
    square = (vector[..., :, None] * vector[..., None, :]).reshape(leading + (F * F,))
    constant = jnp.ones(leading + (1,), vector.dtype)
    return jnp.concatenate([constant, vector * F ** (-0.25), square * (1.0 / math.sqrt(2.0 * F))], -1)

def feature_grad(vector, grad_phi):
    linear = grad_phi[..., 1:1 + F]
    square = grad_phi[..., 1 + F:].reshape(vector.shape[:-1] + (F, F))
    symmetric = square + jnp.swapaxes(square, -1, -2)
    return linear * F ** (-0.25) + jnp.einsum('...ij,...j->...i', symmetric, vector, precision=exact_mode) * (1.0 / math.sqrt(2.0 * F))

def block_inputs(padded, in_weight, conv_kernel, block_id):
    rows_here = lax.dynamic_slice_in_dim(padded, (block_id * BLK).astype(jnp.int32), BLK + 2, 0)
    projected = jnp.dot(rows_here, in_weight.reshape(D, H * CHAN), preferred_element_type=jnp.float32).reshape(BLK + 2, H, CHAN)
    conved = conv_kernel[0] * projected[2:] + conv_kernel[1] * projected[1:-1] + conv_kernel[2] * projected[:-2]
    query_in = conved[..., :F]
    key_in = conved[..., F:2 * F]
    values = rounded(conved[..., 2 * F:]).astype(jnp.float32)
    feat_q = rounded(features(query_in)).astype(jnp.float32)
    feat_k = rounded(features(key_in)).astype(jnp.float32)
    return (query_in, key_in, values, feat_q, feat_k)

def reference(tokens, in_weight, conv_kernel, grad_out):
    padded = jnp.concatenate([jnp.zeros((2, D), tokens.dtype), tokens], 0)
    causal = lax.broadcasted_iota(jnp.int32, (BLK, BLK), 0) >= lax.broadcasted_iota(jnp.int32, (BLK, BLK), 1)
    block_ids = jnp.arange(L // BLK, dtype=jnp.int32)

    def cotangent_of(block_id):
        piece = lax.dynamic_slice_in_dim(grad_out, (block_id * BLK).astype(jnp.int32), BLK, 0)
        return piece.reshape(BLK, H, E).astype(jnp.float32)

    def score_parts(feat_q, feat_k):
        scores = jnp.where(causal[None], jnp.einsum('thp,shp->hts', feat_q, feat_k), 0.0)
        return (scores, rounded(scores).astype(jnp.float32))

    def mixing_of(grad_num, grad_den, values):
        mixing = jnp.where(causal[None], jnp.einsum('the,she->hts', grad_num, values) + grad_den.T[:, :, None], 0.0)
        return rounded(mixing).astype(jnp.float32)

    def forward_block(carry, block_id):
        state_in, key_total = carry
        query_in, key_in, values, feat_q, feat_k = block_inputs(padded, in_weight, conv_kernel, block_id)
        cotangent = cotangent_of(block_id)
        scores, scores_b = score_parts(feat_q, feat_k)
        state_b = rounded(state_in).astype(jnp.float32)
        numerator = jnp.einsum('thp,hpe->the', feat_q, state_b) + jnp.einsum('hts,she->the', scores_b, values)
        denominator = jnp.einsum('thp,hp->th', feat_q, key_total, precision=exact_mode) + lax.optimization_barrier(jnp.sum(scores, -1)).T
        attended = (numerator / denominator[..., None]).astype(jnp.bfloat16).reshape(BLK, H * E)
        grad_num = rounded(cotangent / denominator[..., None]).astype(jnp.float32)
        grad_den = -lax.optimization_barrier(jnp.sum(cotangent * numerator, -1)) / (denominator * denominator)
        mixing_b = mixing_of(grad_num, grad_den, values)
        grad_fq = jnp.einsum('the,hpe->thp', grad_num, state_b) + grad_den[..., None] * key_total[None] + jnp.einsum('hts,shp->thp', mixing_b, feat_k)
        grad_query = feature_grad(query_in, grad_fq)
        new_state = state_in + jnp.einsum('shp,she->hpe', feat_k, values)
        new_total = key_total + lax.optimization_barrier(jnp.sum(feat_k, 0))
        return ((new_state, new_total), (attended, grad_query, grad_den, denominator))
    start = (jnp.zeros((H, FEAT, E), jnp.float32), jnp.zeros((H, FEAT), jnp.float32))
    unused, (attended, grad_query, grad_dens, dens) = lax.scan(forward_block, start, block_ids)

    def backward_block(carry, block_id):
        later_state, later_total = carry
        query_in, key_in, values, feat_q, feat_k = block_inputs(padded, in_weight, conv_kernel, block_id)
        cotangent = cotangent_of(block_id)
        denominator = dens[block_id]
        grad_den = grad_dens[block_id]
        scores, scores_b = score_parts(feat_q, feat_k)
        grad_num = rounded(cotangent / denominator[..., None]).astype(jnp.float32)
        mixing_b = mixing_of(grad_num, grad_den, values)
        later_b = rounded(later_state).astype(jnp.float32)
        grad_fk = jnp.einsum('she,hpe->shp', values, later_b) + later_total[None] + jnp.einsum('hts,thp->shp', mixing_b, feat_q)
        grad_values = jnp.einsum('shp,hpe->she', feat_k, later_b) + jnp.einsum('hts,the->she', scores_b, grad_num)
        grad_key = feature_grad(key_in, grad_fk)
        new_state = later_state + jnp.einsum('thp,the->hpe', feat_q, grad_num)
        new_total = later_total + jnp.einsum('thp,th->hp', feat_q, grad_den, precision=exact_mode)
        return ((new_state, new_total), (grad_key, grad_values))
    unused, (grad_key, grad_values) = lax.scan(backward_block, start, block_ids, reverse=True)
    grad_conved = jnp.concatenate([grad_query, grad_key, grad_values], -1).reshape(L, H, CHAN)
    padded_grad = jnp.concatenate([grad_conved, jnp.zeros((2, H, CHAN), grad_conved.dtype)], 0)
    grad_proj = conv_kernel[0] * padded_grad[:-2] + conv_kernel[1] * padded_grad[1:-1] + conv_kernel[2] * padded_grad[2:]
    grad_proj = grad_proj.astype(jnp.bfloat16).reshape(L, H * CHAN)
    grad_input = jnp.dot(grad_proj, in_weight.reshape(D, H * CHAN).T, preferred_element_type=jnp.float32).astype(jnp.bfloat16)
    grad_weight = jnp.dot(tokens.T, grad_proj, preferred_element_type=jnp.float32).reshape(D, H, CHAN)
    return (attended.reshape(L, H * E), grad_input, grad_weight)
```

```python
import functools
import math

import jax
import jax.numpy as jnp
import numpy as np
from jax import lax
from jax.experimental import pallas as pl
from jax.experimental.pallas import tpu as pltpu
from jax.sharding import PartitionSpec as P

F = 16
E = 128
BLK = 256
CHAN = 160
FS = 160
NF = 1 + F + F * (F + 1) // 2
KAPPA = 32.0 ** -0.25
f32 = jnp.float32
bf16 = jnp.bfloat16
NN = (((1,), (0,)), ((), ()))
NT = (((1,), (1,)), ((), ()))


def dot(a, b, dims=NN):
    return lax.dot_general(a, b, dims, preferred_element_type=f32)


def bf_parts(value, count):
    parts = []
    rest = np.float64(value)
    for _ in range(count):
        part = np.float64(np.asarray(rest, dtype=jnp.bfloat16))
        parts.append(part)
        rest = rest - part
    return parts


def selection(weighted):
    sel = np.zeros((2 * FS, 3 * F), np.float64)
    sel[0, 32] = 1.0
    sel[FS, 32] = 1.0
    for i in range(F):
        row = 1 + i
        sel[row, i] = sel[row, F + i] = 1.0
        for c, part in enumerate(bf_parts(0.5 / KAPPA, 3)):
            sel[FS + row, 32 + c] = part
    row = 1 + F
    for i in range(F):
        for j in range(i, F):
            first = 2.0 if (weighted and j > i) else 1.0
            sel[row, i] = sel[row, F + i] = first
            sel[FS + row, j] = sel[FS + row, F + j] = 1.0
            row += 1
    return sel


def gradient_map(weighted):
    sel = selection(weighted)
    return np.concatenate([sel[:FS, :F].T, sel[FS:, :F].T], 1)


def remote(src, dst, send, recv, **where):
    return pltpu.make_async_remote_copy(
        src_ref=src,
        dst_ref=dst,
        send_sem=send,
        recv_sem=recv,
        device_id=where,
        device_id_type=pl.DeviceIdType.MESH,
    )


def greet(sem, **where):
    pl.semaphore_signal(sem, inc=1, device_id=where, device_id_type=pl.DeviceIdType.MESH)


def gather_kernel(nx, ns, tok, w, gt, p, g, hal, s_own, r_own, s_fwd, r_fwd, s_hal, r_hal):
    x = lax.axis_index("head")
    s = lax.axis_index("seq")
    left, right, opp = (x + nx - 1) % nx, (x + 1) % nx, (x + 2) % nx
    prev, after = (s + ns - 1) % ns, (s + 1) % ns
    rows, depth = tok.shape
    ch = rows // 4
    bar = pltpu.get_barrier_semaphore()
    greet(bar, head=left)
    greet(bar, head=right)
    greet(bar, seq=prev, head=nx - 1)

    @pl.when(x == nx - 1)
    def _():
        for j in range(nx):
            greet(bar, seq=after, head=j)

    pl.semaphore_wait(bar, jnp.where(x == nx - 1, 3 + nx, 3))

    def part(c):
        return pl.ds(c * ch, ch)

    def own(way, c):
        return remote(
            tok.at[part(c)],
            g.at[x, part(c)],
            s_own.at[way, c],
            r_own.at[way, c],
            head=right if way == 0 else left,
        )

    def arrives(way, c):
        slot = left if way == 0 else right
        return remote(
            tok.at[part(c)], g.at[slot, part(c)], s_own.at[way, c], r_own.at[way, c], head=left
        )

    def forward(way, c):
        slot = left if way == 0 else right
        return remote(
            g.at[slot, part(c)],
            g.at[slot, part(c)],
            s_fwd.at[way, c % 2],
            r_fwd.at[way, c % 2],
            head=right if way == 0 else left,
        )

    def arrives_far(way, c):
        return remote(
            tok.at[part(c)], g.at[opp, part(c)], s_fwd.at[way, c % 2], r_fwd.at[way, c % 2], head=left
        )

    def halo(j):
        return remote(tok.at[pl.ds(rows - 16, 16)], hal, s_hal.at[j], r_hal, seq=after, head=j)

    for c in range(4):
        own(0, c).start()
        own(1, (c + 2) % 4).start()
        if c == 0:

            @pl.when(x == nx - 1)
            def _():
                for j in range(nx):
                    halo(j).start()

    def process(slot, src):
        base = pl.multiple_of(slot * rows, rows)
        p[pl.ds(16 + base, rows), :] = dot(src[...], w[...])

        def turn(i, carry):
            at = pl.ds(pl.multiple_of(i * 256, 256), 256)
            gt[at, pl.ds(base, rows)] = src[:, at].T
            return carry

        lax.fori_loop(0, depth // 256, turn, 0)

    process(x, tok)
    for c in range(2):
        arrives(0, c).wait_recv()
        forward(0, c).start()
        arrives(1, c + 2).wait_recv()
        forward(1, c + 2).start()
    halo(0).wait_recv()
    head_rows = dot(hal[...], w[...])
    p[0:16, :] = jnp.where(s == 0, 0.0, head_rows)
    arrives(0, 2).wait_recv()
    arrives(0, 3).wait_recv()
    process(left, g.at[left])
    arrives(1, 0).wait_recv()
    arrives(1, 1).wait_recv()
    process(right, g.at[right])
    for c in range(2):
        arrives_far(0, c).wait_recv()
        arrives_far(1, c + 2).wait_recv()
    process(opp, g.at[opp])
    for c in range(4):
        own(0, c).wait_send()
        own(1, c).wait_send()
    for c in range(2):
        forward(0, c).wait_send()
        forward(1, c + 2).wait_send()

    @pl.when(x == nx - 1)
    def _():
        for j in range(nx):
            halo(j).wait_send()


def gathered_projection(tokens, w, nx, ns):
    rows, depth = tokens.shape
    width = w.shape[1]
    vm = pl.BlockSpec(memory_space=pltpu.VMEM)
    dma = pltpu.SemaphoreType.DMA
    return pl.pallas_call(
        functools.partial(gather_kernel, nx, ns),
        out_shape=(
            jax.ShapeDtypeStruct((depth, nx * rows), bf16),
            jax.ShapeDtypeStruct((16 + nx * rows, width), f32),
        ),
        in_specs=[vm] * 2,
        out_specs=(vm, vm),
        scratch_shapes=[
            pltpu.VMEM((nx, rows, depth), bf16),
            pltpu.VMEM((16, depth), bf16),
            dma((2, 4)),
            dma((2, 4)),
            dma((2, 2)),
            dma((2, 2)),
            dma((nx,)),
            dma(()),
        ],
        compiler_params=pltpu.CompilerParams(
            collective_id=0, has_side_effects=True, vmem_limit_bytes=56 * 2**20
        ),
    )(tokens, w)


def mixer_kernel(
    ga, gb, nh, nb,
    p, taps, go, selq, selk, gmq, gmk,
    att, gp, hc,
    qkt, vaug, fqt, fkt, fq, fk, ub, nin, sco, scot, gna, run, st, pfk, pgv, gc,
    loc, r1, tot, r2, out, res, s1, q1, s2, q2, s3, q3,
):
    s = lax.axis_index("seq")
    me_a, me_b = s % ga, s // ga
    piece = loc.shape[1] // ga
    hb_count = nh * nb
    bar = pltpu.get_barrier_semaphore()
    for k in range(1, ga):
        greet(bar, seq=me_b * ga + (me_a + k) % ga)
    for k in range(1, gb):
        greet(bar, seq=((me_b + k) % gb) * ga + me_a)

    lane = lax.broadcasted_iota(jnp.int32, (BLK, BLK), 1)
    sub = lax.broadcasted_iota(jnp.int32, (BLK, BLK), 0)
    frow = lax.broadcasted_iota(jnp.int32, (FS, E), 0)

    def rows_of(a):
        return pl.ds(pl.multiple_of(a * piece, 16), piece)

    def first(d, k):
        a = (me_a + k) % ga
        return remote(
            loc.at[d, rows_of(a)], r1.at[d, me_a], s1.at[d, k], q1.at[d, k], seq=me_b * ga + a
        )

    def second(d, k):
        b = (me_b + k) % gb
        return remote(tot.at[d], r2.at[d, me_b], s2.at[d, k], q2.at[d, k], seq=b * ga + me_a)

    def third(d, k):
        a = (me_a + k) % ga
        return remote(
            out.at[d, a], res.at[d, rows_of(me_a)], s3.at[d, k], q3.at[d, k], seq=me_b * ga + a
        )

    def exchange_first(d):
        for k in range(1, ga):
            first(d, k).start()
        r1[d, me_a] = loc[d, rows_of(me_a), :]

    def exchange_second(d):
        for k in range(1, ga):
            a = (me_a + ga - k) % ga
            remote(
                loc.at[d, rows_of(a)], r1.at[d, a], s1.at[d, k], q1.at[d, k], seq=s
            ).wait_recv()
        total = jnp.zeros((piece, E), f32)
        for a in range(ga):
            total = total + r1[d, a].astype(f32)
        tot[d] = total
        for k in range(1, gb):
            second(d, k).start()

    def exchange_third(d):
        for k in range(1, gb):
            b = (me_b + gb - k) % gb
            remote(tot.at[d], r2.at[d, b], s2.at[d, k], q2.at[d, k], seq=s).wait_recv()
        r2[d, me_b] = tot[d]
        total = jnp.zeros((piece, E), f32)
        for b in range(gb):
            ahead = b < me_b if d == 0 else b > me_b
            total = total + jnp.where(ahead, r2[d, b], 0.0)
        for step in range(ga):
            a = step if d == 0 else ga - 1 - step
            out[d, a] = total.astype(bf16)
            total = total + r1[d, a].astype(f32)
        for k in range(1, ga):
            third(d, k).start()
        res[d, rows_of(me_a), :] = out[d, me_a]

    def exchange_done(d):
        for k in range(1, ga):
            a = (me_a + ga - k) % ga
            remote(
                out.at[d, a], res.at[d, rows_of(a)], s3.at[d, k], q3.at[d, k], seq=s
            ).wait_recv()

    def pack(d, h, whole):
        column = jnp.concatenate([whole[:, E:], jnp.zeros((2 * E - FS, E), f32)], 0)
        line = column.T[0:1, :]
        body = jnp.where(frow == NF, line[:, :E], jnp.where(frow == NF + 1, line[:, E:], whole[:, :E]))
        loc[d, h * FS : (h + 1) * FS, :] = body.astype(bf16)

    def unpack(d, h):
        body = res[d, h * FS : (h + 1) * FS, :].astype(f32)
        line = jnp.concatenate([body[NF : NF + 1, :], body[NF + 1 : NF + 2, :]], 1)
        column = jnp.broadcast_to(line, (E, 2 * E)).T[:FS, :]
        return jnp.concatenate([jnp.where(frow < NF, body, 0.0), column], 1)

    def factors(u, sel):
        high = u.astype(bf16)
        low = (u - high.astype(f32)).astype(bf16)
        stack = jnp.concatenate([high, low, jnp.ones((F, BLK), bf16)], 0)
        both = dot(sel[...], stack)
        return both[:FS], both[FS:]

    def block_at(b):
        return pl.ds(pl.multiple_of(b * BLK, BLK), BLK)

    def forward_block(b, carry):
        ext = p[pl.ds(pl.multiple_of(b * BLK, BLK), BLK + 16), :]
        conv = taps[0:1, :] * ext[16:] + taps[1:2, :] * ext[15:-1] + taps[2:3, :] * ext[14:-2]
        turned = conv[:, nh * E :].T
        qkt[:, block_at(b)] = turned
        for h in range(nh):
            i = b * nh + h
            va = jnp.concatenate(
                [conv[:, h * E : (h + 1) * E].astype(bf16), jnp.ones((BLK, E), bf16)], 1
            )
            vaug[i] = va
            first_q, second_q = factors(turned[2 * F * h : 2 * F * h + F], selq)
            first_k, second_k = factors(turned[2 * F * h + F : 2 * F * (h + 1)], selk)
            q = (first_q * second_q).astype(bf16)
            k = (first_k * second_k).astype(bf16)
            fqt[i] = q
            fkt[i] = k
            fq[i] = q.T
            fk[i] = k.T
            ub[i] = dot(k, va)
        return carry

    lax.fori_loop(0, nb, forward_block, 0)
    for h in range(nh):
        whole = ub[h]
        for b in range(1, nb):
            whole = whole + ub[b * nh + h]
        pack(0, h, whole)
    pl.semaphore_wait(bar, ga - 1 + gb - 1)
    exchange_first(0)

    def inside(i, carry):
        score = jnp.where(sub >= lane, dot(fq[i], fkt[i]), 0.0).astype(bf16)
        sco[i] = score
        scot[i] = jnp.where(lane >= sub, dot(fk[i], fqt[i]), 0.0).astype(bf16)
        nin[i] = dot(score, vaug[i])
        return carry

    third_of = hb_count // 4
    lax.fori_loop(0, third_of, inside, 0)
    exchange_second(0)
    lax.fori_loop(third_of, 2 * third_of, inside, 0)
    exchange_third(0)
    lax.fori_loop(2 * third_of, hb_count, inside, 0)
    exchange_done(0)
    for h in range(nh):
        run[h] = unpack(0, h)

    ones = jnp.ones((2 * E, E), bf16)

    def attend_block(b, carry):
        for h in range(nh):
            i = b * nh + h
            state = run[h]
            state_b = state.astype(bf16)
            run[h] = state + ub[i]
            both = dot(fq[i], state_b) + nin[i]
            num = both[:, :E]
            inv = 1.0 / both[:, E:]
            mean = num * inv
            at = (block_at(b), slice(h * E, (h + 1) * E))
            att[at] = mean.astype(bf16)
            scaled = go[at].astype(f32) * inv
            product = scaled * mean
            high = product.astype(bf16)
            low = (product - high.astype(f32)).astype(bf16)
            slope = dot(jnp.concatenate([high, low], 1), ones) * (-1.0 / E)
            ga_b = jnp.concatenate([scaled.astype(bf16), slope.astype(bf16)], 1)
            gna[i] = ga_b
            st[i] = state_b
            ub[i] = dot(fqt[i], ga_b)
        return carry

    lax.fori_loop(0, nb, attend_block, 0)
    for h in range(nh):
        whole = ub[h]
        for b in range(1, nb):
            whole = whole + ub[b * nh + h]
        pack(1, h, whole)
    exchange_first(1)

    def feature_gradient(u, sel, gm, grad):
        one, two = factors(u, sel)
        stack = jnp.concatenate([(grad * two).astype(bf16), (grad * one).astype(bf16)], 0)
        return dot(gm[...], stack)

    def inside_back(i, carry):
        b, h = i // nh, i % nh
        ga_b = gna[i]
        va = vaug[i]
        mix = jnp.where(sub >= lane, dot(ga_b, va, NT), 0.0).astype(bf16)
        mixt = jnp.where(lane >= sub, dot(va, ga_b, NT), 0.0).astype(bf16)
        gfq = dot(st[i], ga_b, NT) + dot(fkt[i], mixt)
        at = (pl.ds(pl.multiple_of(h * 2 * F, 2 * F), F), block_at(b))
        gq = feature_gradient(qkt[at], selq, gmq, gfq)
        pfk[i] = dot(fqt[i], mix)
        qkt[at] = gq
        pgv[i] = dot(scot[i], ga_b[:, :E])
        return carry

    lax.fori_loop(0, third_of, inside_back, 0)
    exchange_second(1)
    lax.fori_loop(third_of, 2 * third_of, inside_back, 0)
    exchange_third(1)
    lax.fori_loop(2 * third_of, hb_count, inside_back, 0)
    exchange_done(1)
    for h in range(nh):
        run[h] = unpack(1, h)

    def back_block(step, carry):
        b = nb - 1 - step
        for h in range(nh):
            i = b * nh + h
            state = run[h]
            state_b = state.astype(bf16)
            run[h] = state + ub[i]
            gfk = dot(state_b, vaug[i], NT) + pfk[i]
            at = (slice(2 * F * h + F, 2 * F * (h + 1)), block_at(b))
            qkt[at] = feature_gradient(qkt[at], selk, gmk, gfk)
            gc[block_at(b), h * E : (h + 1) * E] = dot(fk[i], state_b[:, :E]) + pgv[i]
        gc[block_at(b), nh * E :] = qkt[:, block_at(b)].T
        return carry

    gc[nb * BLK :, :] = jnp.zeros((16, gc.shape[1]), f32)
    lax.fori_loop(0, nb, back_block, 0)

    def spread(b, carry):
        ext = gc[pl.ds(pl.multiple_of(b * BLK, BLK), BLK + 16), :]
        grad = taps[0:1, :] * ext[:BLK] + taps[1:2, :] * ext[1 : BLK + 1] + taps[2:3, :] * ext[2 : BLK + 2]
        gp[block_at(b), :] = grad.astype(bf16)
        return carry

    lax.fori_loop(0, nb, spread, 0)
    edge = jnp.concatenate([jnp.zeros((16, gc.shape[1]), f32), gc[0:16, :]], 0)
    hc[...] = (taps[1:2, :] * edge[1:17] + taps[2:3, :] * edge[2:18]).astype(bf16)

    for d in range(2):
        for k in range(1, ga):
            first(d, k).wait_send()
            third(d, k).wait_send()
        for k in range(1, gb):
            second(d, k).wait_send()


def mixer(p, taps, go, ga, gb):
    rows = go.shape[0]
    nh = go.shape[1] // E
    nb = rows // BLK
    n = nh * nb
    width = p.shape[1]
    piece = nh * FS // ga
    vm = pl.BlockSpec(memory_space=pltpu.VMEM)
    dma = pltpu.SemaphoreType.DMA
    consts = [
        jnp.asarray(selection(True), bf16),
        jnp.asarray(selection(False), bf16),
        jnp.asarray(gradient_map(True), bf16),
        jnp.asarray(gradient_map(False), bf16),
    ]
    return pl.pallas_call(
        functools.partial(mixer_kernel, ga, gb, nh, nb),
        out_shape=(
            jax.ShapeDtypeStruct((rows, nh * E), bf16),
            jax.ShapeDtypeStruct((rows, width), bf16),
            jax.ShapeDtypeStruct((16, width), bf16),
        ),
        in_specs=[vm] * 7,
        out_specs=(vm, vm, vm),
        scratch_shapes=[
            pltpu.VMEM((nh * 2 * F, rows), f32),
            pltpu.VMEM((n, BLK, 2 * E), bf16),
            pltpu.VMEM((n, FS, BLK), bf16),
            pltpu.VMEM((n, FS, BLK), bf16),
            pltpu.VMEM((n, BLK, FS), bf16),
            pltpu.VMEM((n, BLK, FS), bf16),
            pltpu.VMEM((n, FS, 2 * E), f32),
            pltpu.VMEM((n, BLK, 2 * E), f32),
            pltpu.VMEM((n, BLK, BLK), bf16),
            pltpu.VMEM((n, BLK, BLK), bf16),
            pltpu.VMEM((n, BLK, 2 * E), bf16),
            pltpu.VMEM((nh, FS, 2 * E), f32),
            pltpu.VMEM((n, FS, 2 * E), bf16),
            pltpu.VMEM((n, FS, BLK), f32),
            pltpu.VMEM((n, BLK, E), f32),
            pltpu.VMEM((rows + 16, width), f32),
            pltpu.VMEM((2, nh * FS, E), bf16),
            pltpu.VMEM((2, ga, piece, E), bf16),
            pltpu.VMEM((2, piece, E), f32),
            pltpu.VMEM((2, gb, piece, E), f32),
            pltpu.VMEM((2, ga, piece, E), bf16),
            pltpu.VMEM((2, nh * FS, E), bf16),
            dma((2, ga)),
            dma((2, ga)),
            dma((2, gb)),
            dma((2, gb)),
            dma((2, ga)),
            dma((2, ga)),
        ],
        compiler_params=pltpu.CompilerParams(
            collective_id=1, has_side_effects=True, vmem_limit_bytes=60 * 2**20
        ),
    )(p, taps, go, *consts)


def tail_kernel(
    nx, ny, nz,
    gp, hc, gt, wf_hbm,
    gi, gw,
    wf, ga, g3, hal, gwb, rp, t, r2a, r2b, ua, ub, r3a, r3b,
    sw, sx, qx, sh, qh, sp, qp, s2a, q2a, s2b, q2b, s3a, q3a, s3b, q3b,
):
    x = lax.axis_index("head")
    s = lax.axis_index("seq")
    ns = ny * nz * 2
    core, z, y = s % 2, (s // 2) % nz, s // (2 * nz)
    rows = ga.shape[1]
    bar = pltpu.get_barrier_semaphore()

    def at_seq(yy, zz, cc):
        return (yy * nz + zz) * 2 + cc

    sibling = at_seq(y, z, 1 - core)
    prev, after = (s + ns - 1) % ns, (s + 1) % ns
    for k in range(1, nx):
        greet(bar, head=(x + k) % nx)
    greet(bar, seq=prev)
    greet(bar, seq=after)
    greet(bar, seq=sibling)
    for k in range(1, nz):
        greet(bar, seq=at_seq(y, (z + k) % nz, core))
    for k in range(1, ny):
        greet(bar, seq=at_seq((y + k) % ny, z, core))
    weights = [pltpu.make_async_copy(wf_hbm.at[j], wf.at[j], sw.at[j]) for j in range(nx)]
    for copy in weights:
        copy.start()
    pl.semaphore_wait(bar, nx - 1 + 3 + nz - 1 + ny - 1)

    edge = remote(hc, hal, sh, qh, seq=prev)
    edge.start()

    def block(j):
        return pl.ds(pl.multiple_of(j * rows, rows), rows)

    def over(k, last):
        j = (x + k) % nx
        src = g3 if last else gp.at[block(j)]
        return remote(src, ga.at[x], sx.at[k], qx.at[k], head=j)

    for k in (1, 3, 2):

        @pl.when((x + k) % nx != nx - 1)
        def _():
            over(k, False).start()

    edge.wait_recv()
    low = gp[(nx - 1) * rows :, :]
    g3[...] = low
    fixed = low[rows - 16 :].astype(f32) + jnp.where(s == ns - 1, 0.0, hal[...].astype(f32))
    g3[rows - 16 :, :] = fixed.astype(bf16)
    for k in (1, 3, 2):

        @pl.when((x + k) % nx == nx - 1)
        def _():
            over(k, True).start()

    @pl.when(x == nx - 1)
    def _():
        ga[x] = g3[...]

    @pl.when(x != nx - 1)
    def _():
        ga[x] = gp[block(x), :]

    pieces = ny * nz
    height = gwb.shape[2]

    def pair(j):
        return remote(gwb.at[j, 1 - core], rp.at[j], sp.at[j], qp.at[j], seq=sibling)

    per = 256 // (2 * height)
    early = (nx - 1) * rows

    def weight_step(i, carry):
        at = pl.ds(pl.multiple_of(i * 256, 256), 256)
        left = gt[at, :]
        whole = dot(left[:, :early], gp[:early, :]) + dot(left[:, early:], g3[...])
        whole = whole.astype(bf16).reshape(per, 2, height, whole.shape[1])
        for q in range(per):
            gwb[i * per + q] = whole[q]
            pair(i * per + q).start()
        return carry

    lax.fori_loop(0, pieces // per, weight_step, 0)

    def pair_sum(j, carry):
        remote(gwb.at[j, core], rp.at[j], sp.at[j], qp.at[j], seq=sibling).wait_recv()
        t[j // nz, j % nz] = (gwb[j, core].astype(f32) + rp[j].astype(f32)).astype(bf16)
        return carry

    lax.fori_loop(0, pieces, pair_sum, 0)
    half = height // 2
    low_half, high_half = pl.ds(0, half), pl.ds(half, half)

    def go_2a(k):
        to = (z + k) % nz
        return remote(
            t.at[:, to, low_half], r2a.at[k], s2a.at[k], q2a.at[k], seq=at_seq(y, to, core)
        )

    def go_2b(k):
        to = (y + k) % ny
        return remote(
            t.at[to, :, high_half], r2b.at[k], s2b.at[k], q2b.at[k], seq=at_seq(to, z, core)
        )

    def go_3a(k):
        to = (y + k) % ny
        return remote(ua.at[to], r3a.at[k], s3a.at[k], q3a.at[k], seq=at_seq(to, z, core))

    def go_3b(k):
        to = (z + k) % nz
        return remote(ub.at[to], r3b.at[k], s3b.at[k], q3b.at[k], seq=at_seq(y, to, core))

    for k in range(1, max(ny, nz)):
        if k < nz:
            go_2a(k).start()
        if k < ny:
            go_2b(k).start()

    for k in (1, 3, 2):
        j = (x + nx - k) % nx
        remote(g3, ga.at[j], sx.at[k], qx.at[k], head=j).wait_recv()
    for copy in weights:
        copy.wait()

    def input_step(i, carry):
        at = pl.ds(pl.multiple_of(i * 256, 256), 256)
        total = dot(ga[0], wf[0, at, :], NT)
        for j in range(1, nx):
            total = total + dot(ga[j], wf[j, at, :], NT)
        gi[:, at] = total.astype(bf16)
        return carry

    steps = gi.shape[1] // 256
    lax.fori_loop(0, steps // 2, input_step, 0)

    for k in range(1, nz):
        go_2a(k).wait_recv()
    for k in range(1, ny):
        go_2b(k).wait_recv()
    for i in range(ny):
        total = t[i, z, 0:half].astype(f32)
        for k in range(1, nz):
            total = total + r2a[k, i].astype(f32)
        ua[i] = total.astype(bf16)
    for i in range(nz):
        total = t[y, i, half:].astype(f32)
        for k in range(1, ny):
            total = total + r2b[k, i].astype(f32)
        ub[i] = total.astype(bf16)
    for k in range(1, max(ny, nz)):
        if k < ny:
            go_3a(k).start()
        if k < nz:
            go_3b(k).start()
    lax.fori_loop(steps // 2, steps, input_step, 0)
    total = ua[y].astype(f32)
    for k in range(1, ny):
        go_3a(k).wait_recv()
        total = total + r3a[k].astype(f32)
    gw[0:half, :] = total
    total = ub[z].astype(f32)
    for k in range(1, nz):
        go_3b(k).wait_recv()
        total = total + r3b[k].astype(f32)
    gw[half:, :] = total

    edge.wait_send()
    for k in range(1, nx):
        over(k, False).wait_send()
    for j in range(pieces):
        pair(j).wait_send()
    for k in range(1, nz):
        go_2a(k).wait_send()
        go_3b(k).wait_send()
    for k in range(1, ny):
        go_2b(k).wait_send()
        go_3a(k).wait_send()


def tail(gp, hc, gt, wf, nx, ny, nz):
    width = gp.shape[1]
    rows = gp.shape[0] // nx
    depth = gt.shape[0]
    ns = ny * nz * 2
    height = depth // ns
    half = height // 2
    vm = pl.BlockSpec(memory_space=pltpu.VMEM)
    dma = pltpu.SemaphoreType.DMA
    return pl.pallas_call(
        functools.partial(tail_kernel, nx, ny, nz),
        out_shape=(
            jax.ShapeDtypeStruct((rows, depth), bf16),
            jax.ShapeDtypeStruct((height, width), f32),
        ),
        in_specs=[vm] * 3 + [pl.BlockSpec(memory_space=pl.ANY)],
        out_specs=(vm, vm),
        scratch_shapes=[
            pltpu.VMEM((nx, depth, width), bf16),
            pltpu.VMEM((nx, rows, width), bf16),
            pltpu.VMEM((rows, width), bf16),
            pltpu.VMEM((16, width), bf16),
            pltpu.VMEM((ny * nz, 2, height, width), bf16),
            pltpu.VMEM((ny * nz, height, width), bf16),
            pltpu.VMEM((ny, nz, height, width), bf16),
            pltpu.VMEM((nz, ny, half, width), bf16),
            pltpu.VMEM((ny, nz, half, width), bf16),
            pltpu.VMEM((ny, half, width), bf16),
            pltpu.VMEM((nz, half, width), bf16),
            pltpu.VMEM((ny, half, width), bf16),
            pltpu.VMEM((nz, half, width), bf16),
            dma((nx,)),
            dma((nx,)),
            dma((nx,)),
            dma(()),
            dma(()),
            dma((ny * nz,)),
            dma((ny * nz,)),
            dma((nz,)),
            dma((nz,)),
            dma((ny,)),
            dma((ny,)),
            dma((ny,)),
            dma((ny,)),
            dma((nz,)),
            dma((nz,)),
        ],
        compiler_params=pltpu.CompilerParams(
            collective_id=2, has_side_effects=True, vmem_limit_bytes=60 * 2**20
        ),
    )(gp, hc, gt, wf)


def ordered(weight):
    lead = weight.shape[0]
    return jnp.concatenate(
        [weight[:, :, 2 * F :].reshape(lead, -1), weight[:, :, : 2 * F].reshape(lead, -1)], 1
    )


def local(nx, ny, nz, tokens, in_weight, conv_kernel, grad_out):
    depth, nh, _ = in_weight.shape
    ns = ny * nz * 2
    w = ordered(in_weight)
    taps = ordered(conv_kernel)
    scale = jnp.where(jnp.arange(taps.shape[1]) < nh * E, 1.0, KAPPA).astype(f32)
    taps = jnp.pad(taps * scale, ((0, 5), (0, 0)))
    height = depth // ns
    own = lax.dynamic_slice_in_dim(w, lax.axis_index("seq") * height, height, 0)
    wf = lax.all_gather(own, ("head", "seq"), axis=0, tiled=True).reshape(nx, depth, -1)
    gt, p = gathered_projection(tokens, w, nx, ns)
    att, gp, hc = mixer(p, taps, grad_out, nz * 2, ny)
    gi, gw = tail(gp, hc, gt, wf, nx, ny, nz)
    gw = jnp.concatenate(
        [gw[:, nh * E :].reshape(height, nh, 2 * F), gw[:, : nh * E].reshape(height, nh, E)], 2
    )
    return att, gi, gw


def solution(mesh):
    nx, ns = mesh.shape["head"], mesh.shape["seq"]
    ny = math.isqrt(ns // 2)
    nz = ns // 2 // ny
    placed = (
        P(("seq", "head"), None),
        P(None, "head", None),
        P(None, "head", None),
        P("seq", "head"),
    )
    return jax.shard_map(
        functools.partial(local, nx, ny, nz),
        mesh=mesh,
        in_specs=placed,
        out_specs=(P("seq", "head"), P(("seq", "head"), None), P("seq", "head", None)),
        check_vma=False,
    )
```

```python
import functools
import math

import jax
import jax.numpy as jnp
import numpy as np
from jax import lax
from jax.experimental import pallas as pl
from jax.experimental.pallas import tpu as pltpu
from jax.sharding import PartitionSpec as P

F = 16
E = 128
BLK = 256
CHAN = 160
FS = 160
NF = 1 + F + F * (F + 1) // 2
KAPPA = 32.0 ** -0.25
f32 = jnp.float32
bf16 = jnp.bfloat16
NN = (((1,), (0,)), ((), ()))
NT = (((1,), (1,)), ((), ()))


def dot(a, b, dims=NN):
    return lax.dot_general(a, b, dims, preferred_element_type=f32)


def bf_parts(value, count):
    parts = []
    rest = np.float64(value)
    for _ in range(count):
        part = np.float64(np.asarray(rest, dtype=jnp.bfloat16))
        parts.append(part)
        rest = rest - part
    return parts


def selection(weighted):
    sel = np.zeros((2 * FS, 3 * F), np.float64)
    sel[0, 32] = 1.0
    sel[FS, 32] = 1.0
    for i in range(F):
        row = 1 + i
        sel[row, i] = sel[row, F + i] = 1.0
        for c, part in enumerate(bf_parts(0.5 / KAPPA, 3)):
            sel[FS + row, 32 + c] = part
    row = 1 + F
    for i in range(F):
        for j in range(i, F):
            first = 2.0 if (weighted and j > i) else 1.0
            sel[row, i] = sel[row, F + i] = first
            sel[FS + row, j] = sel[FS + row, F + j] = 1.0
            row += 1
    return sel


def gradient_map(weighted):
    sel = selection(weighted)
    return np.concatenate([sel[:FS, :F].T, sel[FS:, :F].T], 1)


def remote(src, dst, send, recv, **where):
    return pltpu.make_async_remote_copy(
        src_ref=src,
        dst_ref=dst,
        send_sem=send,
        recv_sem=recv,
        device_id=where,
        device_id_type=pl.DeviceIdType.MESH,
    )


def greet(sem, **where):
    pl.semaphore_signal(sem, inc=1, device_id=where, device_id_type=pl.DeviceIdType.MESH)


def weight_gather(nx, ny, nz, x, y, z, core, w, wf, sems):
    s1, q1, sa, qa, sb, qb, sc, qc, sd, qd, se, qe, so = sems
    chan, depth = w.shape
    half = chan // 2
    quarter = half // 2
    col = depth // (ny * nz)
    rows_c = pl.ds(pl.multiple_of(core * half, 16), half)
    rows_a = pl.ds(pl.multiple_of(core * half, 16), quarter)
    rows_b = pl.ds(pl.multiple_of(core * half + quarter, 16), quarter)
    far = pl.ds(1, nx - 1)

    def cols(yy, zz):
        return pl.ds(pl.multiple_of((yy * nz + zz) * col, 128), col)

    def row_of(yy):
        return pl.ds(pl.multiple_of(yy * nz * col, 128), nz * col)

    def at_seq(yy, zz, cc):
        return (yy * nz + zz) * 2 + cc

    mine = cols(y, z)

    def spread_x(k):
        return remote(
            w.at[rows_c, mine], wf.at[nx - k, rows_c, mine], s1.at[k], q1.at[k], head=(x + k) % nx
        )

    def a_z(k):
        here = wf.at[far, rows_a, mine]
        return remote(here, here, sa.at[k], qa.at[k], seq=at_seq(y, (z + k) % nz, core))

    def b_y(k):
        here = wf.at[far, rows_b, mine]
        return remote(here, here, sb.at[k], qb.at[k], seq=at_seq((y + k) % ny, z, core))

    def a_y(k):
        here = wf.at[far, rows_a, row_of(y)]
        return remote(here, here, sc.at[k], qc.at[k], seq=at_seq((y + k) % ny, z, core))

    def b_z(k, yy):
        here = wf.at[far, rows_b, cols(yy, z)]
        return remote(here, here, sd.at[k, yy], qd.at[k, yy], seq=at_seq(y, (z + k) % nz, core))

    def across(part):
        here = wf.at[far, rows_a if part == 0 else rows_b]
        return remote(here, here, se.at[part], qe.at[part], seq=at_seq(y, z, 1 - core))

    def own():
        return pltpu.make_async_copy(w, wf.at[0], so)

    def arrived(src, sem, **where):
        remote(src, src, sem, sem, **where).wait_recv()

    def step0():
        for k in range(1, nx):
            spread_x(k).start()
        own().start()

    def step1():
        for k in range(1, nx):
            spread_x(k).wait_recv()
        for k in range(1, max(ny, nz)):
            if k < nz:
                a_z(k).start()
            if k < ny:
                b_y(k).start()

    def step2():
        for k in range(1, nz):
            a_z(k).wait_recv()
        for k in range(1, ny):
            a_y(k).start()
        for k in range(1, ny):
            b_y(k).wait_recv()
        for k in range(1, nz):
            for yy in range(ny):
                b_z(k, yy).start()

    def step3():
        for k in range(1, ny):
            a_y(k).wait_recv()
        across(0).start()
        for k in range(1, nz):
            for yy in range(ny):
                b_z(k, yy).wait_recv()
        across(1).start()

    def step4():
        across(0).wait_recv()
        across(1).wait_recv()
        own().wait()
        for k in range(1, nx):
            spread_x(k).wait_send()
        for k in range(1, nz):
            a_z(k).wait_send()
            for yy in range(ny):
                b_z(k, yy).wait_send()
        for k in range(1, ny):
            b_y(k).wait_send()
            a_y(k).wait_send()
        across(0).wait_send()
        across(1).wait_send()

    return step0, step1, step2, step3, step4


def gather_kernel(
    nx, ny, nz, nh,
    tok, wt,
    gt, p, wf,
    w, g, hal, s_own, r_own, s_fwd, r_fwd, s_hal, r_hal, s_w, *sems,
):
    x = lax.axis_index("head")
    s = lax.axis_index("seq")
    ns = 2 * ny * nz
    core, z, y = s % 2, (s // 2) % nz, s // (2 * nz)
    left, right, opp = (x + nx - 1) % nx, (x + 1) % nx, (x + 2) % nx
    prev, after = (s + ns - 1) % ns, (s + 1) % ns
    rows, depth = tok.shape
    ch = rows // 4
    bar = pltpu.get_barrier_semaphore()
    for k in range(1, nx):
        greet(bar, head=(x + k) % nx)
    greet(bar, seq=prev, head=nx - 1)
    greet(bar, seq=s + 1 - 2 * core)
    for k in range(1, nz):
        greet(bar, seq=(y * nz + (z + k) % nz) * 2 + core)
    for k in range(1, ny):
        greet(bar, seq=(((y + k) % ny) * nz + z) * 2 + core)

    @pl.when(x == nx - 1)
    def _():
        for j in range(nx):
            greet(bar, seq=after, head=j)

    loads = []
    for h in range(nh):
        base = h * CHAN
        loads.append(
            pltpu.make_async_copy(
                wt.at[base + 2 * F : base + CHAN], w.at[h * E : (h + 1) * E], s_w.at[2 * h]
            )
        )
        loads.append(
            pltpu.make_async_copy(
                wt.at[base : base + 2 * F],
                w.at[nh * E + 2 * F * h : nh * E + 2 * F * (h + 1)],
                s_w.at[2 * h + 1],
            )
        )
    for copy in loads:
        copy.start()
    greeted = nx - 1 + 2 + nz - 1 + ny - 1
    pl.semaphore_wait(bar, jnp.where(x == nx - 1, greeted + nx, greeted))

    def part(c):
        return pl.ds(c * ch, ch)

    def own(way, c):
        return remote(
            tok.at[part(c)],
            g.at[x, part(c)],
            s_own.at[way, c],
            r_own.at[way, c],
            head=right if way == 0 else left,
        )

    def arrives(way, c):
        slot = left if way == 0 else right
        return remote(
            tok.at[part(c)], g.at[slot, part(c)], s_own.at[way, c], r_own.at[way, c], head=left
        )

    def forward(way, c):
        slot = left if way == 0 else right
        return remote(
            g.at[slot, part(c)],
            g.at[slot, part(c)],
            s_fwd.at[way, c % 2],
            r_fwd.at[way, c % 2],
            head=right if way == 0 else left,
        )

    def arrives_far(way, c):
        return remote(
            tok.at[part(c)], g.at[opp, part(c)], s_fwd.at[way, c % 2], r_fwd.at[way, c % 2], head=left
        )

    def halo(j):
        return remote(tok.at[pl.ds(rows - 16, 16)], hal, s_hal.at[j], r_hal, seq=after, head=j)

    step0, step1, step2, step3, step4 = weight_gather(nx, ny, nz, x, y, z, core, w, wf, sems)
    for c in range(4):
        own(0, c).start()
        own(1, (c + 2) % 4).start()
        if c == 0:

            @pl.when(x == nx - 1)
            def _():
                for j in range(nx):
                    halo(j).start()

            for copy in loads:
                copy.wait()
            step0()

    def process(slot, src):
        base = pl.multiple_of(slot * rows, rows)
        p[pl.ds(16 + base, rows), :] = dot(src[...], w[...], NT)

        def turn(i, carry):
            at = pl.ds(pl.multiple_of(i * 256, 256), 256)
            gt[at, pl.ds(base, rows)] = src[:, at].T
            return carry

        lax.fori_loop(0, depth // 256, turn, 0)

    step1()
    process(x, tok)
    for c in range(2):
        arrives(0, c).wait_recv()
        forward(0, c).start()
        arrives(1, c + 2).wait_recv()
        forward(1, c + 2).start()
    step2()
    halo(0).wait_recv()
    head_rows = dot(hal[...], w[...], NT)
    p[0:16, :] = jnp.where(s == 0, 0.0, head_rows)
    arrives(0, 2).wait_recv()
    arrives(0, 3).wait_recv()
    process(left, g.at[left])
    arrives(1, 0).wait_recv()
    arrives(1, 1).wait_recv()
    process(right, g.at[right])
    step3()
    for c in range(2):
        arrives_far(0, c).wait_recv()
        arrives_far(1, c + 2).wait_recv()
    process(opp, g.at[opp])
    for c in range(4):
        own(0, c).wait_send()
        own(1, c).wait_send()
    for c in range(2):
        forward(0, c).wait_send()
        forward(1, c + 2).wait_send()

    @pl.when(x == nx - 1)
    def _():
        for j in range(nx):
            halo(j).wait_send()

    step4()


def gathered_projection(tokens, wt, nx, ny, nz, nh):
    rows, depth = tokens.shape
    width = wt.shape[0]
    vm = pl.BlockSpec(memory_space=pltpu.VMEM)
    hbm = pl.BlockSpec(memory_space=pl.ANY)
    dma = pltpu.SemaphoreType.DMA
    return pl.pallas_call(
        functools.partial(gather_kernel, nx, ny, nz, nh),
        out_shape=(
            jax.ShapeDtypeStruct((depth, nx * rows), bf16),
            jax.ShapeDtypeStruct((16 + nx * rows, width), f32),
            jax.ShapeDtypeStruct((nx, width, depth), bf16),
        ),
        in_specs=[vm, hbm],
        out_specs=(vm, vm, hbm),
        scratch_shapes=[
            pltpu.VMEM((width, depth), bf16),
            pltpu.VMEM((nx, rows, depth), bf16),
            pltpu.VMEM((16, depth), bf16),
            dma((2, 4)),
            dma((2, 4)),
            dma((2, 2)),
            dma((2, 2)),
            dma((nx,)),
            dma(()),
            dma((2 * nh,)),
            dma((nx,)),
            dma((nx,)),
            dma((nz,)),
            dma((nz,)),
            dma((ny,)),
            dma((ny,)),
            dma((ny,)),
            dma((ny,)),
            dma((nz, ny)),
            dma((nz, ny)),
            dma((2,)),
            dma((2,)),
            dma(()),
        ],
        compiler_params=pltpu.CompilerParams(
            collective_id=0, has_side_effects=True, vmem_limit_bytes=56 * 2**20
        ),
    )(tokens, wt)


def mixer_kernel(
    ga, gb, nh, nb,
    p, cv, go, selq, selk, gmq, gmk,
    att, gp, hc,
    taps, qkt, vaug, fqt, fkt, fq, fk, ub, nin, scot, gna, run, st, pfk, gc,
    loc, r1, tot, r2, out, res, s1, q1, s2, q2, s3, q3,
):
    s = lax.axis_index("seq")
    me_a, me_b = s % ga, s // ga
    piece = loc.shape[1] // ga
    gh = nh // 2
    per = gh * nb
    bar = pltpu.get_barrier_semaphore()
    for k in range(1, ga):
        greet(bar, seq=me_b * ga + (me_a + k) % ga)
    for k in range(1, gb):
        greet(bar, seq=((me_b + k) % gb) * ga + me_a)

    lane = lax.broadcasted_iota(jnp.int32, (BLK, BLK), 1)
    sub = lax.broadcasted_iota(jnp.int32, (BLK, BLK), 0)
    frow = lax.broadcasted_iota(jnp.int32, (FS, E), 0)

    def rows_of(a):
        return pl.ds(pl.multiple_of(a * piece, 16), piece)

    def first(e, k):
        a = (me_a + k) % ga
        return remote(
            loc.at[e, rows_of(a)], r1.at[e, me_a], s1.at[e, k], q1.at[e, k], seq=me_b * ga + a
        )

    def second(e, k):
        b = (me_b + k) % gb
        return remote(tot.at[e], r2.at[e, me_b], s2.at[e, k], q2.at[e, k], seq=b * ga + me_a)

    def third(e, k):
        a = (me_a + k) % ga
        return remote(
            out.at[e, a], res.at[e, rows_of(me_a)], s3.at[e, k], q3.at[e, k], seq=me_b * ga + a
        )

    def exchange_first(e):
        for k in range(1, ga):
            first(e, k).start()
        r1[e, me_a] = loc[e, rows_of(me_a), :]

    def exchange_second(e):
        for k in range(1, ga):
            a = (me_a + ga - k) % ga
            remote(
                loc.at[e, rows_of(a)], r1.at[e, a], s1.at[e, k], q1.at[e, k], seq=s
            ).wait_recv()
        total = jnp.zeros((piece, E), f32)
        for a in range(ga):
            total = total + r1[e, a].astype(f32)
        tot[e] = total.astype(bf16)
        for k in range(1, gb):
            second(e, k).start()

    def exchange_third(e):
        for k in range(1, gb):
            b = (me_b + gb - k) % gb
            remote(tot.at[e], r2.at[e, b], s2.at[e, k], q2.at[e, k], seq=s).wait_recv()
        r2[e, me_b] = tot[e]
        total = jnp.zeros((piece, E), f32)
        for b in range(gb):
            ahead = b < me_b if e < 2 else b > me_b
            total = total + jnp.where(ahead, r2[e, b].astype(f32), 0.0)
        for step in range(ga):
            a = step if e < 2 else ga - 1 - step
            out[e, a] = total.astype(bf16)
            total = total + r1[e, a].astype(f32)
        for k in range(1, ga):
            third(e, k).start()
        res[e, rows_of(me_a), :] = out[e, me_a]

    def exchange_done(e):
        for k in range(1, ga):
            a = (me_a + ga - k) % ga
            remote(
                out.at[e, a], res.at[e, rows_of(a)], s3.at[e, k], q3.at[e, k], seq=s
            ).wait_recv()

    def pack(e, h, whole):
        column = jnp.concatenate([whole[:, E:], jnp.zeros((2 * E - FS, E), f32)], 0)
        line = column.T[0:1, :]
        body = jnp.where(frow == NF, line[:, :E], jnp.where(frow == NF + 1, line[:, E:], whole[:, :E]))
        loc[e, h * FS : (h + 1) * FS, :] = body.astype(bf16)

    def pack_group(e):
        for j in range(gh):
            h = (e % 2) * gh + j
            whole = ub[h * nb]
            for b in range(1, nb):
                whole = whole + ub[h * nb + b]
            pack(e, j, whole)
        if gh * FS < loc.shape[1]:
            loc[e, gh * FS :, :] = jnp.zeros((loc.shape[1] - gh * FS, E), bf16)

    def unpack_group(e):
        for j in range(gh):
            body = res[e, j * FS : (j + 1) * FS, :].astype(f32)
            line = jnp.concatenate([body[NF : NF + 1, :], body[NF + 1 : NF + 2, :]], 1)
            column = jnp.broadcast_to(line, (E, 2 * E)).T[:FS, :]
            run[(e % 2) * gh + j] = jnp.concatenate([jnp.where(frow < NF, body, 0.0), column], 1)

    def factors(u, sel):
        high = u.astype(bf16)
        low = (u - high.astype(f32)).astype(bf16)
        stack = jnp.concatenate([high, low, jnp.ones((F, BLK), bf16)], 0)
        both = dot(sel[...], stack)
        return both[:FS], both[FS:]

    def block_at(b):
        return pl.ds(pl.multiple_of(b * BLK, BLK), BLK)

    for j in range(3):
        lines = [cv[j, h : h + 1, :] for h in range(nh)]
        for h in range(nh):
            taps[j : j + 1, h * E : (h + 1) * E] = lines[h][:, 2 * F :]
        taps[j : j + 1, nh * E :] = jnp.concatenate([v[:, : 2 * F] for v in lines], 1) * KAPPA

    def convolve(b, carry):
        ext = p[pl.ds(pl.multiple_of(b * BLK, BLK), BLK + 16), :]
        conv = taps[0:1, :] * ext[16:] + taps[1:2, :] * ext[15:-1] + taps[2:3, :] * ext[14:-2]
        qkt[:, block_at(b)] = conv[:, nh * E :].T
        for h in range(nh):
            vaug[h * nb + b] = jnp.concatenate(
                [conv[:, h * E : (h + 1) * E].astype(bf16), jnp.ones((BLK, E), bf16)], 1
            )
        return carry

    lax.fori_loop(0, nb, convolve, 0)

    def featurize(group):
        def block(b, carry):
            for j in range(gh):
                h = group * gh + j
                i = h * nb + b
                at = block_at(b)
                first_q, second_q = factors(qkt[2 * F * h : 2 * F * h + F, at], selq)
                first_k, second_k = factors(qkt[2 * F * h + F : 2 * F * (h + 1), at], selk)
                q = (first_q * second_q).astype(bf16)
                k = (first_k * second_k).astype(bf16)
                fqt[i] = q
                fkt[i] = k
                fq[i] = q.T
                fk[i] = k.T
                ub[i] = dot(k, vaug[i])
            return carry

        lax.fori_loop(0, nb, block, 0)
        pack_group(group)

    featurize(0)
    pl.semaphore_wait(bar, ga - 1 + gb - 1)
    exchange_first(0)
    featurize(1)
    exchange_first(1)

    def inside(i, carry):
        score = jnp.where(sub >= lane, dot(fq[i], fkt[i]), 0.0).astype(bf16)
        scot[i] = jnp.where(lane >= sub, dot(fk[i], fqt[i]), 0.0).astype(bf16)
        nin[i] = dot(score, vaug[i])
        return carry

    def quarter(n, body):
        lax.fori_loop(n * per // 2, (n + 1) * per // 2, body, 0, unroll=True)

    quarter(0, inside)
    exchange_second(0)
    quarter(1, inside)
    exchange_second(1)
    quarter(2, inside)
    exchange_third(0)
    quarter(3, inside)
    exchange_third(1)

    ones = jnp.ones((2 * E, E), bf16)

    def attend(group):
        def block(b, carry):
            for j in range(gh):
                h = group * gh + j
                i = h * nb + b
                state = run[h]
                state_b = state.astype(bf16)
                run[h] = state + ub[i]
                both = dot(fq[i], state_b) + nin[i]
                num = both[:, :E]
                inv = 1.0 / both[:, E:]
                mean = num * inv
                at = (block_at(b), slice(h * E, (h + 1) * E))
                att[at] = mean.astype(bf16)
                scaled = go[at].astype(f32) * inv
                product = scaled * mean
                high = product.astype(bf16)
                low = (product - high.astype(f32)).astype(bf16)
                slope = dot(jnp.concatenate([high, low], 1), ones) * (-1.0 / E)
                ga_b = jnp.concatenate([scaled.astype(bf16), slope.astype(bf16)], 1)
                gna[i] = ga_b
                st[i] = state_b
                ub[i] = dot(fqt[i], ga_b)
            return carry

        lax.fori_loop(0, nb, block, 0)
        pack_group(2 + group)

    for group in range(2):
        exchange_done(group)
        unpack_group(group)
        attend(group)
        exchange_first(2 + group)

    def feature_gradient(u, sel, gm, grad):
        one, two = factors(u, sel)
        stack = jnp.concatenate([(grad * two).astype(bf16), (grad * one).astype(bf16)], 0)
        return dot(gm[...], stack)

    def inside_back(i, carry):
        h, b = i // nb, i % nb
        ga_b = gna[i]
        va = vaug[i]
        mix = jnp.where(sub >= lane, dot(ga_b, va, NT), 0.0).astype(bf16)
        mixt = jnp.where(lane >= sub, dot(va, ga_b, NT), 0.0).astype(bf16)
        gfq = dot(st[i], ga_b, NT) + dot(fkt[i], mixt)
        at = (pl.ds(pl.multiple_of(h * 2 * F, 2 * F), F), block_at(b))
        gq = feature_gradient(qkt[at], selq, gmq, gfq)
        pfk[i] = dot(fqt[i], mix)
        qkt[at] = gq
        nin[i, :, :E] = dot(scot[i], ga_b[:, :E])
        return carry

    quarter(0, inside_back)
    exchange_second(2)
    quarter(1, inside_back)
    exchange_second(3)
    quarter(2, inside_back)
    exchange_third(2)
    quarter(3, inside_back)
    exchange_third(3)

    def finish(group):
        def block(step, carry):
            b = nb - 1 - step
            for j in range(gh):
                h = group * gh + j
                i = h * nb + b
                state = run[h]
                state_b = state.astype(bf16)
                run[h] = state + ub[i]
                gfk = dot(state_b, vaug[i], NT) + pfk[i]
                at = (slice(2 * F * h + F, 2 * F * (h + 1)), block_at(b))
                qkt[at] = feature_gradient(qkt[at], selk, gmk, gfk)
                gc[block_at(b), h * E : (h + 1) * E] = dot(fk[i], state_b[:, :E]) + nin[i, :, :E]
            return carry

        lax.fori_loop(0, nb, block, 0)

    for group in range(2):
        exchange_done(2 + group)
        unpack_group(2 + group)
        finish(group)

    gc[nb * BLK :, :] = jnp.zeros((16, gc.shape[1]), f32)
    for b in range(nb):
        gc[b * BLK : (b + 1) * BLK, nh * E :] = qkt[:, b * BLK : (b + 1) * BLK].T

    def spread(b, carry):
        ext = gc[pl.ds(pl.multiple_of(b * BLK, BLK), BLK + 16), :]
        grad = taps[0:1, :] * ext[:BLK] + taps[1:2, :] * ext[1 : BLK + 1] + taps[2:3, :] * ext[2 : BLK + 2]
        gp[block_at(b), :] = grad.astype(bf16)
        return carry

    lax.fori_loop(0, nb, spread, 0)
    edge = jnp.concatenate([jnp.zeros((16, gc.shape[1]), f32), gc[0:16, :]], 0)
    hc[...] = (taps[1:2, :] * edge[1:17] + taps[2:3, :] * edge[2:18]).astype(bf16)

    for e in range(4):
        for k in range(1, ga):
            first(e, k).wait_send()
            third(e, k).wait_send()
        for k in range(1, gb):
            second(e, k).wait_send()


def mixer(p, cv, go, ga, gb):
    rows = go.shape[0]
    nh = go.shape[1] // E
    nb = rows // BLK
    n = nh * nb
    width = p.shape[1]
    piece = -(-(nh // 2) * FS // (16 * ga)) * 16
    vm = pl.BlockSpec(memory_space=pltpu.VMEM)
    dma = pltpu.SemaphoreType.DMA
    consts = [
        jnp.asarray(selection(True), bf16),
        jnp.asarray(selection(False), bf16),
        jnp.asarray(gradient_map(True), bf16),
        jnp.asarray(gradient_map(False), bf16),
    ]
    return pl.pallas_call(
        functools.partial(mixer_kernel, ga, gb, nh, nb),
        out_shape=(
            jax.ShapeDtypeStruct((rows, nh * E), bf16),
            jax.ShapeDtypeStruct((rows, width), bf16),
            jax.ShapeDtypeStruct((16, width), bf16),
        ),
        in_specs=[vm] * 7,
        out_specs=(vm, vm, vm),
        scratch_shapes=[
            pltpu.VMEM((8, width), f32),
            pltpu.VMEM((nh * 2 * F, rows), f32),
            pltpu.VMEM((n, BLK, 2 * E), bf16),
            pltpu.VMEM((n, FS, BLK), bf16),
            pltpu.VMEM((n, FS, BLK), bf16),
            pltpu.VMEM((n, BLK, FS), bf16),
            pltpu.VMEM((n, BLK, FS), bf16),
            pltpu.VMEM((n, FS, 2 * E), f32),
            pltpu.VMEM((n, BLK, 2 * E), f32),
            pltpu.VMEM((n, BLK, BLK), bf16),
            pltpu.VMEM((n, BLK, 2 * E), bf16),
            pltpu.VMEM((nh, FS, 2 * E), f32),
            pltpu.VMEM((n, FS, 2 * E), bf16),
            pltpu.VMEM((n, FS, BLK), f32),
            pltpu.VMEM((rows + 16, width), f32),
            pltpu.VMEM((4, ga * piece, E), bf16),
            pltpu.VMEM((4, ga, piece, E), bf16),
            pltpu.VMEM((4, piece, E), bf16),
            pltpu.VMEM((4, gb, piece, E), bf16),
            pltpu.VMEM((4, ga, piece, E), bf16),
            pltpu.VMEM((4, ga * piece, E), bf16),
            dma((4, ga)),
            dma((4, ga)),
            dma((4, gb)),
            dma((4, gb)),
            dma((4, ga)),
            dma((4, ga)),
        ],
        compiler_params=pltpu.CompilerParams(
            collective_id=1, has_side_effects=True, vmem_limit_bytes=60 * 2**20
        ),
    )(p, cv, go, *consts)


def tail_kernel(
    nx, ny, nz,
    gp, hc, gt, wf_hbm,
    gi, gw,
    wf, ga, g3, hal, gwb, rp, t, r2a, r2b, ua, ub, r3a, r3b,
    sw, sx, qx, sh, qh, sp, qp, s2a, q2a, s2b, q2b, s3a, q3a, s3b, q3b,
):
    x = lax.axis_index("head")
    s = lax.axis_index("seq")
    ns = ny * nz * 2
    core, z, y = s % 2, (s // 2) % nz, s // (2 * nz)
    rows = ga.shape[1]
    bar = pltpu.get_barrier_semaphore()

    def at_seq(yy, zz, cc):
        return (yy * nz + zz) * 2 + cc

    sibling = at_seq(y, z, 1 - core)
    prev, after = (s + ns - 1) % ns, (s + 1) % ns
    for k in range(1, nx):
        greet(bar, head=(x + k) % nx)
    greet(bar, seq=prev)
    greet(bar, seq=after)
    greet(bar, seq=sibling)
    for k in range(1, nz):
        greet(bar, seq=at_seq(y, (z + k) % nz, core))
    for k in range(1, ny):
        greet(bar, seq=at_seq((y + k) % ny, z, core))
    weights = [pltpu.make_async_copy(wf_hbm.at[j], wf.at[j], sw.at[j]) for j in range(nx)]
    for copy in weights:
        copy.start()
    pl.semaphore_wait(bar, nx - 1 + 3 + nz - 1 + ny - 1)

    edge = remote(hc, hal, sh, qh, seq=prev)
    edge.start()

    def block(j):
        return pl.ds(pl.multiple_of(j * rows, rows), rows)

    def over(k, last):
        j = (x + k) % nx
        src = g3 if last else gp.at[block(j)]
        return remote(src, ga.at[nx - k], sx.at[k], qx.at[nx - k], head=j)

    for k in (1, 3, 2):

        @pl.when((x + k) % nx != nx - 1)
        def _():
            over(k, False).start()

    edge.wait_recv()
    low = gp[(nx - 1) * rows :, :]
    g3[...] = low
    fixed = low[rows - 16 :].astype(f32) + jnp.where(s == ns - 1, 0.0, hal[...].astype(f32))
    g3[rows - 16 :, :] = fixed.astype(bf16)
    for k in (1, 3, 2):

        @pl.when((x + k) % nx == nx - 1)
        def _():
            over(k, True).start()

    @pl.when(x == nx - 1)
    def _():
        ga[0] = g3[...]

    @pl.when(x != nx - 1)
    def _():
        ga[0] = gp[block(x), :]

    pieces = ny * nz
    height = gwb.shape[2]

    def pair(j):
        return remote(gwb.at[j, 1 - core], rp.at[j], sp.at[j], qp.at[j], seq=sibling)

    per = 256 // (2 * height)
    early = (nx - 1) * rows

    def weight_step(i, carry):
        at = pl.ds(pl.multiple_of(i * 256, 256), 256)
        left = gt[at, :]
        whole = dot(left[:, :early], gp[:early, :]) + dot(left[:, early:], g3[...])
        whole = whole.astype(bf16).reshape(per, 2, height, whole.shape[1])
        for q in range(per):
            gwb[i * per + q] = whole[q]
            pair(i * per + q).start()
        return carry

    lax.fori_loop(0, pieces // per, weight_step, 0)

    def pair_sum(j, carry):
        remote(gwb.at[j, core], rp.at[j], sp.at[j], qp.at[j], seq=sibling).wait_recv()
        t[j // nz, j % nz] = (gwb[j, core].astype(f32) + rp[j].astype(f32)).astype(bf16)
        return carry

    lax.fori_loop(0, pieces, pair_sum, 0)
    half = height // 2
    low_half, high_half = pl.ds(0, half), pl.ds(half, half)

    def go_2a(k):
        to = (z + k) % nz
        return remote(
            t.at[:, to, low_half], r2a.at[k], s2a.at[k], q2a.at[k], seq=at_seq(y, to, core)
        )

    def go_2b(k):
        to = (y + k) % ny
        return remote(
            t.at[to, :, high_half], r2b.at[k], s2b.at[k], q2b.at[k], seq=at_seq(to, z, core)
        )

    def go_3a(k):
        to = (y + k) % ny
        return remote(ua.at[to], r3a.at[k], s3a.at[k], q3a.at[k], seq=at_seq(to, z, core))

    def go_3b(k):
        to = (z + k) % nz
        return remote(ub.at[to], r3b.at[k], s3b.at[k], q3b.at[k], seq=at_seq(y, to, core))

    for k in range(1, max(ny, nz)):
        if k < nz:
            go_2a(k).start()
        if k < ny:
            go_2b(k).start()

    for k in (1, 3, 2):
        remote(g3, ga.at[k], sx.at[k], qx.at[k], head=(x + k) % nx).wait_recv()
    for copy in weights:
        copy.wait()

    def input_step(i, carry):
        at = pl.ds(pl.multiple_of(i * 256, 256), 256)
        total = dot(ga[0], wf[0, :, at])
        for j in range(1, nx):
            total = total + dot(ga[j], wf[j, :, at])
        gi[:, at] = total.astype(bf16)
        return carry

    steps = gi.shape[1] // 256
    lax.fori_loop(0, steps // 2, input_step, 0)

    for k in range(1, nz):
        go_2a(k).wait_recv()
    for k in range(1, ny):
        go_2b(k).wait_recv()
    for i in range(ny):
        total = t[i, z, 0:half].astype(f32)
        for k in range(1, nz):
            total = total + r2a[k, i].astype(f32)
        ua[i] = total.astype(bf16)
    for i in range(nz):
        total = t[y, i, half:].astype(f32)
        for k in range(1, ny):
            total = total + r2b[k, i].astype(f32)
        ub[i] = total.astype(bf16)
    for k in range(1, max(ny, nz)):
        if k < ny:
            go_3a(k).start()
        if k < nz:
            go_3b(k).start()
    lax.fori_loop(steps // 2, steps, input_step, 0)
    nh = gw.shape[1]

    def put(at, total):
        for h in range(nh):
            narrow = total[:, nh * E + 2 * F * h : nh * E + 2 * F * (h + 1)]
            gw[at, h, :] = jnp.concatenate([narrow, total[:, h * E : (h + 1) * E]], 1)

    total = ua[y].astype(f32)
    for k in range(1, ny):
        go_3a(k).wait_recv()
        total = total + r3a[k].astype(f32)
    put(slice(0, half), total)
    total = ub[z].astype(f32)
    for k in range(1, nz):
        go_3b(k).wait_recv()
        total = total + r3b[k].astype(f32)
    put(slice(half, height), total)

    edge.wait_send()
    for k in range(1, nx):
        over(k, False).wait_send()
    for j in range(pieces):
        pair(j).wait_send()
    for k in range(1, nz):
        go_2a(k).wait_send()
        go_3b(k).wait_send()
    for k in range(1, ny):
        go_2b(k).wait_send()
        go_3a(k).wait_send()


def tail(gp, hc, gt, wf, nx, ny, nz):
    width = gp.shape[1]
    rows = gp.shape[0] // nx
    depth = gt.shape[0]
    ns = ny * nz * 2
    height = depth // ns
    half = height // 2
    vm = pl.BlockSpec(memory_space=pltpu.VMEM)
    dma = pltpu.SemaphoreType.DMA
    return pl.pallas_call(
        functools.partial(tail_kernel, nx, ny, nz),
        out_shape=(
            jax.ShapeDtypeStruct((rows, depth), bf16),
            jax.ShapeDtypeStruct((height, width // CHAN, CHAN), f32),
        ),
        in_specs=[vm] * 3 + [pl.BlockSpec(memory_space=pl.ANY)],
        out_specs=(vm, vm),
        scratch_shapes=[
            pltpu.VMEM((nx, width, depth), bf16),
            pltpu.VMEM((nx, rows, width), bf16),
            pltpu.VMEM((rows, width), bf16),
            pltpu.VMEM((16, width), bf16),
            pltpu.VMEM((ny * nz, 2, height, width), bf16),
            pltpu.VMEM((ny * nz, height, width), bf16),
            pltpu.VMEM((ny, nz, height, width), bf16),
            pltpu.VMEM((nz, ny, half, width), bf16),
            pltpu.VMEM((ny, nz, half, width), bf16),
            pltpu.VMEM((ny, half, width), bf16),
            pltpu.VMEM((nz, half, width), bf16),
            pltpu.VMEM((ny, half, width), bf16),
            pltpu.VMEM((nz, half, width), bf16),
            dma((nx,)),
            dma((nx,)),
            dma((nx,)),
            dma(()),
            dma(()),
            dma((ny * nz,)),
            dma((ny * nz,)),
            dma((nz,)),
            dma((nz,)),
            dma((ny,)),
            dma((ny,)),
            dma((ny,)),
            dma((ny,)),
            dma((nz,)),
            dma((nz,)),
        ],
        compiler_params=pltpu.CompilerParams(
            collective_id=2, has_side_effects=True, vmem_limit_bytes=60 * 2**20
        ),
    )(gp, hc, gt, wf)


def local(nx, ny, nz, tokens, in_weight, conv_kernel, grad_out):
    depth, nh, _ = in_weight.shape
    wt = jnp.transpose(in_weight, (1, 2, 0)).reshape(nh * CHAN, depth)
    gt, p, wf = gathered_projection(tokens, wt, nx, ny, nz, nh)
    att, gp, hc = mixer(p, conv_kernel, grad_out, nz * 2, ny)
    gi, gw = tail(gp, hc, gt, wf, nx, ny, nz)
    return att, gi, gw


def solution(mesh):
    nx, ns = mesh.shape["head"], mesh.shape["seq"]
    ny = math.isqrt(ns // 2)
    nz = ns // 2 // ny
    placed = (
        P(("seq", "head"), None),
        P(None, "head", None),
        P(None, "head", None),
        P("seq", "head"),
    )
    return jax.shard_map(
        functools.partial(local, nx, ny, nz),
        mesh=mesh,
        in_specs=placed,
        out_specs=(P("seq", "head"), P(("seq", "head"), None), P("seq", "head", None)),
        check_vma=False,
    )
```

```python
import functools
import math

import jax
import jax.numpy as jnp
import numpy as np
from jax import lax
from jax.experimental import pallas as pl
from jax.experimental.pallas import tpu as pltpu
from jax.sharding import PartitionSpec as P

F = 16
E = 128
BLK = 256
CHAN = 160
FS = 160
NF = 1 + F + F * (F + 1) // 2
KAPPA = 32.0 ** -0.25
f32 = jnp.float32
bf16 = jnp.bfloat16
NN = (((1,), (0,)), ((), ()))
NT = (((1,), (1,)), ((), ()))


def dot(a, b, dims=NN):
    return lax.dot_general(a, b, dims, preferred_element_type=f32)


def bf_parts(value, count):
    parts = []
    rest = np.float64(value)
    for _ in range(count):
        part = np.float64(np.asarray(rest, dtype=jnp.bfloat16))
        parts.append(part)
        rest = rest - part
    return parts


def selection(weighted):
    sel = np.zeros((2 * FS, 3 * F), np.float64)
    sel[0, 32] = 1.0
    sel[FS, 32] = 1.0
    for i in range(F):
        row = 1 + i
        sel[row, i] = sel[row, F + i] = 1.0
        for c, part in enumerate(bf_parts(0.5 / KAPPA, 3)):
            sel[FS + row, 32 + c] = part
    row = 1 + F
    for i in range(F):
        for j in range(i, F):
            first = 2.0 if (weighted and j > i) else 1.0
            sel[row, i] = sel[row, F + i] = first
            sel[FS + row, j] = sel[FS + row, F + j] = 1.0
            row += 1
    return sel


def gradient_map(weighted):
    sel = selection(weighted)
    return np.concatenate([sel[:FS, :F].T, sel[FS:, :F].T], 1)


def remote(src, dst, send, recv, **where):
    return pltpu.make_async_remote_copy(
        src_ref=src,
        dst_ref=dst,
        send_sem=send,
        recv_sem=recv,
        device_id=where,
        device_id_type=pl.DeviceIdType.MESH,
    )


def greet(sem, **where):
    pl.semaphore_signal(sem, inc=1, device_id=where, device_id_type=pl.DeviceIdType.MESH)


def weight_gather(nx, ny, nz, x, y, z, core, w, wf, sems):
    s1, q1, sa, qa, sb, qb, sc, qc, sd, qd, se, qe = sems
    chan, depth = w.shape
    half = chan // 2
    quarter = half // 2
    col = depth // (ny * nz)
    rows_c = pl.ds(pl.multiple_of(core * half, 16), half)
    rows_a = pl.ds(pl.multiple_of(core * half, 16), quarter)
    rows_b = pl.ds(pl.multiple_of(core * half + quarter, 16), quarter)
    far = pl.ds(0, nx - 1)

    def cols(yy, zz):
        return pl.ds(pl.multiple_of((yy * nz + zz) * col, 128), col)

    def row_of(yy):
        return pl.ds(pl.multiple_of(yy * nz * col, 128), nz * col)

    def at_seq(yy, zz, cc):
        return (yy * nz + zz) * 2 + cc

    mine = cols(y, z)

    def spread_x(k):
        return remote(
            w.at[rows_c, mine], wf.at[nx - k - 1, rows_c, mine], s1.at[k], q1.at[k], head=(x + k) % nx
        )

    def a_z(k):
        here = wf.at[far, rows_a, mine]
        return remote(here, here, sa.at[k], qa.at[k], seq=at_seq(y, (z + k) % nz, core))

    def b_y(k):
        here = wf.at[far, rows_b, mine]
        return remote(here, here, sb.at[k], qb.at[k], seq=at_seq((y + k) % ny, z, core))

    def a_y(k):
        here = wf.at[far, rows_a, row_of(y)]
        return remote(here, here, sc.at[k], qc.at[k], seq=at_seq((y + k) % ny, z, core))

    def b_z(k, yy):
        here = wf.at[far, rows_b, cols(yy, z)]
        return remote(here, here, sd.at[k, yy], qd.at[k, yy], seq=at_seq(y, (z + k) % nz, core))

    def across(part):
        here = wf.at[far, rows_a if part == 0 else rows_b]
        return remote(here, here, se.at[part], qe.at[part], seq=at_seq(y, z, 1 - core))

    def arrived(src, sem, **where):
        remote(src, src, sem, sem, **where).wait_recv()

    def step0():
        for k in range(1, nx):
            spread_x(k).start()

    def step1():
        for k in range(1, nx):
            spread_x(k).wait_recv()
        for k in range(1, max(ny, nz)):
            if k < nz:
                a_z(k).start()
            if k < ny:
                b_y(k).start()

    def step2():
        for k in range(1, nz):
            a_z(k).wait_recv()
        for k in range(1, ny):
            a_y(k).start()
        for k in range(1, ny):
            b_y(k).wait_recv()
        for k in range(1, nz):
            for yy in range(ny):
                b_z(k, yy).start()

    def step3():
        for k in range(1, ny):
            a_y(k).wait_recv()
        across(0).start()
        for k in range(1, nz):
            for yy in range(ny):
                b_z(k, yy).wait_recv()
        across(1).start()

    def step4():
        across(0).wait_recv()
        across(1).wait_recv()
        for k in range(1, nx):
            spread_x(k).wait_send()
        for k in range(1, nz):
            a_z(k).wait_send()
            for yy in range(ny):
                b_z(k, yy).wait_send()
        for k in range(1, ny):
            b_y(k).wait_send()
            a_y(k).wait_send()
        across(0).wait_send()
        across(1).wait_send()

    return step0, step1, step2, step3, step4


def kernel(
    nx, ny, nz, nh,
    tok, wt, cv, go, selq, selk, gmq, gmk,
    att, gi, gw, wf,
    w, g, gt, p, hal, taps, qkt, vaug, fqt, fkt, fq, fk, ub, nin, scot, gna, run, st, pfk, gp, hc,
    loc, r1, tot, r2, out, res,
    wbuf, gin, g3, hal2, gwb, rp, t, r2a, r2b, va, vb, r3a, r3b,
    s_own, r_own, s_fwd, r_fwd, s_hal, r_hal, s_w, s_tok,
    s1, q1, s2, q2, s3, q3,
    sw, sx, qx, sh, qh, sp, qp, s2a, q2a, s2b, q2b, s3a, q3a, s3b, q3b,
    *sems,
):
    x = lax.axis_index("head")
    s = lax.axis_index("seq")
    ns = 2 * ny * nz
    core, z, y = s % 2, (s // 2) % nz, s // (2 * nz)
    left, right, opp = (x + nx - 1) % nx, (x + 1) % nx, (x + 2) % nx
    prev, after = (s + ns - 1) % ns, (s + 1) % ns
    ga, gb = 2 * nz, ny
    me_a, me_b = s % ga, s // ga
    rows, depth = tok.shape
    nb = go.shape[0] // BLK
    ch = rows // 4
    piece = loc.shape[1] // ga
    gh = nh // 2
    per = gh * nb

    def at_seq(yy, zz, cc):
        return (yy * nz + zz) * 2 + cc

    sibling = at_seq(y, z, 1 - core)
    bar = pltpu.get_barrier_semaphore()
    for k in range(1, nx):
        greet(bar, head=(x + k) % nx)
    for k in range(1, ga):
        greet(bar, seq=me_b * ga + (me_a + k) % ga)
    for k in range(1, gb):
        greet(bar, seq=((me_b + k) % gb) * ga + me_a)
    greet(bar, seq=prev)
    greet(bar, seq=after)
    greet(bar, seq=prev, head=nx - 1)

    @pl.when(x == nx - 1)
    def _():
        for j in range(nx):
            greet(bar, seq=after, head=j)

    local_tok = pltpu.make_async_copy(tok, g.at[x], s_tok)
    local_tok.start()
    loads = []
    for h in range(nh):
        base = h * CHAN
        loads.append(
            pltpu.make_async_copy(
                wt.at[base + 2 * F : base + CHAN], w.at[h * E : (h + 1) * E], s_w.at[2 * h]
            )
        )
        loads.append(
            pltpu.make_async_copy(
                wt.at[base : base + 2 * F],
                w.at[nh * E + 2 * F * h : nh * E + 2 * F * (h + 1)],
                s_w.at[2 * h + 1],
            )
        )
    for copy in loads:
        copy.start()
    greeted = nx - 1 + ga - 1 + gb - 1 + 3
    pl.semaphore_wait(bar, jnp.where(x == nx - 1, greeted + nx, greeted))

    def part(c):
        return pl.ds(c * ch, ch)

    def own(way, c):
        return remote(
            tok.at[part(c)],
            g.at[x, part(c)],
            s_own.at[way, c],
            r_own.at[way, c],
            head=right if way == 0 else left,
        )

    def arrives(way, c):
        slot = left if way == 0 else right
        return remote(
            tok.at[part(c)], g.at[slot, part(c)], s_own.at[way, c], r_own.at[way, c], head=left
        )

    def forward(way, c):
        slot = left if way == 0 else right
        return remote(
            g.at[slot, part(c)],
            g.at[slot, part(c)],
            s_fwd.at[way, c % 2],
            r_fwd.at[way, c % 2],
            head=right if way == 0 else left,
        )

    def arrives_far(way, c):
        return remote(
            tok.at[part(c)], g.at[opp, part(c)], s_fwd.at[way, c % 2], r_fwd.at[way, c % 2], head=left
        )

    def halo(j):
        return remote(tok.at[pl.ds(rows - 16, 16)], hal, s_hal.at[j], r_hal, seq=after, head=j)

    step0, step1, step2, step3, step4 = weight_gather(nx, ny, nz, x, y, z, core, w, wf, sems)
    for c in range(2):
        own(0, c).start()
        own(1, c + 2).start()

    @pl.when(x == nx - 1)
    def _():
        for j in range(nx):
            halo(j).start()

    for copy in loads:
        copy.wait()
    step0()

    lane = lax.broadcasted_iota(jnp.int32, (BLK, BLK), 1)
    sub = lax.broadcasted_iota(jnp.int32, (BLK, BLK), 0)
    frow = lax.broadcasted_iota(jnp.int32, (FS, E), 0)

    for j in range(3):
        lines = [cv[j, h : h + 1, :] for h in range(nh)]
        for h in range(nh):
            taps[j : j + 1, h * E : (h + 1) * E] = lines[h][:, 2 * F :]
        taps[j : j + 1, nh * E :] = jnp.concatenate([v[:, : 2 * F] for v in lines], 1) * KAPPA

    def rows_of(a):
        return pl.ds(pl.multiple_of(a * piece, 16), piece)

    def first(e, k):
        a = (me_a + k) % ga
        return remote(
            loc.at[e, rows_of(a)], r1.at[e, me_a], s1.at[e, k], q1.at[e, k], seq=me_b * ga + a
        )

    def second(e, k):
        b = (me_b + k) % gb
        return remote(tot.at[e], r2.at[e, me_b], s2.at[e, k], q2.at[e, k], seq=b * ga + me_a)

    def third(e, k):
        a = (me_a + k) % ga
        return remote(
            out.at[e, a], res.at[e, rows_of(me_a)], s3.at[e, k], q3.at[e, k], seq=me_b * ga + a
        )

    def exchange_first(e):
        for k in range(1, ga):
            first(e, k).start()
        r1[e, me_a] = loc[e, rows_of(me_a), :]

    def exchange_second(e):
        for k in range(1, ga):
            a = (me_a + ga - k) % ga
            remote(
                loc.at[e, rows_of(a)], r1.at[e, a], s1.at[e, k], q1.at[e, k], seq=s
            ).wait_recv()
        total = jnp.zeros((piece, E), f32)
        for a in range(ga):
            total = total + r1[e, a].astype(f32)
        tot[e] = total.astype(bf16)
        for k in range(1, gb):
            second(e, k).start()

    def exchange_third(e):
        for k in range(1, gb):
            b = (me_b + gb - k) % gb
            remote(tot.at[e], r2.at[e, b], s2.at[e, k], q2.at[e, k], seq=s).wait_recv()
        r2[e, me_b] = tot[e]
        total = jnp.zeros((piece, E), f32)
        for b in range(gb):
            ahead = b < me_b if e < 2 else b > me_b
            total = total + jnp.where(ahead, r2[e, b].astype(f32), 0.0)
        for step in range(ga):
            a = step if e < 2 else ga - 1 - step
            out[e, a] = total.astype(bf16)
            total = total + r1[e, a].astype(f32)
        for k in range(1, ga):
            third(e, k).start()
        res[e, rows_of(me_a), :] = out[e, me_a]

    def exchange_done(e):
        for k in range(1, ga):
            a = (me_a + ga - k) % ga
            remote(
                out.at[e, a], res.at[e, rows_of(a)], s3.at[e, k], q3.at[e, k], seq=s
            ).wait_recv()

    def pack(e, h, whole):
        column = jnp.concatenate([whole[:, E:], jnp.zeros((2 * E - FS, E), f32)], 0)
        line = column.T[0:1, :]
        body = jnp.where(frow == NF, line[:, :E], jnp.where(frow == NF + 1, line[:, E:], whole[:, :E]))
        loc[e, h * FS : (h + 1) * FS, :] = body.astype(bf16)

    def pack_group(e):
        for j in range(gh):
            h = (e % 2) * gh + j
            whole = ub[h * nb]
            for b in range(1, nb):
                whole = whole + ub[h * nb + b]
            pack(e, j, whole)
        if gh * FS < loc.shape[1]:
            loc[e, gh * FS :, :] = jnp.zeros((loc.shape[1] - gh * FS, E), bf16)

    def unpack_group(e):
        for j in range(gh):
            body = res[e, j * FS : (j + 1) * FS, :].astype(f32)
            line = jnp.concatenate([body[NF : NF + 1, :], body[NF + 1 : NF + 2, :]], 1)
            column = jnp.broadcast_to(line, (E, 2 * E)).T[:FS, :]
            run[(e % 2) * gh + j] = jnp.concatenate([jnp.where(frow < NF, body, 0.0), column], 1)

    def factors(u, sel):
        high = u.astype(bf16)
        low = (u - high.astype(f32)).astype(bf16)
        stack = jnp.concatenate([high, low, jnp.ones((F, BLK), bf16)], 0)
        both = dot(sel[...], stack)
        return both[:FS], both[FS:]

    def block_at(b):
        return pl.ds(pl.multiple_of(b * BLK, BLK), BLK)

    def convolve(b):
        ext = p[pl.ds(pl.multiple_of(b * BLK, BLK), BLK + 16), :]
        conv = taps[0:1, :] * ext[16:] + taps[1:2, :] * ext[15:-1] + taps[2:3, :] * ext[14:-2]
        qkt[:, block_at(b)] = conv[:, nh * E :].T
        for h in range(nh):
            vaug[h * nb + b] = jnp.concatenate(
                [conv[:, h * E : (h + 1) * E].astype(bf16), jnp.ones((BLK, E), bf16)], 1
            )

    def featurize(b, group):
        for j in range(gh):
            h = group * gh + j
            i = h * nb + b
            at = block_at(b)
            first_q, second_q = factors(qkt[2 * F * h : 2 * F * h + F, at], selq)
            first_k, second_k = factors(qkt[2 * F * h + F : 2 * F * (h + 1), at], selk)
            q = (first_q * second_q).astype(bf16)
            k = (first_k * second_k).astype(bf16)
            fqt[i] = q
            fkt[i] = k
            fq[i] = q.T
            fk[i] = k.T
            ub[i] = dot(k, vaug[i])

    def project(slot):
        base = pl.multiple_of(slot * rows, rows)
        p[pl.ds(16 + base, rows), :] = dot(g[slot], w[...], NT)

    def turn(slot):
        base = pl.multiple_of(slot * rows, rows)

        def piece_of(i, carry):
            at = pl.ds(pl.multiple_of(i * 256, 256), 256)
            gt[at, pl.ds(base, rows)] = g[slot, :, at].T
            return carry

        lax.fori_loop(0, depth // 256, piece_of, 0)

    local_tok.wait()
    project(x)
    for c in range(2):
        own(0, c).wait_send()
        own(1, c + 2).wait_send()
        own(0, c + 2).start()
        own(1, c).start()
    step1()
    for c in range(2):
        arrives(0, c).wait_recv()
        forward(0, c).start()
        arrives(1, c + 2).wait_recv()
        forward(1, c + 2).start()
    turn(x)
    halo(0).wait_recv()
    head_rows = dot(hal[...], w[...], NT)
    p[0:16, :] = jnp.where(s == 0, 0.0, head_rows)
    step2()
    arrives(0, 2).wait_recv()
    arrives(0, 3).wait_recv()
    project(left)
    arrives(1, 0).wait_recv()
    arrives(1, 1).wait_recv()
    project(right)
    for b in (x, right):
        convolve(b)
        featurize(b, 0)
        featurize(b, 1)
    turn(left)
    turn(right)
    for c in range(2):
        arrives_far(0, c).wait_recv()
        arrives_far(1, c + 2).wait_recv()
    project(opp)
    for b in (opp, left):
        convolve(b)
        featurize(b, 0)
    pack_group(0)
    exchange_first(0)
    for b in (opp, left):
        featurize(b, 1)
    pack_group(1)
    exchange_first(1)

    def inside(i, carry):
        score = jnp.where(sub >= lane, dot(fq[i], fkt[i]), 0.0).astype(bf16)
        scot[i] = jnp.where(lane >= sub, dot(fk[i], fqt[i]), 0.0).astype(bf16)
        nin[i] = dot(score, vaug[i])
        return carry

    def quarter(n, body):
        lax.fori_loop(n * per // 2, (n + 1) * per // 2, body, 0, unroll=True)

    turn(opp)
    quarter(0, inside)
    exchange_second(0)
    quarter(1, inside)
    exchange_second(1)
    quarter(2, inside)
    exchange_third(0)
    quarter(3, inside)
    exchange_third(1)

    ones = jnp.ones((2 * E, E), bf16)

    def attend(group):
        def block(b, carry):
            for j in range(gh):
                h = group * gh + j
                i = h * nb + b
                state = run[h]
                state_b = state.astype(bf16)
                run[h] = state + ub[i]
                both = dot(fq[i], state_b) + nin[i]
                num = both[:, :E]
                inv = 1.0 / both[:, E:]
                mean = num * inv
                at = (block_at(b), slice(h * E, (h + 1) * E))
                att[at] = mean.astype(bf16)
                scaled = go[at].astype(f32) * inv
                product = scaled * mean
                high = product.astype(bf16)
                low = (product - high.astype(f32)).astype(bf16)
                slope = dot(jnp.concatenate([high, low], 1), ones) * (-1.0 / E)
                ga_b = jnp.concatenate([scaled.astype(bf16), slope.astype(bf16)], 1)
                gna[i] = ga_b
                st[i] = state_b
                ub[i] = dot(fqt[i], ga_b)
            return carry

        lax.fori_loop(0, nb, block, 0)
        pack_group(2 + group)

    for group in range(2):
        exchange_done(group)
        unpack_group(group)
        attend(group)
        exchange_first(2 + group)

    def feature_gradient(u, sel, gm, grad):
        one, two = factors(u, sel)
        stack = jnp.concatenate([(grad * two).astype(bf16), (grad * one).astype(bf16)], 0)
        return dot(gm[...], stack)

    def inside_back(i, carry):
        h, b = i // nb, i % nb
        ga_b = gna[i]
        va = vaug[i]
        mix = jnp.where(sub >= lane, dot(ga_b, va, NT), 0.0).astype(bf16)
        mixt = jnp.where(lane >= sub, dot(va, ga_b, NT), 0.0).astype(bf16)
        gfq = dot(st[i], ga_b, NT) + dot(fkt[i], mixt)
        at = (pl.ds(pl.multiple_of(h * 2 * F, 2 * F), F), block_at(b))
        gq = feature_gradient(qkt[at], selq, gmq, gfq)
        pfk[i] = dot(fqt[i], mix)
        qkt[at] = gq
        nin[i, :, :E] = dot(scot[i], ga_b[:, :E])
        return carry

    step3()
    quarter(0, inside_back)
    exchange_second(2)
    quarter(1, inside_back)
    exchange_second(3)
    quarter(2, inside_back)
    exchange_third(2)
    quarter(3, inside_back)
    exchange_third(3)

    def finish(group):
        def block(step, carry):
            b = nb - 1 - step
            for j in range(gh):
                h = group * gh + j
                i = h * nb + b
                state = run[h]
                state_b = state.astype(bf16)
                run[h] = state + ub[i]
                gfk = dot(state_b, vaug[i], NT) + pfk[i]
                at = (slice(2 * F * h + F, 2 * F * (h + 1)), block_at(b))
                qkt[at] = feature_gradient(qkt[at], selk, gmk, gfk)
                p[block_at(b), h * E : (h + 1) * E] = dot(fk[i], state_b[:, :E]) + nin[i, :, :E]
            return carry

        lax.fori_loop(0, nb, block, 0)

    for group in range(2):
        exchange_done(2 + group)
        unpack_group(2 + group)
        finish(group)

    p[nb * BLK :, :] = jnp.zeros((16, p.shape[1]), f32)
    for b in range(nb):
        p[b * BLK : (b + 1) * BLK, nh * E :] = qkt[:, b * BLK : (b + 1) * BLK].T

    def spread(b, carry):
        ext = p[pl.ds(pl.multiple_of(b * BLK, BLK), BLK + 16), :]
        grad = taps[0:1, :] * ext[:BLK] + taps[1:2, :] * ext[1 : BLK + 1] + taps[2:3, :] * ext[2 : BLK + 2]
        gp[block_at(b), :] = grad.astype(bf16)
        return carry

    lax.fori_loop(0, nb, spread, 0)
    edge = jnp.concatenate([jnp.zeros((16, p.shape[1]), f32), p[0:16, :]], 0)
    hc[...] = (taps[1:2, :] * edge[1:17] + taps[2:3, :] * edge[2:18]).astype(bf16)


    rows = gin.shape[1]
    steps = gi.shape[1] // 256

    def load(i, slot):
        return pltpu.make_async_copy(
            wf.at[:, :, pl.ds(pl.multiple_of(i * 256, 256), 256)], wbuf.at[slot], sw.at[slot]
        )

    back = remote(hc, hal2, sh, qh, seq=prev)
    back.start()

    def rows_at(j):
        return pl.ds(pl.multiple_of(j * rows, rows), rows)

    def over(k, last):
        j = (x + k) % nx
        src = g3 if last else gp.at[rows_at(j)]
        return remote(src, gin.at[nx - k], sx.at[k], qx.at[nx - k], head=j)

    for k in (2, 1, 3):

        @pl.when((x + k) % nx != nx - 1)
        def _():
            over(k, False).start()

    back.wait_recv()
    low = gp[(nx - 1) * rows :, :]
    g3[...] = low
    fixed = low[rows - 16 :].astype(f32) + jnp.where(s == ns - 1, 0.0, hal2[...].astype(f32))
    g3[rows - 16 :, :] = fixed.astype(bf16)
    for k in (2, 1, 3):

        @pl.when((x + k) % nx == nx - 1)
        def _():
            over(k, True).start()

    @pl.when(x == nx - 1)
    def _():
        gin[0] = g3[...]

    @pl.when(x != nx - 1)
    def _():
        gin[0] = gp[rows_at(x), :]

    pieces = ny * nz
    height = gwb.shape[2]

    def pair(j):
        return remote(gwb.at[j, 1 - core], rp.at[j], sp.at[j], qp.at[j], seq=sibling)

    per_step = 256 // (2 * height)
    early = (nx - 1) * rows

    def weight_step(i, carry):
        at = pl.ds(pl.multiple_of(i * 256, 256), 256)
        left = gt[at, :]
        whole = dot(left[:, :early], gp[:early, :]) + dot(left[:, early:], g3[...])
        whole = whole.astype(bf16).reshape(per_step, 2, height, whole.shape[1])
        for q in range(per_step):
            gwb[i * per_step + q] = whole[q]
            pair(i * per_step + q).start()
        return carry

    lax.fori_loop(0, pieces // per_step, weight_step, 0)

    step4()
    load(0, 0).start()
    load(1, 1).start()

    def pair_sum(j, carry):
        remote(gwb.at[j, core], rp.at[j], sp.at[j], qp.at[j], seq=sibling).wait_recv()
        t[j // nz, j % nz] = (gwb[j, core].astype(f32) + rp[j].astype(f32)).astype(bf16)
        return carry

    lax.fori_loop(0, pieces, pair_sum, 0)
    half = height // 2
    low_half, high_half = pl.ds(0, half), pl.ds(half, half)

    def go_2a(k):
        to = (z + k) % nz
        return remote(
            t.at[:, to, low_half], r2a.at[k], s2a.at[k], q2a.at[k], seq=at_seq(y, to, core)
        )

    def go_2b(k):
        to = (y + k) % ny
        return remote(
            t.at[to, :, high_half], r2b.at[k], s2b.at[k], q2b.at[k], seq=at_seq(to, z, core)
        )

    def go_3a(k):
        to = (y + k) % ny
        return remote(va.at[to], r3a.at[k], s3a.at[k], q3a.at[k], seq=at_seq(to, z, core))

    def go_3b(k):
        to = (z + k) % nz
        return remote(vb.at[to], r3b.at[k], s3b.at[k], q3b.at[k], seq=at_seq(y, to, core))

    for k in range(1, max(ny, nz)):
        if k < nz:
            go_2a(k).start()
        if k < ny:
            go_2b(k).start()

    for k in (2, 1, 3):
        remote(g3, gin.at[k], sx.at[k], qx.at[k], head=(x + k) % nx).wait_recv()

    def input_step(i, carry):
        at = pl.ds(pl.multiple_of(i * 256, 256), 256)
        slot = i % 2
        total = dot(gin[0], w[:, at])
        load(i, slot).wait()
        for j in range(1, nx):
            total = total + dot(gin[j], wbuf[slot, j - 1])
        gi[:, at] = total.astype(bf16)

        @pl.when(i + 2 < steps)
        def _():
            load(i + 2, slot).start()

        return carry

    lax.fori_loop(0, steps // 2, input_step, 0)

    for k in range(1, nz):
        go_2a(k).wait_recv()
    for k in range(1, ny):
        go_2b(k).wait_recv()
    for i in range(ny):
        total = t[i, z, 0:half].astype(f32)
        for k in range(1, nz):
            total = total + r2a[k, i].astype(f32)
        va[i] = total.astype(bf16)
    for i in range(nz):
        total = t[y, i, half:].astype(f32)
        for k in range(1, ny):
            total = total + r2b[k, i].astype(f32)
        vb[i] = total.astype(bf16)
    for k in range(1, max(ny, nz)):
        if k < ny:
            go_3a(k).start()
        if k < nz:
            go_3b(k).start()
    lax.fori_loop(steps // 2, steps, input_step, 0)
    def put(at, total):
        for h in range(nh):
            narrow = total[:, nh * E + 2 * F * h : nh * E + 2 * F * (h + 1)]
            gw[at, h, :] = jnp.concatenate([narrow, total[:, h * E : (h + 1) * E]], 1)

    total = va[y].astype(f32)
    for k in range(1, ny):
        go_3a(k).wait_recv()
        total = total + r3a[k].astype(f32)
    put(slice(0, half), total)
    total = vb[z].astype(f32)
    for k in range(1, nz):
        go_3b(k).wait_recv()
        total = total + r3b[k].astype(f32)
    put(slice(half, height), total)

    back.wait_send()
    for k in range(1, nx):
        over(k, False).wait_send()
    for j in range(pieces):
        pair(j).wait_send()
    for k in range(1, nz):
        go_2a(k).wait_send()
        go_3b(k).wait_send()
    for k in range(1, ny):
        go_2b(k).wait_send()
        go_3a(k).wait_send()
    for e in range(4):
        for k in range(1, ga):
            first(e, k).wait_send()
            third(e, k).wait_send()
        for k in range(1, gb):
            second(e, k).wait_send()
    for c in range(2):
        own(0, c + 2).wait_send()
        own(1, c).wait_send()
        forward(0, c).wait_send()
        forward(1, c + 2).wait_send()

    @pl.when(x == nx - 1)
    def _():
        for j in range(nx):
            halo(j).wait_send()


def local(nx, ny, nz, tokens, in_weight, conv_kernel, grad_out):
    depth, nh, _ = in_weight.shape
    wt = jnp.transpose(in_weight, (1, 2, 0)).reshape(nh * CHAN, depth)
    rows = tokens.shape[0]
    every = grad_out.shape[0]
    width = nh * CHAN
    nb = every // BLK
    n = nh * nb
    ga, gb, ns = 2 * nz, ny, 2 * ny * nz
    piece = -(-(nh // 2) * FS // (16 * ga)) * 16
    height = depth // ns
    half = height // 2
    vm = pl.BlockSpec(memory_space=pltpu.VMEM)
    hbm = pl.BlockSpec(memory_space=pl.ANY)
    dma = pltpu.SemaphoreType.DMA
    consts = [
        jnp.asarray(selection(True), bf16),
        jnp.asarray(selection(False), bf16),
        jnp.asarray(gradient_map(True), bf16),
        jnp.asarray(gradient_map(False), bf16),
    ]
    att, gi, gw, _ = pl.pallas_call(
        functools.partial(kernel, nx, ny, nz, nh),
        out_shape=(
            jax.ShapeDtypeStruct((every, nh * E), bf16),
            jax.ShapeDtypeStruct((rows, depth), bf16),
            jax.ShapeDtypeStruct((height, nh, CHAN), f32),
            jax.ShapeDtypeStruct((nx - 1, width, depth), bf16),
        ),
        in_specs=[hbm, hbm] + [vm] * 6,
        out_specs=(vm, vm, vm, hbm),
        scratch_shapes=[
            pltpu.VMEM((width, depth), bf16),
            pltpu.VMEM((nx, rows, depth), bf16),
            pltpu.VMEM((depth, every), bf16),
            pltpu.VMEM((16 + every, width), f32),
            pltpu.VMEM((16, depth), bf16),
            pltpu.VMEM((8, width), f32),
            pltpu.VMEM((nh * 2 * F, every), f32),
            pltpu.VMEM((n, BLK, 2 * E), bf16),
            pltpu.VMEM((n, FS, BLK), bf16),
            pltpu.VMEM((n, FS, BLK), bf16),
            pltpu.VMEM((n, BLK, FS), bf16),
            pltpu.VMEM((n, BLK, FS), bf16),
            pltpu.VMEM((n, FS, 2 * E), f32),
            pltpu.VMEM((n, BLK, 2 * E), f32),
            pltpu.VMEM((n, BLK, BLK), bf16),
            pltpu.VMEM((n, BLK, 2 * E), bf16),
            pltpu.VMEM((nh, FS, 2 * E), f32),
            pltpu.VMEM((n, FS, 2 * E), bf16),
            pltpu.VMEM((n, FS, BLK), f32),
            pltpu.VMEM((every, width), bf16),
            pltpu.VMEM((16, width), bf16),
            pltpu.VMEM((4, ga * piece, E), bf16),
            pltpu.VMEM((4, ga, piece, E), bf16),
            pltpu.VMEM((4, piece, E), bf16),
            pltpu.VMEM((4, gb, piece, E), bf16),
            pltpu.VMEM((4, ga, piece, E), bf16),
            pltpu.VMEM((4, ga * piece, E), bf16),
            pltpu.VMEM((2, nx - 1, width, 256), bf16),
            pltpu.VMEM((nx, rows, width), bf16),
            pltpu.VMEM((rows, width), bf16),
            pltpu.VMEM((16, width), bf16),
            pltpu.VMEM((ny * nz, 2, height, width), bf16),
            pltpu.VMEM((ny * nz, height, width), bf16),
            pltpu.VMEM((ny, nz, height, width), bf16),
            pltpu.VMEM((nz, ny, half, width), bf16),
            pltpu.VMEM((ny, nz, half, width), bf16),
            pltpu.VMEM((ny, half, width), bf16),
            pltpu.VMEM((nz, half, width), bf16),
            pltpu.VMEM((ny, half, width), bf16),
            pltpu.VMEM((nz, half, width), bf16),
            dma((2, 4)),
            dma((2, 4)),
            dma((2, 2)),
            dma((2, 2)),
            dma((nx,)),
            dma(()),
            dma((2 * nh,)),
            dma(()),
            dma((4, ga)),
            dma((4, ga)),
            dma((4, gb)),
            dma((4, gb)),
            dma((4, ga)),
            dma((4, ga)),
            dma((2,)),
            dma((nx,)),
            dma((nx,)),
            dma(()),
            dma(()),
            dma((ny * nz,)),
            dma((ny * nz,)),
            dma((nz,)),
            dma((nz,)),
            dma((ny,)),
            dma((ny,)),
            dma((ny,)),
            dma((ny,)),
            dma((nz,)),
            dma((nz,)),
            dma((nx,)),
            dma((nx,)),
            dma((nz,)),
            dma((nz,)),
            dma((ny,)),
            dma((ny,)),
            dma((ny,)),
            dma((ny,)),
            dma((nz, ny)),
            dma((nz, ny)),
            dma((2,)),
            dma((2,)),
        ],
        compiler_params=pltpu.CompilerParams(
            collective_id=0, has_side_effects=True, vmem_limit_bytes=62 * 2**20
        ),
    )(tokens, wt, conv_kernel, grad_out, *consts)
    return att, gi, gw


def solution(mesh):
    nx, ns = mesh.shape["head"], mesh.shape["seq"]
    ny = math.isqrt(ns // 2)
    nz = ns // 2 // ny
    placed = (
        P(("seq", "head"), None),
        P(None, "head", None),
        P(None, "head", None),
        P("seq", "head"),
    )
    return jax.shard_map(
        functools.partial(local, nx, ny, nz),
        mesh=mesh,
        in_specs=placed,
        out_specs=(P("seq", "head"), P(("seq", "head"), None), P("seq", "head", None)),
        check_vma=False,
    )
```

```python
import functools
import math

import jax
import jax.numpy as jnp
import numpy as np
from jax import lax
from jax.experimental import pallas as pl
from jax.experimental.pallas import tpu as pltpu
from jax.sharding import PartitionSpec as P

F = 16
E = 128
BLK = 256
CHAN = 160
FS = 160
NF = 1 + F + F * (F + 1) // 2
KAPPA = 32.0 ** -0.25
f32 = jnp.float32
bf16 = jnp.bfloat16
NN = (((1,), (0,)), ((), ()))
NT = (((1,), (1,)), ((), ()))


def dot(a, b, dims=NN):
    return lax.dot_general(a, b, dims, preferred_element_type=f32)


def bf_parts(value, count):
    parts = []
    rest = np.float64(value)
    for _ in range(count):
        part = np.float64(np.asarray(rest, dtype=jnp.bfloat16))
        parts.append(part)
        rest = rest - part
    return parts


def selection(weighted):
    sel = np.zeros((2 * FS, 3 * F), np.float64)
    sel[0, 32] = 1.0
    sel[FS, 32] = 1.0
    for i in range(F):
        row = 1 + i
        sel[row, i] = sel[row, F + i] = 1.0
        for c, part in enumerate(bf_parts(0.5 / KAPPA, 3)):
            sel[FS + row, 32 + c] = part
    row = 1 + F
    for i in range(F):
        for j in range(i, F):
            first = 2.0 if (weighted and j > i) else 1.0
            sel[row, i] = sel[row, F + i] = first
            sel[FS + row, j] = sel[FS + row, F + j] = 1.0
            row += 1
    return sel


def gradient_map(weighted):
    sel = selection(weighted)
    return np.concatenate([sel[:FS, :F].T, sel[FS:, :F].T], 1)


def remote(src, dst, send, recv, **where):
    return pltpu.make_async_remote_copy(
        src_ref=src,
        dst_ref=dst,
        send_sem=send,
        recv_sem=recv,
        device_id=where,
        device_id_type=pl.DeviceIdType.MESH,
    )


def arrived(ref, sem):
    remote(ref, ref, sem, sem, seq=lax.axis_index("seq")).wait_recv()


def sent(ref, sem):
    remote(ref, ref, sem, sem, seq=lax.axis_index("seq")).wait_send()


def greet(sem, **where):
    pl.semaphore_signal(sem, inc=1, device_id=where, device_id_type=pl.DeviceIdType.MESH)


def weight_gather(nx, ny, nz, x, y, z, core, w, wf, sems):
    s1, q1, sr, qr, sa, qa, sb, qb, sc, qc, sd, qd, sf, qf, sg, qg, se, qe = sems
    chan, depth = w.shape
    half = chan // 2
    quarter = half // 2
    eighth = quarter // 2
    col = depth // (ny * nz)
    base = core * half
    rows_c = pl.ds(pl.multiple_of(base, 16), half)
    rows_a = pl.ds(pl.multiple_of(base, 16), quarter)
    rows_b = pl.ds(pl.multiple_of(base + quarter, 16), quarter)
    far = pl.ds(0, nx - 1)

    def piece_a(n):
        return pl.ds(pl.multiple_of(base + n * eighth, 16), eighth)

    def piece_b(n):
        return pl.ds(pl.multiple_of(base + quarter + n * eighth, 16), eighth)

    def cols(yy, zz):
        return pl.ds(pl.multiple_of((yy * nz + zz) * col, 128), col)

    def row_of(yy):
        return pl.ds(pl.multiple_of(yy * nz * col, 128), nz * col)

    def at_seq(yy, zz, cc):
        return (yy * nz + zz) * 2 + cc

    mine = cols(y, z)
    ring_y = (1, ny - 1) if ny > 2 else (1,)
    ring_z = (1, nz - 1) if nz > 2 else (1,)

    def spread_x(k):
        return remote(w.at[rows_c, mine], wf.at[nx - k - 1, rows_c, mine], s1, q1, head=(x + k) % nx)

    def spread_on(k):
        here = wf.at[nx - k - 1, rows_a if k == 1 else rows_b, mine]
        there = wf.at[nx // 2 - 1, rows_a if k == 1 else rows_b, mine]
        return remote(here, there, sr, qr, head=(x + k) % nx)

    def a_z(k):
        here = wf.at[far, rows_a, mine]
        return remote(here, here, sa, qa, seq=at_seq(y, (z + k) % nz, core))

    def b_y(k):
        here = wf.at[far, rows_b, mine]
        return remote(here, here, sb, qb, seq=at_seq((y + k) % ny, z, core))

    def a_y(k):
        here = wf.at[far, rows_a, row_of(y)]
        return remote(here, here, sc.at[k], qc.at[k], seq=at_seq((y + k) % ny, z, core))

    def b_z(k, yy):
        here = wf.at[far, rows_b, cols(yy, z)]
        return remote(here, here, sd.at[k], qd.at[k], seq=at_seq(y, (z + k) % nz, core))

    def a_y_on(k):
        here = wf.at[far, piece_a(0 if k == 1 else 1), row_of((y - k) % ny)]
        return remote(here, here, sf, qf, seq=at_seq((y + k) % ny, z, core))

    def b_z_on(k, yy):
        here = wf.at[far, piece_b(0 if k == 1 else 1), cols(yy, (z - k) % nz)]
        return remote(here, here, sg, qg, seq=at_seq(y, (z + k) % nz, core))

    def across(part):
        here = wf.at[far, rows_a if part == 0 else rows_b]
        return remote(here, here, se.at[part], qe.at[part], seq=at_seq(y, z, 1 - core))

    def lanes(rows, count):
        return wf.at[far, rows, pl.ds(0, count * col)]

    def step0():
        for k in (1, nx - 1):
            spread_x(k).start()

    def step1():
        arrived(wf.at[pl.ds(0, 2), rows_c, mine], q1)
        for k in (1, nx - 1):
            spread_on(k).start()

    def step2():
        arrived(wf.at[0, rows_c, mine], qr)
        for k in range(1, max(ny, nz)):
            if k < nz:
                a_z(k).start()
            if k < ny:
                b_y(k).start()

    def step3():
        arrived(lanes(rows_a, nz - 1), qa)
        for k in ring_y:
            a_y(k).start()
        arrived(lanes(rows_b, ny - 1), qb)
        for k in ring_z:
            for yy in range(ny):
                b_z(k, yy).start()

    def step4():
        for k in ring_y:
            arrived(lanes(rows_a, nz), qc.at[ny - k])
            if ny > 2:
                a_y_on(ny - k).start()
        for k in ring_z:
            arrived(lanes(rows_b, ny), qd.at[nz - k])
            if nz > 2:
                for yy in range(ny):
                    b_z_on(nz - k, yy).start()

    def step5():
        if ny > 2:
            arrived(lanes(rows_a, nz), qf)
        across(0).start()
        if nz > 2:
            arrived(lanes(rows_b, ny), qg)
        across(1).start()

    def step6():
        across(0).wait_recv()
        across(1).wait_recv()

    def step7():
        sent(wf.at[pl.ds(0, 2), rows_c, mine], s1)
        sent(wf.at[0, rows_c, mine], sr)
        sent(lanes(rows_a, nz - 1), sa)
        sent(lanes(rows_b, ny - 1), sb)
        for k in ring_y:
            sent(lanes(rows_a, nz), sc.at[k])
        for k in ring_z:
            sent(lanes(rows_b, ny), sd.at[k])
        if ny > 2:
            sent(lanes(rows_a, nz), sf)
        if nz > 2:
            sent(lanes(rows_b, ny), sg)
        across(0).wait_send()
        across(1).wait_send()

    return step0, step1, step2, step3, step4, step5, step6, step7


def kernel(
    nx, ny, nz, nh,
    tok, wt, cv_hbm, go, selq_hbm, selk_hbm, gmq_hbm, gmk_hbm,
    att, gi, gw, wf,
    cv, selq, selk, gmq, gmk, go_v, att_v, gi_v, gw_v, w, g, gt, p, hal, taps, qkt, vaug, fqt, fkt, fq, fk, ub, nin, scot, gna, run, st, pfk, gp,
    loc, r1, tot, r2, out, res,
    wbuf, gin, hi, gwb, rp, t, r2a, r2b, va, vb, r3a, r3b,
    s_own, r_own, r_rest, s_fwd, r_fwd, s_hal, r_hal, s_w, s_tok,
    s1, q1, s2, q2, s3, q3,
    sw, sx, qx, sh, qh, sp, qp, s2a, q2a, s2b, q2b, s3a, q3a, s3b, q3b, s_att, s_gi, s_gw, s_go, s_const,
    *sems,
):
    x = lax.axis_index("head")
    s = lax.axis_index("seq")
    ns = 2 * ny * nz
    core, z, y = s % 2, (s // 2) % nz, s // (2 * nz)
    left, right, opp = (x + nx - 1) % nx, (x + 1) % nx, (x + 2) % nx
    prev, after = (s + ns - 1) % ns, (s + 1) % ns
    ga, gb = 2 * nz, ny
    me_a, me_b = s % ga, s // ga
    rows, depth = tok.shape
    nb = go.shape[0] // BLK
    ch = rows // 4
    piece = loc.shape[1] // ga
    gh = nh // 2
    per = gh * nb

    def at_seq(yy, zz, cc):
        return (yy * nz + zz) * 2 + cc

    sibling = at_seq(y, z, 1 - core)
    bar = pltpu.get_barrier_semaphore()
    for k in range(1, nx):
        greet(bar, head=(x + k) % nx)
    for k in range(1, ga):
        greet(bar, seq=me_b * ga + (me_a + k) % ga)
    for k in range(1, gb):
        greet(bar, seq=((me_b + k) % gb) * ga + me_a)
    greet(bar, seq=prev)
    greet(bar, seq=after)
    greet(bar, seq=prev, head=nx - 1)

    @pl.when(x == nx - 1)
    def _():
        for j in range(nx):
            greet(bar, seq=after, head=j)

    local_tok = pltpu.make_async_copy(tok, g.at[x], s_tok)
    local_tok.start()
    local_go = pltpu.make_async_copy(go, go_v, s_go)
    local_go.start()
    small = [
        pltpu.make_async_copy(src, dst, s_const.at[i])
        for i, (src, dst) in enumerate(
            ((cv_hbm, cv), (selq_hbm, selq), (selk_hbm, selk), (gmq_hbm, gmq), (gmk_hbm, gmk))
        )
    ]
    for copy in small:
        copy.start()
    loads = []
    for h in range(nh):
        base = h * CHAN
        loads.append(
            pltpu.make_async_copy(
                wt.at[base + 2 * F : base + CHAN], w.at[h * E : (h + 1) * E], s_w
            )
        )
        loads.append(
            pltpu.make_async_copy(
                wt.at[base : base + 2 * F],
                w.at[nh * E + 2 * F * h : nh * E + 2 * F * (h + 1)],
                s_w,
            )
        )
    for copy in loads:
        copy.start()
    greeted = nx - 1 + ga - 1 + gb - 1 + 3
    pl.semaphore_wait(bar, jnp.where(x == nx - 1, greeted + nx, greeted))

    def chunk(c):
        return pl.ds(c * ch, ch)

    def own(way, c, first):
        return remote(
            tok.at[chunk(c)],
            g.at[x, chunk(c)],
            s_own.at[0 if first else 1],
            r_own.at[way, c % 2] if first else r_rest.at[way],
            head=right if way == 0 else left,
        )

    def forward(way, c):
        slot = left if way == 0 else right
        return remote(
            g.at[slot, chunk(c)],
            g.at[slot, chunk(c)],
            s_fwd,
            r_fwd,
            head=right if way == 0 else left,
        )

    def halo(j):
        return remote(tok.at[pl.ds(rows - 16, 16)], hal, s_hal, r_hal, seq=after, head=j)

    step0, step1, step2, step3, step4, step5, step6, step7 = weight_gather(
        nx, ny, nz, x, y, z, core, w, wf, sems
    )
    pltpu.make_async_copy(w, w, s_w).wait()
    step0()
    own(0, 0, True).start()
    own(1, 2, True).start()
    @pl.when(x == nx - 1)
    def _():
        for j in range(nx):
            halo(j).start()

    lane = lax.broadcasted_iota(jnp.int32, (BLK, BLK), 1)
    sub = lax.broadcasted_iota(jnp.int32, (BLK, BLK), 0)
    frow = lax.broadcasted_iota(jnp.int32, (FS, E), 0)

    for copy in small:
        copy.wait()

    for j in range(3):
        lines = [cv[j, h : h + 1, :] for h in range(nh)]
        for h in range(nh):
            taps[j : j + 1, h * E : (h + 1) * E] = lines[h][:, 2 * F :]
        taps[j : j + 1, nh * E :] = jnp.concatenate([v[:, : 2 * F] for v in lines], 1) * KAPPA

    def rows_of(a):
        return pl.ds(pl.multiple_of(a * piece, 16), piece)

    def first(e, k):
        a = (me_a + k) % ga
        return remote(
            loc.at[e, rows_of(a)], r1.at[e, me_a], s1.at[e], q1.at[e], seq=me_b * ga + a
        )

    def second(e, k):
        b = (me_b + k) % gb
        return remote(tot.at[e], r2.at[e, me_b], s2.at[e], q2.at[e], seq=b * ga + me_a)

    def third(e, k):
        a = (me_a + k) % ga
        return remote(
            out.at[e, a], res.at[e, rows_of(me_a)], s3.at[e], q3.at[e], seq=me_b * ga + a
        )

    def exchange_first(e):
        for k in range(1, ga):
            first(e, k).start()
        r1[e, me_a] = loc[e, rows_of(me_a), :]

    def exchange_second(e):
        arrived(r1.at[e, pl.ds(0, ga - 1)], q1.at[e])
        total = jnp.zeros((piece, E), f32)
        for a in range(ga):
            total = total + r1[e, a].astype(f32)
        tot[e] = total.astype(bf16)
        for k in range(1, gb):
            second(e, k).start()

    def exchange_third(e):
        arrived(r2.at[e, pl.ds(0, gb - 1)], q2.at[e])
        r2[e, me_b] = tot[e]
        total = jnp.zeros((piece, E), f32)
        for b in range(gb):
            ahead = b < me_b if e < 2 else b > me_b
            total = total + jnp.where(ahead, r2[e, b].astype(f32), 0.0)
        for step in range(ga):
            a = step if e < 2 else ga - 1 - step
            out[e, a] = total.astype(bf16)
            total = total + r1[e, a].astype(f32)
        for k in range(1, ga):
            third(e, k).start()
        res[e, rows_of(me_a), :] = out[e, me_a]

    def exchange_done(e):
        arrived(res.at[e, pl.ds(0, (ga - 1) * piece)], q3.at[e])

    def pack(e, h, whole):
        column = jnp.concatenate([whole[:, E:], jnp.zeros((2 * E - FS, E), f32)], 0)
        line = column.T[0:1, :]
        body = jnp.where(frow == NF, line[:, :E], jnp.where(frow == NF + 1, line[:, E:], whole[:, :E]))
        loc[e, h * FS : (h + 1) * FS, :] = body.astype(bf16)

    def pack_group(e):
        for j in range(gh):
            h = (e % 2) * gh + j
            whole = ub[h * nb]
            for b in range(1, nb):
                whole = whole + ub[h * nb + b]
            pack(e, j, whole)
        if gh * FS < loc.shape[1]:
            loc[e, gh * FS :, :] = jnp.zeros((loc.shape[1] - gh * FS, E), bf16)

    def unpack_group(e):
        for j in range(gh):
            body = res[e, j * FS : (j + 1) * FS, :].astype(f32)
            line = jnp.concatenate([body[NF : NF + 1, :], body[NF + 1 : NF + 2, :]], 1)
            column = jnp.broadcast_to(line, (E, 2 * E)).T[:FS, :]
            run[(e % 2) * gh + j] = jnp.concatenate([jnp.where(frow < NF, body, 0.0), column], 1)

    def factors(u, sel):
        high = u.astype(bf16)
        low = (u - high.astype(f32)).astype(bf16)
        stack = jnp.concatenate([high, low, jnp.ones((F, BLK), bf16)], 0)
        both = dot(sel[...], stack)
        return both[:FS], both[FS:]

    def block_at(b):
        return pl.ds(pl.multiple_of(b * BLK, BLK), BLK)

    def convolve(b):
        ext = p[pl.ds(pl.multiple_of(b * BLK, BLK), BLK + 16), :]
        conv = taps[0:1, :] * ext[16:] + taps[1:2, :] * ext[15:-1] + taps[2:3, :] * ext[14:-2]
        qkt[:, block_at(b)] = conv[:, nh * E :].T
        for h in range(nh):
            vaug[h * nb + b] = jnp.concatenate(
                [conv[:, h * E : (h + 1) * E].astype(bf16), jnp.ones((BLK, E), bf16)], 1
            )

    def featurize(b, group):
        for j in range(gh):
            h = group * gh + j
            i = h * nb + b
            at = block_at(b)
            first_q, second_q = factors(qkt[2 * F * h : 2 * F * h + F, at], selq)
            first_k, second_k = factors(qkt[2 * F * h + F : 2 * F * (h + 1), at], selk)
            q = (first_q * second_q).astype(bf16)
            k = (first_k * second_k).astype(bf16)
            fqt[i] = q
            fkt[i] = k
            fq[i] = q.T
            fk[i] = k.T
            ub[i] = dot(k, vaug[i])

    def project(slot):
        base = pl.multiple_of(slot * rows, rows)
        p[pl.ds(16 + base, rows), :] = dot(g[slot], w[...], NT)

    def turn(slot):
        base = pl.multiple_of(slot * rows, rows)

        def piece_of(i, carry):
            at = pl.ds(pl.multiple_of(i * 256, 256), 256)
            gt[at, pl.ds(base, rows)] = g[slot, :, at].T
            return carry

        lax.fori_loop(0, depth // 256, piece_of, 0)

    local_tok.wait()
    project(x)
    turn(x)
    step1()
    own(0, 1, True).start()
    own(1, 3, True).start()
    own(0, 2, False).start()
    own(1, 0, False).start()
    step2()
    sent(tok, s_own.at[0])
    own(0, 3, False).start()
    own(1, 1, False).start()
    for c in range(2):
        arrived(g.at[left, chunk(c)], r_own.at[0, c])
        forward(0, c).start()
        arrived(g.at[right, chunk(c + 2)], r_own.at[1, c])
        forward(1, c + 2).start()
    step3()
    arrived(hal, r_hal)
    head_rows = dot(hal[...], w[...], NT)
    p[0:16, :] = jnp.where(s == 0, 0.0, head_rows)

    def turn_halo(i, carry):
        at = pl.ds(pl.multiple_of(i * 256, 256), 256)
        tail_rows = jnp.concatenate([hal[:, at], jnp.zeros((E - 16, 256), bf16)], 0)
        gt[at, nb * BLK :] = tail_rows.T
        return carry

    lax.fori_loop(0, depth // 256, turn_halo, 0)
    arrived(g.at[left, pl.ds(0, 2 * ch)], r_rest.at[0])
    project(left)
    arrived(g.at[right, pl.ds(0, 2 * ch)], r_rest.at[1])
    project(right)
    step4()
    for b in (x, right):
        convolve(b)
        featurize(b, 0)
        featurize(b, 1)
    arrived(g.at[opp], r_fwd)
    project(opp)
    for b in (opp, left):
        convolve(b)
        featurize(b, 0)
    pack_group(0)
    exchange_first(0)
    for b in (opp, left):
        featurize(b, 1)
    pack_group(1)
    exchange_first(1)

    def inside(i, carry):
        score = jnp.where(sub >= lane, dot(fq[i], fkt[i]), 0.0).astype(bf16)
        scot[i] = jnp.where(lane >= sub, dot(fk[i], fqt[i]), 0.0).astype(bf16)
        nin[i] = dot(score, vaug[i])
        return carry

    def quarter(n, body):
        lax.fori_loop(n * per // 2, (n + 1) * per // 2, body, 0, unroll=True)

    for slot in (opp, left, right):
        turn(slot)
    quarter(0, inside)
    exchange_second(0)
    quarter(1, inside)
    exchange_second(1)
    quarter(2, inside)
    exchange_third(0)
    quarter(3, inside)
    exchange_third(1)

    ones = jnp.ones((2 * E, E), bf16)

    def attend(group):
        for b in range(nb):
            for j in range(gh):
                h = group * gh + j
                i = h * nb + b
                state = run[h]
                state_b = state.astype(bf16)
                run[h] = state + ub[i]
                both = dot(fq[i], state_b) + nin[i]
                num = both[:, :E]
                inv = 1.0 / both[:, E:]
                mean = num * inv
                at = (slice(b * BLK, (b + 1) * BLK), slice(h * E, (h + 1) * E))
                att_v[at] = mean.astype(bf16)
                scaled = go_v[at].astype(f32) * inv
                product = scaled * mean
                high = product.astype(bf16)
                low = (product - high.astype(f32)).astype(bf16)
                slope = dot(jnp.concatenate([high, low], 1), ones) * (-1.0 / E)
                ga_b = jnp.concatenate([scaled.astype(bf16), slope.astype(bf16)], 1)
                gna[i] = ga_b
                st[i] = state_b
                ub[i] = dot(fqt[i], ga_b)
        pack_group(2 + group)

    def att_out(group):
        at = pl.ds(group * gh * E, gh * E)
        return pltpu.make_async_copy(att_v.at[:, at], att.at[:, at], s_att)

    local_go.wait()
    for group in range(2):
        exchange_done(group)
        unpack_group(group)
        attend(group)
        exchange_first(2 + group)
        att_out(group).start()

    def feature_gradient(u, sel, gm, grad):
        one, two = factors(u, sel)
        stack = jnp.concatenate([(grad * two).astype(bf16), (grad * one).astype(bf16)], 0)
        return dot(gm[...], stack)

    def inside_back(i, carry):
        h, b = i // nb, i % nb
        ga_b = gna[i]
        va = vaug[i]
        mix = jnp.where(sub >= lane, dot(ga_b, va, NT), 0.0).astype(bf16)
        mixt = mix.T
        gfq = dot(st[i], ga_b, NT) + dot(fkt[i], mixt)
        at = (pl.ds(pl.multiple_of(h * 2 * F, 2 * F), F), block_at(b))
        gq = feature_gradient(qkt[at], selq, gmq, gfq)
        pfk[i] = dot(fqt[i], mix)
        qkt[at] = gq
        nin[i, :, :E] = dot(scot[i], ga_b[:, :E])
        return carry

    step5()
    quarter(0, inside_back)
    exchange_second(2)
    quarter(1, inside_back)
    exchange_second(3)
    quarter(2, inside_back)
    exchange_third(2)
    quarter(3, inside_back)
    exchange_third(3)

    def value_gradient(group):
        for b in reversed(range(nb)):
            for j in range(gh):
                h = group * gh + j
                i = h * nb + b
                state = run[h]
                state_b = state.astype(bf16)
                st[i] = state_b
                run[h] = state + ub[i]
                rows_b = slice(b * BLK, (b + 1) * BLK)
                p[rows_b, h * E : (h + 1) * E] = dot(fk[i], state_b[:, :E]) + nin[i, :, :E]

    def key_gradient(b):
        rows_b = slice(b * BLK, (b + 1) * BLK)
        for h in range(nh):
            i = h * nb + b
            gfk = dot(st[i], vaug[i], NT) + pfk[i]
            at = (slice(2 * F * h + F, 2 * F * (h + 1)), rows_b)
            qkt[at] = feature_gradient(qkt[at], selk, gmk, gfk)
        p[rows_b, nh * E :] = qkt[:, rows_b].T

    total_rows = nb * BLK
    width = gp.shape[1]
    lanes = ((0, gh * E), (gh * E, nh * E), (nh * E, width))

    def spread(part):
        lo, up = lanes[part]
        one, two, three = taps[0:1, lo:up], taps[1:2, lo:up], taps[2:3, lo:up]
        p[total_rows:, lo:up] = jnp.zeros((16, up - lo), f32)
        for b in range(nb):
            ext = p[b * BLK : (b + 1) * BLK + 16, lo:up]
            grad = one * ext[:BLK] + two * ext[1 : BLK + 1] + three * ext[2 : BLK + 2]
            gp[b * BLK : (b + 1) * BLK, lo:up] = grad.astype(bf16)
        edge = jnp.concatenate([jnp.zeros((16, up - lo), f32), p[0:16, lo:up]], 0)
        edge = jnp.where(s == 0, 0.0, two * edge[1:17] + three * edge[2:18])
        gp[total_rows : total_rows + 16, lo:up] = edge.astype(bf16)
        gp[total_rows + 16 :, lo:up] = jnp.zeros((E - 16, up - lo), bf16)

    def rows_at(j):
        return pl.ds(pl.multiple_of(j * rows, rows), rows)

    def part_of(part):
        return pl.ds(lanes[part][0], lanes[part][1] - lanes[part][0])

    def back(part):
        return remote(
            gp.at[pl.ds(total_rows, 16), part_of(part)],
            hi.at[(x + 1) % nx, :, part_of(part)],
            sh.at[part],
            qh.at[part],
            seq=prev,
            head=nx - 1,
        )

    def over(part, k):
        j = (x + k) % nx
        return remote(
            gp.at[rows_at(j), part_of(part)],
            gin.at[:, pl.ds((nx - k) * width + lanes[part][0], lanes[part][1] - lanes[part][0])],
            sx.at[part],
            qx.at[part],
            head=j,
        )

    def send_rows(part):
        for k in (2, 1, 3):
            over(part, k).start()
        back(part).start()

    pieces = ny * nz
    height = gwb.shape[2]
    half = height // 2
    per_step = 512 // (2 * height)
    low_half, high_half = pl.ds(0, half), pl.ds(half, half)

    def pair(part, j):
        at = part_of(part)
        return remote(
            gwb.at[j, 1 - core, :, at], rp.at[j, :, at], sp.at[part], qp.at[part], seq=sibling
        )

    def weight_part(part):
        lo, up = lanes[part]

        def weight_step(i, carry):
            at = pl.ds(pl.multiple_of(i * 512, 512), 512)
            whole = dot(gt[at, :], gp[:, lo:up]).astype(bf16)
            whole = whole.reshape(per_step, 2, height, up - lo)
            for q in range(per_step):
                gwb[i * per_step + q, :, :, lo:up] = whole[q]
                pair(part, i * per_step + q).start()
            return carry

        lax.fori_loop(0, pieces // per_step, weight_step, 0)

    def go_2a(part, k):
        to, at = (z + k) % nz, part_of(part)
        return remote(
            t.at[:, to, low_half, at],
            r2a.at[k, :, :, at],
            s2a.at[part],
            q2a.at[part],
            seq=at_seq(y, to, core),
        )

    def go_2b(part, k):
        to, at = (y + k) % ny, part_of(part)
        return remote(
            t.at[to, :, high_half, at],
            r2b.at[k, :, :, at],
            s2b.at[part],
            q2b.at[part],
            seq=at_seq(to, z, core),
        )

    def go_3a(part, k):
        to, at = (y + k) % ny, part_of(part)
        return remote(
            va.at[to, :, at],
            r3a.at[k, :, at],
            s3a.at[part],
            q3a.at[part],
            seq=at_seq(to, z, core),
        )

    def go_3b(part, k):
        to, at = (z + k) % nz, part_of(part)
        return remote(
            vb.at[to, :, at],
            r3b.at[k, :, at],
            s3b.at[part],
            q3b.at[part],
            seq=at_seq(y, to, core),
        )

    def weight_second(part):
        lo, up = lanes[part]

        def pair_sum(j, carry):
            both = gwb[j, core, :, lo:up].astype(f32) + rp[j, :, lo:up].astype(f32)
            t[j // nz, j % nz, :, lo:up] = both.astype(bf16)
            return carry

        arrived(rp.at[:, :, part_of(part)], qp.at[part])
        lax.fori_loop(0, pieces, pair_sum, 0)
        for k in range(1, max(ny, nz)):
            if k < nz:
                go_2a(part, k).start()
            if k < ny:
                go_2b(part, k).start()

    def weight_third(part):
        lo, up = lanes[part]
        at = part_of(part)
        arrived(r2a.at[pl.ds(1, nz - 1), :, :, at], q2a.at[part])
        arrived(r2b.at[pl.ds(1, ny - 1), :, :, at], q2b.at[part])
        for i in range(ny):
            total = t[i, z, 0:half, lo:up].astype(f32)
            for k in range(1, nz):
                total = total + r2a[k, i, :, lo:up].astype(f32)
            va[i, :, lo:up] = total.astype(bf16)
        for i in range(nz):
            total = t[y, i, half:, lo:up].astype(f32)
            for k in range(1, ny):
                total = total + r2b[k, i, :, lo:up].astype(f32)
            vb[i, :, lo:up] = total.astype(bf16)
        for k in range(1, max(ny, nz)):
            if k < ny:
                go_3a(part, k).start()
            if k < nz:
                go_3b(part, k).start()

    exchange_done(2)
    unpack_group(2)
    value_gradient(0)
    spread(0)
    send_rows(0)
    weight_part(0)
    exchange_done(3)
    unpack_group(3)
    value_gradient(1)
    spread(1)
    send_rows(1)
    weight_second(0)
    for b in range(nb):
        key_gradient(b)
    spread(2)
    send_rows(2)
    weight_part(1)
    weight_second(1)
    weight_part(2)
    weight_third(0)

    steps = depth // 256

    def load(i, slot):
        at = pl.ds(pl.multiple_of(i * 256, 256), 256)
        for j in range(nx):
            src = w.at[:, at] if j == 0 else wf.at[j - 1, :, at]
            dst = wbuf.at[slot, pl.ds(j * width, width)]
            pltpu.make_async_copy(src, dst, sw.at[slot]).start()

    def three(part):
        return gin.at[:, pl.ds(0, (nx - 1) * (lanes[part][1] - lanes[part][0]))]

    def gi_out(i):
        at = pl.ds(pl.multiple_of(i * 256, 256), 256)
        return pltpu.make_async_copy(gi_v.at[:, at], gi.at[:, at], s_gi)

    step6()
    load(0, 0)
    load(1, 1)
    weight_second(2)
    gin[:, :width] = gp[rows_at(x), :]
    for part in range(3):
        arrived(three(part), qx.at[part])

    @pl.when(x == nx - 1)
    def _():
        for part in range(3):
            arrived(hi.at[:, :, part_of(part)], qh.at[part])
        for k in range(nx):
            at = slice(k * width, (k + 1) * width)
            last = gin[rows - 16 :, at].astype(f32) + hi[k].astype(f32)
            gin[rows - 16 :, at] = last.astype(bf16)

    def input_step(i, carry):
        at = pl.ds(pl.multiple_of(i * 256, 256), 256)
        slot = i % 2
        pltpu.make_async_copy(wbuf.at[slot], wbuf.at[slot], sw.at[slot]).wait()
        gi_v[:, at] = dot(gin[...], wbuf[slot]).astype(bf16)
        gi_out(i).start()

        @pl.when(i + 2 < steps)
        def _():
            load(i + 2, slot)

        return carry

    lax.fori_loop(0, steps // 4, input_step, 0)
    weight_third(1)
    lax.fori_loop(steps // 4, 5 * steps // 8, input_step, 0)
    weight_third(2)
    lax.fori_loop(5 * steps // 8, steps, input_step, 0)

    for part in range(3):
        at = part_of(part)
        arrived(r3a.at[pl.ds(1, ny - 1), :, at], q3a.at[part])
        arrived(r3b.at[pl.ds(1, nz - 1), :, at], q3b.at[part])

    def put(at, total):
        for h in range(nh):
            narrow = total[:, nh * E + 2 * F * h : nh * E + 2 * F * (h + 1)]
            gw_v[at, h, :] = jnp.concatenate([narrow, total[:, h * E : (h + 1) * E]], 1)

    total = va[y].astype(f32)
    for k in range(1, ny):
        total = total + r3a[k].astype(f32)
    put(slice(0, half), total)
    total = vb[z].astype(f32)
    for k in range(1, nz):
        total = total + r3b[k].astype(f32)
    put(slice(half, height), total)
    gw_out = pltpu.make_async_copy(gw_v, gw, s_gw)
    gw_out.start()

    for part in range(3):
        at = part_of(part)
        back(part).wait_send()
        sent(three(part), sx.at[part])
        sent(rp.at[:, :, at], sp.at[part])
        sent(r2a.at[pl.ds(1, nz - 1), :, :, at], s2a.at[part])
        sent(r2b.at[pl.ds(1, ny - 1), :, :, at], s2b.at[part])
        sent(r3a.at[pl.ds(1, ny - 1), :, at], s3a.at[part])
        sent(r3b.at[pl.ds(1, nz - 1), :, at], s3b.at[part])
    for e in range(4):
        sent(r1.at[e, pl.ds(0, ga - 1)], s1.at[e])
        sent(r2.at[e, pl.ds(0, gb - 1)], s2.at[e])
        sent(res.at[e, pl.ds(0, (ga - 1) * piece)], s3.at[e])
    sent(tok, s_own.at[1])
    sent(g.at[opp], s_fwd)

    @pl.when(x == nx - 1)
    def _():
        sent(tok.at[pl.ds(0, 16 * nx)], s_hal)

    step7()
    pltpu.make_async_copy(att_v, att, s_att).wait()
    pltpu.make_async_copy(gi_v, gi, s_gi).wait()
    gw_out.wait()


def hand_on_kernel(count, *refs):
    srcs, dsts, held = refs[:count], refs[count : 2 * count], refs[2 * count : 3 * count]
    come, leave = refs[3 * count :]
    cuts = come.shape[1]

    def slices(i, c):
        size = srcs[i].shape[0] // cuts
        at = pl.ds(c * size, size)
        return (
            pltpu.make_async_copy(srcs[i].at[at], held[i].at[at], come.at[i, c]),
            pltpu.make_async_copy(held[i].at[at], dsts[i].at[at], leave.at[i, c]),
        )

    every = [slices(i, c) for c in range(cuts) for i in range(count)]
    for first, _ in every:
        first.start()
    for first, second in every:
        first.wait()
        second.start()
    for _, second in every:
        second.wait()


def hand_on(*arrays):
    hbm = pl.BlockSpec(memory_space=pl.ANY)
    count = len(arrays)
    return pl.pallas_call(
        functools.partial(hand_on_kernel, count),
        out_shape=tuple(jax.ShapeDtypeStruct(a.shape, a.dtype) for a in arrays),
        in_specs=[hbm] * count,
        out_specs=(hbm,) * count,
        scratch_shapes=[pltpu.VMEM(a.shape, a.dtype) for a in arrays]
        + [pltpu.SemaphoreType.DMA((count, 4))] * 2,
        compiler_params=pltpu.CompilerParams(vmem_limit_bytes=60 * 2**20),
    )(*arrays)


def local(nx, ny, nz, tokens, in_weight, conv_kernel, grad_out):
    depth, nh, _ = in_weight.shape
    wt = jnp.transpose(in_weight, (1, 2, 0)).reshape(nh * CHAN, depth)
    rows = tokens.shape[0]
    every = grad_out.shape[0]
    width = nh * CHAN
    nb = every // BLK
    n = nh * nb
    ga, gb, ns = 2 * nz, ny, 2 * ny * nz
    piece = -(-(nh // 2) * FS // (16 * ga)) * 16
    height = depth // ns
    half = height // 2
    hbm = pl.BlockSpec(memory_space=pl.ANY)
    dma = pltpu.SemaphoreType.DMA
    consts = [
        jnp.asarray(selection(True), bf16),
        jnp.asarray(selection(False), bf16),
        jnp.asarray(gradient_map(True), bf16),
        jnp.asarray(gradient_map(False), bf16),
    ]
    att, gi, gw, _ = pl.pallas_call(
        functools.partial(kernel, nx, ny, nz, nh),
        out_shape=(
            jax.ShapeDtypeStruct((every, nh * E), bf16),
            jax.ShapeDtypeStruct((rows, depth), bf16),
            jax.ShapeDtypeStruct((height, nh, CHAN), f32),
            jax.ShapeDtypeStruct((nx - 1, width, depth), bf16),
        ),
        in_specs=[hbm] * 8,
        out_specs=(hbm, hbm, hbm, hbm),
        scratch_shapes=[
            pltpu.VMEM(conv_kernel.shape, f32),
            pltpu.VMEM((2 * FS, 3 * F), bf16),
            pltpu.VMEM((2 * FS, 3 * F), bf16),
            pltpu.VMEM((F, 2 * FS), bf16),
            pltpu.VMEM((F, 2 * FS), bf16),
            pltpu.VMEM((every, nh * E), bf16),
            pltpu.VMEM((every, nh * E), bf16),
            pltpu.VMEM((rows, depth), bf16),
            pltpu.VMEM((height, nh, CHAN), f32),
            pltpu.VMEM((width, depth), bf16),
            pltpu.VMEM((nx, rows, depth), bf16),
            pltpu.VMEM((depth, every + E), bf16),
            pltpu.VMEM((16 + every, width), f32),
            pltpu.VMEM((16, depth), bf16),
            pltpu.VMEM((8, width), f32),
            pltpu.VMEM((nh * 2 * F, every), f32),
            pltpu.VMEM((n, BLK, 2 * E), bf16),
            pltpu.VMEM((n, FS, BLK), bf16),
            pltpu.VMEM((n, FS, BLK), bf16),
            pltpu.VMEM((n, BLK, FS), bf16),
            pltpu.VMEM((n, BLK, FS), bf16),
            pltpu.VMEM((n, FS, 2 * E), f32),
            pltpu.VMEM((n, BLK, 2 * E), f32),
            pltpu.VMEM((n, BLK, BLK), bf16),
            pltpu.VMEM((n, BLK, 2 * E), bf16),
            pltpu.VMEM((nh, FS, 2 * E), f32),
            pltpu.VMEM((n, FS, 2 * E), bf16),
            pltpu.VMEM((n, FS, BLK), f32),
            pltpu.VMEM((every + E, width), bf16),
            pltpu.VMEM((4, ga * piece, E), bf16),
            pltpu.VMEM((4, ga, piece, E), bf16),
            pltpu.VMEM((4, piece, E), bf16),
            pltpu.VMEM((4, gb, piece, E), bf16),
            pltpu.VMEM((4, ga, piece, E), bf16),
            pltpu.VMEM((4, ga * piece, E), bf16),
            pltpu.VMEM((2, nx * width, 256), bf16),
            pltpu.VMEM((rows, nx * width), bf16),
            pltpu.VMEM((nx, 16, width), bf16),
            pltpu.VMEM((ny * nz, 2, height, width), bf16),
            pltpu.VMEM((ny * nz, height, width), bf16),
            pltpu.VMEM((ny, nz, height, width), bf16),
            pltpu.VMEM((nz, ny, half, width), bf16),
            pltpu.VMEM((ny, nz, half, width), bf16),
            pltpu.VMEM((ny, half, width), bf16),
            pltpu.VMEM((nz, half, width), bf16),
            pltpu.VMEM((ny, half, width), bf16),
            pltpu.VMEM((nz, half, width), bf16),
            dma((2,)),
            dma((2, 2)),
            dma((2,)),
            dma(()),
            dma(()),
            dma(()),
            dma(()),
            dma(()),
            dma(()),
            dma((4,)),
            dma((4,)),
            dma((4,)),
            dma((4,)),
            dma((4,)),
            dma((4,)),
            dma((2,)),
            dma((3,)),
            dma((3,)),
            dma((3,)),
            dma((3,)),
            dma((3,)),
            dma((3,)),
            dma((3,)),
            dma((3,)),
            dma((3,)),
            dma((3,)),
            dma((3,)),
            dma((3,)),
            dma((3,)),
            dma((3,)),
            dma(()),
            dma(()),
            dma(()),
            dma(()),
            dma((5,)),
            dma(()),
            dma(()),
            dma(()),
            dma(()),
            dma(()),
            dma(()),
            dma(()),
            dma(()),
            dma((ny,)),
            dma((ny,)),
            dma((nz,)),
            dma((nz,)),
            dma(()),
            dma(()),
            dma(()),
            dma(()),
            dma((2,)),
            dma((2,)),
        ],
        compiler_params=pltpu.CompilerParams(
            collective_id=0, has_side_effects=True, vmem_limit_bytes=62 * 2**20
        ),
    )(tokens, wt, conv_kernel, grad_out, *consts)
    return hand_on(att, gi, gw)


def solution(mesh):
    nx, ns = mesh.shape["head"], mesh.shape["seq"]
    ny = math.isqrt(ns // 2)
    nz = ns // 2 // ny
    placed = (
        P(("seq", "head"), None),
        P(None, "head", None),
        P(None, "head", None),
        P("seq", "head"),
    )
    return jax.shard_map(
        functools.partial(local, nx, ny, nz),
        mesh=mesh,
        in_specs=placed,
        out_specs=(P("seq", "head"), P(("seq", "head"), None), P("seq", "head", None)),
        check_vma=False,
    )
```

```python
import functools
import math

import jax
import jax.numpy as jnp
import numpy as np
from jax import lax
from jax.experimental import pallas as pl
from jax.experimental.pallas import tpu as pltpu
from jax.sharding import PartitionSpec as P

F = 16
E = 128
BLK = 256
CHAN = 160
FS = 160
NF = 1 + F + F * (F + 1) // 2
KAPPA = 32.0 ** -0.25
f32 = jnp.float32
bf16 = jnp.bfloat16
NN = (((1,), (0,)), ((), ()))
NT = (((1,), (1,)), ((), ()))


def dot(a, b, dims=NN):
    return lax.dot_general(a, b, dims, preferred_element_type=f32)


def bf_parts(value, count):
    parts = []
    rest = np.float64(value)
    for _ in range(count):
        part = np.float64(np.asarray(rest, dtype=jnp.bfloat16))
        parts.append(part)
        rest = rest - part
    return parts


def selection(weighted):
    sel = np.zeros((2 * FS, 3 * F), np.float64)
    sel[0, 32] = 1.0
    sel[FS, 32] = 1.0
    for i in range(F):
        row = 1 + i
        sel[row, i] = sel[row, F + i] = 1.0
        for c, part in enumerate(bf_parts(0.5 / KAPPA, 3)):
            sel[FS + row, 32 + c] = part
    row = 1 + F
    for i in range(F):
        for j in range(i, F):
            first = 2.0 if (weighted and j > i) else 1.0
            sel[row, i] = sel[row, F + i] = first
            sel[FS + row, j] = sel[FS + row, F + j] = 1.0
            row += 1
    return sel


def gradient_map(weighted):
    sel = selection(weighted)
    return np.concatenate([sel[:FS, :F].T, sel[FS:, :F].T], 1)


def remote(src, dst, send, recv, **where):
    return pltpu.make_async_remote_copy(
        src_ref=src,
        dst_ref=dst,
        send_sem=send,
        recv_sem=recv,
        device_id=where,
        device_id_type=pl.DeviceIdType.MESH,
    )


def arrived(ref, sem):
    remote(ref, ref, sem, sem, seq=lax.axis_index("seq")).wait_recv()


def sent(ref, sem):
    remote(ref, ref, sem, sem, seq=lax.axis_index("seq")).wait_send()


def greet(sem, **where):
    pl.semaphore_signal(sem, inc=1, device_id=where, device_id_type=pl.DeviceIdType.MESH)


def weight_gather(nx, ny, nz, x, y, z, core, w, wf, sems):
    s1, q1, sr, qr, sa, qa, sb, qb, sc, qc, sd, qd, sf, qf, sg, qg, se, qe = sems
    chan, depth = w.shape
    half = chan // 2
    quarter = half // 2
    eighth = quarter // 2
    col = depth // (ny * nz)
    base = core * half
    rows_c = pl.ds(pl.multiple_of(base, 16), half)
    rows_a = pl.ds(pl.multiple_of(base, 16), quarter)
    rows_b = pl.ds(pl.multiple_of(base + quarter, 16), quarter)
    far = pl.ds(0, nx - 1)

    def piece_a(n):
        return pl.ds(pl.multiple_of(base + n * eighth, 16), eighth)

    def piece_b(n):
        return pl.ds(pl.multiple_of(base + quarter + n * eighth, 16), eighth)

    def cols(yy, zz):
        return pl.ds(pl.multiple_of((yy * nz + zz) * col, 128), col)

    def row_of(yy):
        return pl.ds(pl.multiple_of(yy * nz * col, 128), nz * col)

    def at_seq(yy, zz, cc):
        return (yy * nz + zz) * 2 + cc

    mine = cols(y, z)
    ring_y = (1, ny - 1) if ny > 2 else (1,)
    ring_z = (1, nz - 1) if nz > 2 else (1,)

    def spread_x(k):
        return remote(w.at[rows_c, mine], wf.at[nx - k - 1, rows_c, mine], s1, q1, head=(x + k) % nx)

    def spread_on(k):
        here = wf.at[nx - k - 1, rows_a if k == 1 else rows_b, mine]
        there = wf.at[nx // 2 - 1, rows_a if k == 1 else rows_b, mine]
        return remote(here, there, sr, qr, head=(x + k) % nx)

    def a_z(k):
        here = wf.at[far, rows_a, mine]
        return remote(here, here, sa, qa, seq=at_seq(y, (z + k) % nz, core))

    def b_y(k):
        here = wf.at[far, rows_b, mine]
        return remote(here, here, sb, qb, seq=at_seq((y + k) % ny, z, core))

    def a_y(k):
        here = wf.at[far, rows_a, row_of(y)]
        return remote(here, here, sc.at[k], qc.at[k], seq=at_seq((y + k) % ny, z, core))

    def b_z(k, yy):
        here = wf.at[far, rows_b, cols(yy, z)]
        return remote(here, here, sd.at[k], qd.at[k], seq=at_seq(y, (z + k) % nz, core))

    def a_y_on(k):
        here = wf.at[far, piece_a(0 if k == 1 else 1), row_of((y - k) % ny)]
        return remote(here, here, sf, qf, seq=at_seq((y + k) % ny, z, core))

    def b_z_on(k, yy):
        here = wf.at[far, piece_b(0 if k == 1 else 1), cols(yy, (z - k) % nz)]
        return remote(here, here, sg, qg, seq=at_seq(y, (z + k) % nz, core))

    def across(part):
        here = wf.at[far, rows_a if part == 0 else rows_b]
        return remote(here, here, se.at[part], qe.at[part], seq=at_seq(y, z, 1 - core))

    def lanes(rows, count):
        return wf.at[far, rows, pl.ds(0, count * col)]

    def step0():
        for k in (1, nx - 1):
            spread_x(k).start()

    def step1():
        arrived(wf.at[pl.ds(0, 2), rows_c, mine], q1)
        for k in (1, nx - 1):
            spread_on(k).start()

    def step2():
        arrived(wf.at[0, rows_c, mine], qr)
        for k in range(1, max(ny, nz)):
            if k < nz:
                a_z(k).start()
            if k < ny:
                b_y(k).start()

    def step3():
        arrived(lanes(rows_a, nz - 1), qa)
        for k in ring_y:
            a_y(k).start()
        arrived(lanes(rows_b, ny - 1), qb)
        for k in ring_z:
            for yy in range(ny):
                b_z(k, yy).start()

    def step4():
        for k in ring_y:
            arrived(lanes(rows_a, nz), qc.at[ny - k])
            if ny > 2:
                a_y_on(ny - k).start()
        for k in ring_z:
            arrived(lanes(rows_b, ny), qd.at[nz - k])
            if nz > 2:
                for yy in range(ny):
                    b_z_on(nz - k, yy).start()

    def step5():
        if ny > 2:
            arrived(lanes(rows_a, nz), qf)
        across(0).start()
        if nz > 2:
            arrived(lanes(rows_b, ny), qg)
        across(1).start()

    def step6():
        across(0).wait_recv()
        across(1).wait_recv()

    def step7():
        sent(wf.at[pl.ds(0, 2), rows_c, mine], s1)
        sent(wf.at[0, rows_c, mine], sr)
        sent(lanes(rows_a, nz - 1), sa)
        sent(lanes(rows_b, ny - 1), sb)
        for k in ring_y:
            sent(lanes(rows_a, nz), sc.at[k])
        for k in ring_z:
            sent(lanes(rows_b, ny), sd.at[k])
        if ny > 2:
            sent(lanes(rows_a, nz), sf)
        if nz > 2:
            sent(lanes(rows_b, ny), sg)
        across(0).wait_send()
        across(1).wait_send()

    return step0, step1, step2, step3, step4, step5, step6, step7


def kernel(
    nx, ny, nz, nh,
    tok, wt, cv_hbm, go, selq_hbm, selk_hbm, gmq_hbm, gmk_hbm,
    att, gi, gw, wf,
    cv, selq, selk, gmq, gmk, go_v, att_v, gi_v, gw_v, w, g, gt, p, hal, taps, qkt, vaug, fqt, fkt, fq, fk, ub, nin, scot, gna, run, st, pfk, gp,
    loc, r1, tot, r2, out, res,
    wbuf, gin, relay, hi, gwb, rp, t, r2a, r2b, va, vb, r3a, r3b,
    s_own, r_own, r_rest, s_fwd, r_fwd, s_hal, r_hal, s_w, s_tok,
    s1, q1, s2, q2, s3, q3,
    sw, sr1, qr1, sr2, qr2, sx, qx, sh, qh, sp, qp, s2a, q2a, s2b, q2b, s3a, q3a, s3b, q3b, s_att, s_gi, s_gw, s_go, s_const,
    *sems,
):
    x = lax.axis_index("head")
    s = lax.axis_index("seq")
    ns = 2 * ny * nz
    core, z, y = s % 2, (s // 2) % nz, s // (2 * nz)
    left, right, opp = (x + nx - 1) % nx, (x + 1) % nx, (x + 2) % nx
    prev, after = (s + ns - 1) % ns, (s + 1) % ns
    ga, gb = 2 * nz, ny
    me_a, me_b = s % ga, s // ga
    rows, depth = tok.shape
    nb = go.shape[0] // BLK
    ch = rows // 4
    piece = loc.shape[1] // ga
    gh = nh // 2
    per = gh * nb

    def at_seq(yy, zz, cc):
        return (yy * nz + zz) * 2 + cc

    sibling = at_seq(y, z, 1 - core)
    bar = pltpu.get_barrier_semaphore()
    for k in range(1, nx):
        greet(bar, head=(x + k) % nx)
    for k in range(1, ga):
        greet(bar, seq=me_b * ga + (me_a + k) % ga)
    for k in range(1, gb):
        greet(bar, seq=((me_b + k) % gb) * ga + me_a)
    greet(bar, seq=prev)
    greet(bar, seq=after)
    greet(bar, seq=prev, head=nx - 1)

    @pl.when(x == nx - 1)
    def _():
        for j in range(nx):
            greet(bar, seq=after, head=j)

    local_tok = pltpu.make_async_copy(tok, g.at[x], s_tok)
    local_tok.start()
    local_go = pltpu.make_async_copy(go, go_v, s_go)
    local_go.start()
    small = [
        pltpu.make_async_copy(src, dst, s_const.at[i])
        for i, (src, dst) in enumerate(
            ((cv_hbm, cv), (selq_hbm, selq), (selk_hbm, selk), (gmq_hbm, gmq), (gmk_hbm, gmk))
        )
    ]
    for copy in small:
        copy.start()
    loads = []
    for h in range(nh):
        base = h * CHAN
        loads.append(
            pltpu.make_async_copy(
                wt.at[base + 2 * F : base + CHAN], w.at[h * E : (h + 1) * E], s_w
            )
        )
        loads.append(
            pltpu.make_async_copy(
                wt.at[base : base + 2 * F],
                w.at[nh * E + 2 * F * h : nh * E + 2 * F * (h + 1)],
                s_w,
            )
        )
    for copy in loads:
        copy.start()
    greeted = nx - 1 + ga - 1 + gb - 1 + 3
    pl.semaphore_wait(bar, jnp.where(x == nx - 1, greeted + nx, greeted))

    def chunk(c):
        return pl.ds(c * ch, ch)

    def own(way, c, first):
        return remote(
            tok.at[chunk(c)],
            g.at[x, chunk(c)],
            s_own.at[0 if first else 1],
            r_own.at[way, c % 2] if first else r_rest.at[way],
            head=right if way == 0 else left,
        )

    def forward(way, c):
        slot = left if way == 0 else right
        return remote(
            g.at[slot, chunk(c)],
            g.at[slot, chunk(c)],
            s_fwd,
            r_fwd,
            head=right if way == 0 else left,
        )

    def halo(j):
        return remote(tok.at[pl.ds(rows - 16, 16)], hal, s_hal, r_hal, seq=after, head=j)

    step0, step1, step2, step3, step4, step5, step6, step7 = weight_gather(
        nx, ny, nz, x, y, z, core, w, wf, sems
    )
    pltpu.make_async_copy(w, w, s_w).wait()
    step0()
    own(0, 0, True).start()
    own(1, 2, True).start()
    @pl.when(x == nx - 1)
    def _():
        for j in range(nx):
            halo(j).start()

    lane = lax.broadcasted_iota(jnp.int32, (BLK, BLK), 1)
    sub = lax.broadcasted_iota(jnp.int32, (BLK, BLK), 0)
    frow = lax.broadcasted_iota(jnp.int32, (FS, E), 0)

    for copy in small:
        copy.wait()

    for j in range(3):
        lines = [cv[j, h : h + 1, :] for h in range(nh)]
        for h in range(nh):
            taps[j : j + 1, h * E : (h + 1) * E] = lines[h][:, 2 * F :]
        taps[j : j + 1, nh * E :] = jnp.concatenate([v[:, : 2 * F] for v in lines], 1) * KAPPA

    def rows_of(a):
        return pl.ds(pl.multiple_of(a * piece, 16), piece)

    def first(e, k):
        a = (me_a + k) % ga
        return remote(
            loc.at[e, rows_of(a)], r1.at[e, me_a], s1.at[e], q1.at[e], seq=me_b * ga + a
        )

    def second(e, k):
        b = (me_b + k) % gb
        return remote(tot.at[e], r2.at[e, me_b], s2.at[e], q2.at[e], seq=b * ga + me_a)

    def third(e, k):
        a = (me_a + k) % ga
        return remote(
            out.at[e, a], res.at[e, rows_of(me_a)], s3.at[e], q3.at[e], seq=me_b * ga + a
        )

    def exchange_first(e):
        for k in range(1, ga):
            first(e, k).start()
        r1[e, me_a] = loc[e, rows_of(me_a), :]

    def exchange_second(e):
        arrived(r1.at[e, pl.ds(0, ga - 1)], q1.at[e])
        total = jnp.zeros((piece, E), f32)
        for a in range(ga):
            total = total + r1[e, a].astype(f32)
        tot[e] = total.astype(bf16)
        for k in range(1, gb):
            second(e, k).start()

    def exchange_third(e):
        arrived(r2.at[e, pl.ds(0, gb - 1)], q2.at[e])
        r2[e, me_b] = tot[e]
        total = jnp.zeros((piece, E), f32)
        for b in range(gb):
            ahead = b < me_b if e < 2 else b > me_b
            total = total + jnp.where(ahead, r2[e, b].astype(f32), 0.0)
        for step in range(ga):
            a = step if e < 2 else ga - 1 - step
            out[e, a] = total.astype(bf16)
            total = total + r1[e, a].astype(f32)
        for k in range(1, ga):
            third(e, k).start()
        res[e, rows_of(me_a), :] = out[e, me_a]

    def exchange_done(e):
        arrived(res.at[e, pl.ds(0, (ga - 1) * piece)], q3.at[e])

    def pack(e, h, whole):
        column = jnp.concatenate([whole[:, E:], jnp.zeros((2 * E - FS, E), f32)], 0)
        line = column.T[0:1, :]
        body = jnp.where(frow == NF, line[:, :E], jnp.where(frow == NF + 1, line[:, E:], whole[:, :E]))
        loc[e, h * FS : (h + 1) * FS, :] = body.astype(bf16)

    def pack_group(e):
        for j in range(gh):
            h = (e % 2) * gh + j
            whole = ub[h * nb]
            for b in range(1, nb):
                whole = whole + ub[h * nb + b]
            pack(e, j, whole)
        if gh * FS < loc.shape[1]:
            loc[e, gh * FS :, :] = jnp.zeros((loc.shape[1] - gh * FS, E), bf16)

    def unpack_group(e):
        for j in range(gh):
            body = res[e, j * FS : (j + 1) * FS, :].astype(f32)
            line = jnp.concatenate([body[NF : NF + 1, :], body[NF + 1 : NF + 2, :]], 1)
            column = jnp.broadcast_to(line, (E, 2 * E)).T[:FS, :]
            run[(e % 2) * gh + j] = jnp.concatenate([jnp.where(frow < NF, body, 0.0), column], 1)

    def factors(u, sel):
        high = u.astype(bf16)
        low = (u - high.astype(f32)).astype(bf16)
        stack = jnp.concatenate([high, low, jnp.ones((F, BLK), bf16)], 0)
        both = dot(sel[...], stack)
        return both[:FS], both[FS:]

    def block_at(b):
        return pl.ds(pl.multiple_of(b * BLK, BLK), BLK)

    def convolve(b):
        ext = p[pl.ds(pl.multiple_of(b * BLK, BLK), BLK + 16), :]
        conv = taps[0:1, :] * ext[16:] + taps[1:2, :] * ext[15:-1] + taps[2:3, :] * ext[14:-2]
        qkt[:, block_at(b)] = conv[:, nh * E :].T
        for h in range(nh):
            vaug[h * nb + b] = jnp.concatenate(
                [conv[:, h * E : (h + 1) * E].astype(bf16), jnp.ones((BLK, E), bf16)], 1
            )

    def featurize(b, group):
        for j in range(gh):
            h = group * gh + j
            i = h * nb + b
            at = block_at(b)
            first_q, second_q = factors(qkt[2 * F * h : 2 * F * h + F, at], selq)
            first_k, second_k = factors(qkt[2 * F * h + F : 2 * F * (h + 1), at], selk)
            q = (first_q * second_q).astype(bf16)
            k = (first_k * second_k).astype(bf16)
            fqt[i] = q
            fkt[i] = k
            fq[i] = q.T
            fk[i] = k.T
            ub[i] = dot(k, vaug[i])

    def project(slot):
        base = pl.multiple_of(slot * rows, rows)
        p[pl.ds(16 + base, rows), :] = dot(g[slot], w[...], NT)

    def turn(slot):
        base = pl.multiple_of(slot * rows, rows)

        def piece_of(i, carry):
            at = pl.ds(pl.multiple_of(i * 256, 256), 256)
            gt[at, pl.ds(base, rows)] = g[slot, :, at].T
            return carry

        lax.fori_loop(0, depth // 256, piece_of, 0)

    local_tok.wait()
    project(x)
    turn(x)
    step1()
    own(0, 1, True).start()
    own(1, 3, True).start()
    own(0, 2, False).start()
    own(1, 0, False).start()
    step2()
    sent(tok, s_own.at[0])
    own(0, 3, False).start()
    own(1, 1, False).start()
    for c in range(2):
        arrived(g.at[left, chunk(c)], r_own.at[0, c])
        forward(0, c).start()
        arrived(g.at[right, chunk(c + 2)], r_own.at[1, c])
        forward(1, c + 2).start()
    step3()
    arrived(hal, r_hal)
    head_rows = dot(hal[...], w[...], NT)
    p[0:16, :] = jnp.where(s == 0, 0.0, head_rows)

    def turn_halo(i, carry):
        at = pl.ds(pl.multiple_of(i * 256, 256), 256)
        tail_rows = jnp.concatenate([hal[:, at], jnp.zeros((E - 16, 256), bf16)], 0)
        gt[at, nb * BLK :] = tail_rows.T
        return carry

    lax.fori_loop(0, depth // 256, turn_halo, 0)
    arrived(g.at[left, pl.ds(0, 2 * ch)], r_rest.at[0])
    project(left)
    arrived(g.at[right, pl.ds(0, 2 * ch)], r_rest.at[1])
    project(right)
    step4()
    for b in (x, right):
        convolve(b)
        featurize(b, 0)
        featurize(b, 1)
    turn(left)
    turn(right)
    arrived(g.at[opp], r_fwd)
    project(opp)
    for b in (opp, left):
        convolve(b)
        featurize(b, 0)
    pack_group(0)
    exchange_first(0)
    for b in (opp, left):
        featurize(b, 1)
    pack_group(1)
    exchange_first(1)

    def inside(i):
        score = jnp.where(sub >= lane, dot(fq[i], fkt[i]), 0.0).astype(bf16)
        scot[i] = jnp.where(lane >= sub, dot(fk[i], fqt[i]), 0.0).astype(bf16)
        nin[i] = dot(score, vaug[i])

    fold = g.shape[2] // BLK

    def raw_at(i):
        return (i // fold, slice(None), slice(i % fold * BLK, (i % fold + 1) * BLK))

    def inside_raw(i):
        h, b = i // nb, i % nb
        cot = go_v[b * BLK : (b + 1) * BLK, h * E : (h + 1) * E]
        g[raw_at(i)] = dot(cot, vaug[i, :, :E], NT).astype(bf16)

    def quarter(n, body):
        for i in range(n * per // 2, (n + 1) * per // 2):
            body(i)

    turn(opp)
    local_go.wait()
    quarter(0, inside)
    exchange_second(0)
    quarter(1, inside)
    exchange_second(1)
    quarter(2, inside)
    exchange_third(0)
    exchange_third(1)
    quarter(3, inside)
    sent(g.at[opp], s_fwd)
    for n in range(4):
        quarter(n, inside_raw)

    ones = jnp.ones((2 * E, E), bf16)

    def attend(group):
        for b in range(nb):
            for j in range(gh):
                h = group * gh + j
                i = h * nb + b
                state = run[h]
                state_b = state.astype(bf16)
                run[h] = state + ub[i]
                both = dot(fq[i], state_b) + nin[i]
                num = both[:, :E]
                inv = 1.0 / both[:, E:]
                mean = num * inv
                at = (slice(b * BLK, (b + 1) * BLK), slice(h * E, (h + 1) * E))
                att_v[at] = mean.astype(bf16)
                scaled = go_v[at].astype(f32) * inv
                product = scaled * mean
                high = product.astype(bf16)
                low = (product - high.astype(f32)).astype(bf16)
                slope = dot(jnp.concatenate([high, low], 1), ones) * (-1.0 / E)
                ga_b = jnp.concatenate([scaled.astype(bf16), slope.astype(bf16)], 1)
                gna[i] = ga_b
                nin[i, :, E:] = inv
                st[i] = state_b
                ub[i] = dot(fqt[i], ga_b)
        pack_group(2 + group)

    def att_out(group):
        at = pl.ds(group * gh * E, gh * E)
        return pltpu.make_async_copy(att_v.at[:, at], att.at[:, at], s_att)

    for group in range(2):
        exchange_done(group)
        unpack_group(group)
        attend(group)
        exchange_first(2 + group)
        att_out(group).start()

    def feature_gradient(u, sel, gm, grad):
        one, two = factors(u, sel)
        stack = jnp.concatenate([(grad * two).astype(bf16), (grad * one).astype(bf16)], 0)
        return dot(gm[...], stack)

    def inside_back(i):
        h, b = i // nb, i % nb
        ga_b = gna[i]
        inv = nin[i, :, E:]
        slope = ga_b[:, E:].astype(f32) * float(E)
        scaled = g[raw_at(i)].astype(f32) * jnp.concatenate([inv, inv], 1)
        mix = scaled + jnp.concatenate([slope, slope], 1)
        mix = jnp.where(sub >= lane, mix, 0.0).astype(bf16)
        mixt = mix.T
        gfq = dot(st[i], ga_b, NT) + dot(fkt[i], mixt)
        at = (slice(h * 2 * F, h * 2 * F + F), slice(b * BLK, (b + 1) * BLK))
        gq = feature_gradient(qkt[at], selq, gmq, gfq)
        pfk[i] = dot(fqt[i], mix)
        qkt[at] = gq
        nin[i, :, :E] = dot(scot[i], ga_b[:, :E])

    step5()
    exchange_second(2)
    quarter(0, inside_back)
    quarter(1, inside_back)
    exchange_second(3)
    exchange_third(2)
    quarter(2, inside_back)
    quarter(3, inside_back)
    exchange_third(3)

    def value_gradient(group):
        for b in reversed(range(nb)):
            for j in range(gh):
                h = group * gh + j
                i = h * nb + b
                state = run[h]
                state_b = state.astype(bf16)
                st[i] = state_b
                run[h] = state + ub[i]
                rows_b = slice(b * BLK, (b + 1) * BLK)
                p[rows_b, h * E : (h + 1) * E] = dot(fk[i], state_b[:, :E]) + nin[i, :, :E]

    def key_gradient(b):
        rows_b = slice(b * BLK, (b + 1) * BLK)
        for h in range(nh):
            i = h * nb + b
            gfk = dot(st[i], vaug[i], NT) + pfk[i]
            at = (slice(2 * F * h + F, 2 * F * (h + 1)), rows_b)
            qkt[at] = feature_gradient(qkt[at], selk, gmk, gfk)
        p[rows_b, nh * E :] = qkt[:, rows_b].T

    total_rows = nb * BLK
    width = gp.shape[1]
    lanes = ((0, gh * E), (gh * E, nh * E), (nh * E, width))

    def spread(part):
        lo, up = lanes[part]
        one, two, three = taps[0:1, lo:up], taps[1:2, lo:up], taps[2:3, lo:up]
        p[total_rows:, lo:up] = jnp.zeros((16, up - lo), f32)
        for b in range(nb):
            ext = p[b * BLK : (b + 1) * BLK + 16, lo:up]
            grad = one * ext[:BLK] + two * ext[1 : BLK + 1] + three * ext[2 : BLK + 2]
            gp[b * BLK : (b + 1) * BLK, lo:up] = grad.astype(bf16)
        edge = jnp.concatenate([jnp.zeros((16, up - lo), f32), p[0:16, lo:up]], 0)
        edge = jnp.where(s == 0, 0.0, two * edge[1:17] + three * edge[2:18])
        gp[total_rows : total_rows + 16, lo:up] = edge.astype(bf16)
        gp[total_rows + 16 :, lo:up] = jnp.zeros((E - 16, up - lo), bf16)

    def rows_at(j):
        return pl.ds(pl.multiple_of(j * rows, rows), rows)

    def part_of(part):
        return pl.ds(lanes[part][0], lanes[part][1] - lanes[part][0])

    def back(part):
        return remote(
            gp.at[pl.ds(total_rows, 16), part_of(part)],
            hi.at[(x + 1) % nx, :, part_of(part)],
            sh.at[part],
            qh.at[part],
            seq=prev,
            head=nx - 1,
        )

    near = rows // 2

    def out_far(part, way):
        j = (x + 2) % nx
        src = pl.ds(pl.multiple_of(j * rows + way * near, near), near)
        return remote(
            gp.at[src, part_of(part)],
            relay.at[way, :, part_of(part)],
            sr1.at[part],
            qr1.at[part, way],
            head=right if way == 0 else left,
        )

    def on_far(part, way):
        lo, up = lanes[part]
        return remote(
            relay.at[way, :, part_of(part)],
            gin.at[pl.ds(way * near, near), pl.ds(2 * width + lo, up - lo)],
            sr2.at[part],
            qr2.at[part],
            head=right if way == 0 else left,
        )

    def pass_on(part):
        for way in range(2):
            arrived(relay.at[way, :, part_of(part)], qr1.at[part, way])
            on_far(part, way).start()

    def over(part, k):
        j = (x + k) % nx
        return remote(
            gp.at[rows_at(j), part_of(part)],
            gin.at[:, pl.ds((nx - k) * width + lanes[part][0], lanes[part][1] - lanes[part][0])],
            sx.at[part],
            qx.at[part],
            head=j,
        )

    def send_rows(part):
        if part < 2:
            out_far(part, 0).start()
            out_far(part, 1).start()
        else:
            over(part, 2).start()
        over(part, 1).start()
        over(part, 3).start()
        back(part).start()

    pieces = ny * nz
    height = gwb.shape[2]
    half = height // 2
    per_step = 512 // (2 * height)
    low_half, high_half = pl.ds(0, half), pl.ds(half, half)

    def pair(part, j):
        at = part_of(part)
        return remote(
            gwb.at[j, 1 - core, :, at], rp.at[j, :, at], sp.at[part], qp.at[part], seq=sibling
        )

    def weight_part(part):
        lo, up = lanes[part]

        def weight_step(i, carry):
            at = pl.ds(pl.multiple_of(i * 512, 512), 512)
            whole = dot(gt[at, :], gp[:, lo:up]).astype(bf16)
            whole = whole.reshape(per_step, 2, height, up - lo)
            for q in range(per_step):
                gwb[i * per_step + q, :, :, lo:up] = whole[q]
                pair(part, i * per_step + q).start()
            return carry

        lax.fori_loop(0, pieces // per_step, weight_step, 0)

    def go_2a(part, k):
        to, at = (z + k) % nz, part_of(part)
        return remote(
            t.at[:, to, low_half, at],
            r2a.at[k, :, :, at],
            s2a.at[part],
            q2a.at[part],
            seq=at_seq(y, to, core),
        )

    def go_2b(part, k):
        to, at = (y + k) % ny, part_of(part)
        return remote(
            t.at[to, :, high_half, at],
            r2b.at[k, :, :, at],
            s2b.at[part],
            q2b.at[part],
            seq=at_seq(to, z, core),
        )

    def go_3a(part, k):
        to, at = (y + k) % ny, part_of(part)
        return remote(
            va.at[to, :, at],
            r3a.at[k, :, at],
            s3a.at[part],
            q3a.at[part],
            seq=at_seq(to, z, core),
        )

    def go_3b(part, k):
        to, at = (z + k) % nz, part_of(part)
        return remote(
            vb.at[to, :, at],
            r3b.at[k, :, at],
            s3b.at[part],
            q3b.at[part],
            seq=at_seq(y, to, core),
        )

    def weight_second(part):
        lo, up = lanes[part]

        def pair_sum(j, carry):
            both = gwb[j, core, :, lo:up].astype(f32) + rp[j, :, lo:up].astype(f32)
            t[j // nz, j % nz, :, lo:up] = both.astype(bf16)
            return carry

        arrived(rp.at[:, :, part_of(part)], qp.at[part])
        lax.fori_loop(0, pieces, pair_sum, 0)
        for k in range(1, max(ny, nz)):
            if k < nz:
                go_2a(part, k).start()
            if k < ny:
                go_2b(part, k).start()

    def weight_third(part):
        lo, up = lanes[part]
        at = part_of(part)
        arrived(r2a.at[pl.ds(1, nz - 1), :, :, at], q2a.at[part])
        arrived(r2b.at[pl.ds(1, ny - 1), :, :, at], q2b.at[part])
        for i in range(ny):
            total = t[i, z, 0:half, lo:up].astype(f32)
            for k in range(1, nz):
                total = total + r2a[k, i, :, lo:up].astype(f32)
            va[i, :, lo:up] = total.astype(bf16)
        for i in range(nz):
            total = t[y, i, half:, lo:up].astype(f32)
            for k in range(1, ny):
                total = total + r2b[k, i, :, lo:up].astype(f32)
            vb[i, :, lo:up] = total.astype(bf16)
        for k in range(1, max(ny, nz)):
            if k < ny:
                go_3a(part, k).start()
            if k < nz:
                go_3b(part, k).start()

    exchange_done(2)
    unpack_group(2)
    value_gradient(0)
    spread(0)
    send_rows(0)
    weight_part(0)
    exchange_done(3)
    unpack_group(3)
    value_gradient(1)
    spread(1)
    send_rows(1)
    weight_second(0)
    for b in range(nb):
        key_gradient(b)
        if b == nb // 2:
            pass_on(0)
    spread(2)
    send_rows(2)
    weight_part(1)
    pass_on(1)
    weight_second(1)
    weight_part(2)
    weight_third(0)

    steps = depth // 256

    def load(i, slot):
        at = pl.ds(pl.multiple_of(i * 256, 256), 256)
        for j in range(nx):
            src = w.at[:, at] if j == 0 else wf.at[j - 1, :, at]
            dst = wbuf.at[slot, pl.ds(j * width, width)]
            pltpu.make_async_copy(src, dst, sw.at[slot]).start()

    def as_many(part, count):
        return gin.at[:, pl.ds(0, count * (lanes[part][1] - lanes[part][0]))]

    def gi_out(i):
        at = pl.ds(pl.multiple_of(i * 256, 256), 256)
        return pltpu.make_async_copy(gi_v.at[:, at], gi.at[:, at], s_gi)

    step6()
    load(0, 0)
    load(1, 1)
    weight_second(2)
    gin[:, :width] = gp[rows_at(x), :]
    for part in range(3):
        if part < 2:
            arrived(as_many(part, 1), qr2.at[part])
        arrived(as_many(part, 2 if part < 2 else 3), qx.at[part])

    @pl.when(x == nx - 1)
    def _():
        for part in range(3):
            arrived(hi.at[:, :, part_of(part)], qh.at[part])
        for k in range(nx):
            at = slice(k * width, (k + 1) * width)
            last = gin[rows - 16 :, at].astype(f32) + hi[k].astype(f32)
            gin[rows - 16 :, at] = last.astype(bf16)

    def input_step(i, carry):
        at = pl.ds(pl.multiple_of(i * 256, 256), 256)
        slot = i % 2
        pltpu.make_async_copy(wbuf.at[slot], wbuf.at[slot], sw.at[slot]).wait()
        gi_v[:, at] = dot(gin[...], wbuf[slot]).astype(bf16)
        gi_out(i).start()

        @pl.when(i + 2 < steps)
        def _():
            load(i + 2, slot)

        return carry

    lax.fori_loop(0, steps // 4, input_step, 0)
    weight_third(1)
    lax.fori_loop(steps // 4, 5 * steps // 8, input_step, 0)
    weight_third(2)
    lax.fori_loop(5 * steps // 8, steps, input_step, 0)

    for part in range(3):
        at = part_of(part)
        arrived(r3a.at[pl.ds(1, ny - 1), :, at], q3a.at[part])
        arrived(r3b.at[pl.ds(1, nz - 1), :, at], q3b.at[part])

    def put(at, total):
        for h in range(nh):
            narrow = total[:, nh * E + 2 * F * h : nh * E + 2 * F * (h + 1)]
            gw_v[at, h, :] = jnp.concatenate([narrow, total[:, h * E : (h + 1) * E]], 1)

    total = va[y].astype(f32)
    for k in range(1, ny):
        total = total + r3a[k].astype(f32)
    put(slice(0, half), total)
    total = vb[z].astype(f32)
    for k in range(1, nz):
        total = total + r3b[k].astype(f32)
    put(slice(half, height), total)
    gw_out = pltpu.make_async_copy(gw_v, gw, s_gw)
    gw_out.start()

    for part in range(3):
        at = part_of(part)
        back(part).wait_send()
        if part < 2:
            sent(as_many(part, 1), sr1.at[part])
            sent(as_many(part, 1), sr2.at[part])
        sent(as_many(part, 2 if part < 2 else 3), sx.at[part])
        sent(rp.at[:, :, at], sp.at[part])
        sent(r2a.at[pl.ds(1, nz - 1), :, :, at], s2a.at[part])
        sent(r2b.at[pl.ds(1, ny - 1), :, :, at], s2b.at[part])
        sent(r3a.at[pl.ds(1, ny - 1), :, at], s3a.at[part])
        sent(r3b.at[pl.ds(1, nz - 1), :, at], s3b.at[part])
    for e in range(4):
        sent(r1.at[e, pl.ds(0, ga - 1)], s1.at[e])
        sent(r2.at[e, pl.ds(0, gb - 1)], s2.at[e])
        sent(res.at[e, pl.ds(0, (ga - 1) * piece)], s3.at[e])
    sent(tok, s_own.at[1])

    @pl.when(x == nx - 1)
    def _():
        sent(tok.at[pl.ds(0, 16 * nx)], s_hal)

    step7()
    pltpu.make_async_copy(att_v, att, s_att).wait()
    pltpu.make_async_copy(gi_v, gi, s_gi).wait()
    gw_out.wait()


def hand_on_kernel(count, *refs):
    srcs, dsts, held = refs[:count], refs[count : 2 * count], refs[2 * count : 3 * count]
    come, leave = refs[3 * count :]
    cuts = come.shape[1]

    def slices(i, c):
        size = srcs[i].shape[0] // cuts
        at = pl.ds(c * size, size)
        return (
            pltpu.make_async_copy(srcs[i].at[at], held[i].at[at], come.at[i, c]),
            pltpu.make_async_copy(held[i].at[at], dsts[i].at[at], leave.at[i, c]),
        )

    every = [slices(i, c) for c in range(cuts) for i in range(count)]
    for first, _ in every:
        first.start()
    for first, second in every:
        first.wait()
        second.start()
    for _, second in every:
        second.wait()


def hand_on(*arrays):
    hbm = pl.BlockSpec(memory_space=pl.ANY)
    count = len(arrays)
    return pl.pallas_call(
        functools.partial(hand_on_kernel, count),
        out_shape=tuple(jax.ShapeDtypeStruct(a.shape, a.dtype) for a in arrays),
        in_specs=[hbm] * count,
        out_specs=(hbm,) * count,
        scratch_shapes=[pltpu.VMEM(a.shape, a.dtype) for a in arrays]
        + [pltpu.SemaphoreType.DMA((count, 4))] * 2,
        compiler_params=pltpu.CompilerParams(vmem_limit_bytes=60 * 2**20),
    )(*arrays)


def local(nx, ny, nz, tokens, in_weight, conv_kernel, grad_out):
    depth, nh, _ = in_weight.shape
    wt = jnp.transpose(in_weight, (1, 2, 0)).reshape(nh * CHAN, depth)
    rows = tokens.shape[0]
    every = grad_out.shape[0]
    width = nh * CHAN
    nb = every // BLK
    n = nh * nb
    ga, gb, ns = 2 * nz, ny, 2 * ny * nz
    piece = -(-(nh // 2) * FS // (16 * ga)) * 16
    height = depth // ns
    half = height // 2
    hbm = pl.BlockSpec(memory_space=pl.ANY)
    dma = pltpu.SemaphoreType.DMA
    consts = [
        jnp.asarray(selection(True), bf16),
        jnp.asarray(selection(False), bf16),
        jnp.asarray(gradient_map(True), bf16),
        jnp.asarray(gradient_map(False), bf16),
    ]
    att, gi, gw, _ = pl.pallas_call(
        functools.partial(kernel, nx, ny, nz, nh),
        out_shape=(
            jax.ShapeDtypeStruct((every, nh * E), bf16),
            jax.ShapeDtypeStruct((rows, depth), bf16),
            jax.ShapeDtypeStruct((height, nh, CHAN), f32),
            jax.ShapeDtypeStruct((nx - 1, width, depth), bf16),
        ),
        in_specs=[hbm] * 8,
        out_specs=(hbm, hbm, hbm, hbm),
        scratch_shapes=[
            pltpu.VMEM(conv_kernel.shape, f32),
            pltpu.VMEM((2 * FS, 3 * F), bf16),
            pltpu.VMEM((2 * FS, 3 * F), bf16),
            pltpu.VMEM((F, 2 * FS), bf16),
            pltpu.VMEM((F, 2 * FS), bf16),
            pltpu.VMEM((every, nh * E), bf16),
            pltpu.VMEM((every, nh * E), bf16),
            pltpu.VMEM((rows, depth), bf16),
            pltpu.VMEM((height, nh, CHAN), f32),
            pltpu.VMEM((width, depth), bf16),
            pltpu.VMEM((nx, rows, depth), bf16),
            pltpu.VMEM((depth, every + E), bf16),
            pltpu.VMEM((16 + every, width), f32),
            pltpu.VMEM((16, depth), bf16),
            pltpu.VMEM((8, width), f32),
            pltpu.VMEM((nh * 2 * F, every), f32),
            pltpu.VMEM((n, BLK, 2 * E), bf16),
            pltpu.VMEM((n, FS, BLK), bf16),
            pltpu.VMEM((n, FS, BLK), bf16),
            pltpu.VMEM((n, BLK, FS), bf16),
            pltpu.VMEM((n, BLK, FS), bf16),
            pltpu.VMEM((n, FS, 2 * E), f32),
            pltpu.VMEM((n, BLK, 2 * E), f32),
            pltpu.VMEM((n, BLK, BLK), bf16),
            pltpu.VMEM((n, BLK, 2 * E), bf16),
            pltpu.VMEM((nh, FS, 2 * E), f32),
            pltpu.VMEM((n, FS, 2 * E), bf16),
            pltpu.VMEM((n, FS, BLK), f32),
            pltpu.VMEM((every + E, width), bf16),
            pltpu.VMEM((4, ga * piece, E), bf16),
            pltpu.VMEM((4, ga, piece, E), bf16),
            pltpu.VMEM((4, piece, E), bf16),
            pltpu.VMEM((4, gb, piece, E), bf16),
            pltpu.VMEM((4, ga, piece, E), bf16),
            pltpu.VMEM((4, ga * piece, E), bf16),
            pltpu.VMEM((2, nx * width, 256), bf16),
            pltpu.VMEM((rows, nx * width), bf16),
            pltpu.VMEM((2, rows // 2, nh * E), bf16),
            pltpu.VMEM((nx, 16, width), bf16),
            pltpu.VMEM((ny * nz, 2, height, width), bf16),
            pltpu.VMEM((ny * nz, height, width), bf16),
            pltpu.VMEM((ny, nz, height, width), bf16),
            pltpu.VMEM((nz, ny, half, width), bf16),
            pltpu.VMEM((ny, nz, half, width), bf16),
            pltpu.VMEM((ny, half, width), bf16),
            pltpu.VMEM((nz, half, width), bf16),
            pltpu.VMEM((ny, half, width), bf16),
            pltpu.VMEM((nz, half, width), bf16),
            dma((2,)),
            dma((2, 2)),
            dma((2,)),
            dma(()),
            dma(()),
            dma(()),
            dma(()),
            dma(()),
            dma(()),
            dma((4,)),
            dma((4,)),
            dma((4,)),
            dma((4,)),
            dma((4,)),
            dma((4,)),
            dma((2,)),
            dma((2,)),
            dma((2, 2)),
            dma((2,)),
            dma((2,)),
            dma((3,)),
            dma((3,)),
            dma((3,)),
            dma((3,)),
            dma((3,)),
            dma((3,)),
            dma((3,)),
            dma((3,)),
            dma((3,)),
            dma((3,)),
            dma((3,)),
            dma((3,)),
            dma((3,)),
            dma((3,)),
            dma(()),
            dma(()),
            dma(()),
            dma(()),
            dma((5,)),
            dma(()),
            dma(()),
            dma(()),
            dma(()),
            dma(()),
            dma(()),
            dma(()),
            dma(()),
            dma((ny,)),
            dma((ny,)),
            dma((nz,)),
            dma((nz,)),
            dma(()),
            dma(()),
            dma(()),
            dma(()),
            dma((2,)),
            dma((2,)),
        ],
        compiler_params=pltpu.CompilerParams(
            collective_id=0, has_side_effects=True, vmem_limit_bytes=62 * 2**20
        ),
    )(tokens, wt, conv_kernel, grad_out, *consts)
    return hand_on(att, gi, gw)


def solution(mesh):
    nx, ns = mesh.shape["head"], mesh.shape["seq"]
    ny = math.isqrt(ns // 2)
    nz = ns // 2 // ny
    placed = (
        P(("seq", "head"), None),
        P(None, "head", None),
        P(None, "head", None),
        P("seq", "head"),
    )
    return jax.shard_map(
        functools.partial(local, nx, ny, nz),
        mesh=mesh,
        in_specs=placed,
        out_specs=(P("seq", "head"), P(("seq", "head"), None), P("seq", "head", None)),
        check_vma=False,
    )
```

```python
import functools
import math

import jax
import jax.numpy as jnp
import numpy as np
from jax import lax
from jax.experimental import pallas as pl
from jax.experimental.pallas import tpu as pltpu
from jax.sharding import PartitionSpec as P

F = 16
E = 128
BLK = 256
CHAN = 160
FS = 160
NF = 1 + F + F * (F + 1) // 2
KAPPA = 32.0 ** -0.25
f32 = jnp.float32
bf16 = jnp.bfloat16
NN = (((1,), (0,)), ((), ()))
NT = (((1,), (1,)), ((), ()))


def dot(a, b, dims=NN):
    return lax.dot_general(a, b, dims, preferred_element_type=f32)


def bf_parts(value, count):
    parts = []
    rest = np.float64(value)
    for _ in range(count):
        part = np.float64(np.asarray(rest, dtype=jnp.bfloat16))
        parts.append(part)
        rest = rest - part
    return parts


def selection(weighted):
    sel = np.zeros((2 * FS, 3 * F), np.float64)
    sel[0, 32] = 1.0
    sel[FS, 32] = 1.0
    for i in range(F):
        row = 1 + i
        sel[row, i] = sel[row, F + i] = 1.0
        for c, part in enumerate(bf_parts(0.5 / KAPPA, 3)):
            sel[FS + row, 32 + c] = part
    row = 1 + F
    for i in range(F):
        for j in range(i, F):
            first = 2.0 if (weighted and j > i) else 1.0
            sel[row, i] = sel[row, F + i] = first
            sel[FS + row, j] = sel[FS + row, F + j] = 1.0
            row += 1
    return sel


def gradient_map(weighted):
    sel = selection(weighted)
    return np.concatenate([sel[:FS, :F].T, sel[FS:, :F].T], 1)


def remote(src, dst, send, recv, **where):
    return pltpu.make_async_remote_copy(
        src_ref=src,
        dst_ref=dst,
        send_sem=send,
        recv_sem=recv,
        device_id=where,
        device_id_type=pl.DeviceIdType.MESH,
    )


def arrived(ref, sem):
    remote(ref, ref, sem, sem, seq=lax.axis_index("seq")).wait_recv()


def sent(ref, sem):
    remote(ref, ref, sem, sem, seq=lax.axis_index("seq")).wait_send()


def greet(sem, **where):
    pl.semaphore_signal(sem, inc=1, device_id=where, device_id_type=pl.DeviceIdType.MESH)


def weight_gather(nx, ny, nz, x, y, z, core, w, wf, sems):
    s1, q1, sr, qr, sa, qa, sb, qb, sc, qc, sd, qd, sf, qf, sg, qg, se, qe = sems
    chan, depth = w.shape
    half = chan // 2
    quarter = half // 2
    eighth = quarter // 2
    col = depth // (ny * nz)
    base = core * half
    rows_c = pl.ds(pl.multiple_of(base, 16), half)
    rows_a = pl.ds(pl.multiple_of(base, 16), quarter)
    rows_b = pl.ds(pl.multiple_of(base + quarter, 16), quarter)
    far = pl.ds(0, nx - 1)

    def piece_a(n):
        return pl.ds(pl.multiple_of(base + n * eighth, 16), eighth)

    def piece_b(n):
        return pl.ds(pl.multiple_of(base + quarter + n * eighth, 16), eighth)

    def cols(yy, zz):
        return pl.ds(pl.multiple_of((yy * nz + zz) * col, 128), col)

    def row_of(yy):
        return pl.ds(pl.multiple_of(yy * nz * col, 128), nz * col)

    def at_seq(yy, zz, cc):
        return (yy * nz + zz) * 2 + cc

    mine = cols(y, z)
    ring_y = (1, ny - 1) if ny > 2 else (1,)
    ring_z = (1, nz - 1) if nz > 2 else (1,)

    def spread_x(k):
        return remote(w.at[rows_c, mine], wf.at[nx - k - 1, rows_c, mine], s1, q1, head=(x + k) % nx)

    def spread_on(k):
        here = wf.at[nx - k - 1, rows_a if k == 1 else rows_b, mine]
        there = wf.at[nx // 2 - 1, rows_a if k == 1 else rows_b, mine]
        return remote(here, there, sr, qr, head=(x + k) % nx)

    def a_z(k):
        here = wf.at[far, rows_a, mine]
        return remote(here, here, sa, qa, seq=at_seq(y, (z + k) % nz, core))

    def b_y(k):
        here = wf.at[far, rows_b, mine]
        return remote(here, here, sb, qb, seq=at_seq((y + k) % ny, z, core))

    def a_y(k):
        here = wf.at[far, rows_a, row_of(y)]
        return remote(here, here, sc.at[k], qc.at[k], seq=at_seq((y + k) % ny, z, core))

    def b_z(k, yy):
        here = wf.at[far, rows_b, cols(yy, z)]
        return remote(here, here, sd.at[k], qd.at[k], seq=at_seq(y, (z + k) % nz, core))

    def a_y_on(k):
        here = wf.at[far, piece_a(0 if k == 1 else 1), row_of((y - k) % ny)]
        return remote(here, here, sf, qf, seq=at_seq((y + k) % ny, z, core))

    def b_z_on(k, yy):
        here = wf.at[far, piece_b(0 if k == 1 else 1), cols(yy, (z - k) % nz)]
        return remote(here, here, sg, qg, seq=at_seq(y, (z + k) % nz, core))

    def across(part):
        here = wf.at[far, rows_a if part == 0 else rows_b]
        return remote(here, here, se.at[part], qe.at[part], seq=at_seq(y, z, 1 - core))

    def lanes(rows, count):
        return wf.at[far, rows, pl.ds(0, count * col)]

    def step0():
        for k in (1, nx - 1):
            spread_x(k).start()

    def step1():
        arrived(wf.at[pl.ds(0, 2), rows_c, mine], q1)
        for k in (1, nx - 1):
            spread_on(k).start()

    def step2():
        arrived(wf.at[0, rows_c, mine], qr)
        for k in range(1, max(ny, nz)):
            if k < nz:
                a_z(k).start()
            if k < ny:
                b_y(k).start()

    def step3():
        arrived(lanes(rows_a, nz - 1), qa)
        for k in ring_y:
            a_y(k).start()
        arrived(lanes(rows_b, ny - 1), qb)
        for k in ring_z:
            for yy in range(ny):
                b_z(k, yy).start()

    def step4():
        for k in ring_y:
            arrived(lanes(rows_a, nz), qc.at[ny - k])
            if ny > 2:
                a_y_on(ny - k).start()
        for k in ring_z:
            arrived(lanes(rows_b, ny), qd.at[nz - k])
            if nz > 2:
                for yy in range(ny):
                    b_z_on(nz - k, yy).start()

    def step5():
        if ny > 2:
            arrived(lanes(rows_a, nz), qf)
        across(0).start()
        if nz > 2:
            arrived(lanes(rows_b, ny), qg)
        across(1).start()

    def step6():
        across(0).wait_recv()
        across(1).wait_recv()

    def step7():
        sent(wf.at[pl.ds(0, 2), rows_c, mine], s1)
        sent(wf.at[0, rows_c, mine], sr)
        sent(lanes(rows_a, nz - 1), sa)
        sent(lanes(rows_b, ny - 1), sb)
        for k in ring_y:
            sent(lanes(rows_a, nz), sc.at[k])
        for k in ring_z:
            sent(lanes(rows_b, ny), sd.at[k])
        if ny > 2:
            sent(lanes(rows_a, nz), sf)
        if nz > 2:
            sent(lanes(rows_b, ny), sg)
        across(0).wait_send()
        across(1).wait_send()

    return step0, step1, step2, step3, step4, step5, step6, step7


def kernel(
    nx, ny, nz, nh,
    tok, wt, cv_hbm, go, selq_hbm, selk_hbm, gmq_hbm, gmk_hbm,
    att, gi, gw, wf,
    cv, selq, selk, gmq, gmk, go_v, att_v, gi_v, gw_v, w, g, gt, p, hal, taps, qkt, vaug, fqt, fkt, fq, fk, ub, nin, scot, gna, run, st, pfk, gp,
    loc, r1, tot, r2, out, res,
    wbuf, gin, relay, hi, gwb, rp, t, r2a, r2b, va, vb, r3a, r3b,
    s_own, r_own, r_rest, s_fwd, r_fwd, s_hal, r_hal, s_w, s_tok,
    s1, q1, s2, q2, s3, q3,
    sw, sr1, qr1, sr2, qr2, sx, qx, sh, qh, sp, qp, s2a, q2a, s2b, q2b, s3a, q3a, s3b, q3b, s_att, s_gi, s_gw, s_go, s_const,
    *sems,
):
    x = lax.axis_index("head")
    s = lax.axis_index("seq")
    ns = 2 * ny * nz
    core, z, y = s % 2, (s // 2) % nz, s // (2 * nz)
    left, right, opp = (x + nx - 1) % nx, (x + 1) % nx, (x + 2) % nx
    prev, after = (s + ns - 1) % ns, (s + 1) % ns
    ga, gb = 2 * nz, ny
    me_a, me_b = s % ga, s // ga
    rows, depth = tok.shape
    nb = go.shape[0] // BLK
    ch = rows // 4
    piece = loc.shape[1] // ga
    gh = nh // 2
    per = gh * nb

    def at_seq(yy, zz, cc):
        return (yy * nz + zz) * 2 + cc

    sibling = at_seq(y, z, 1 - core)
    bar = pltpu.get_barrier_semaphore()
    for k in range(1, nx):
        greet(bar, head=(x + k) % nx)
    for k in range(1, ga):
        greet(bar, seq=me_b * ga + (me_a + k) % ga)
    for k in range(1, gb):
        greet(bar, seq=((me_b + k) % gb) * ga + me_a)
    greet(bar, seq=prev)
    greet(bar, seq=after)
    greet(bar, seq=prev, head=nx - 1)

    @pl.when(x == nx - 1)
    def _():
        for j in range(nx):
            greet(bar, seq=after, head=j)

    local_tok = pltpu.make_async_copy(tok, g.at[x], s_tok)
    local_tok.start()
    local_go = pltpu.make_async_copy(go, go_v, s_go)
    local_go.start()
    small = [
        pltpu.make_async_copy(src, dst, s_const.at[i])
        for i, (src, dst) in enumerate(
            ((cv_hbm, cv), (selq_hbm, selq), (selk_hbm, selk), (gmq_hbm, gmq), (gmk_hbm, gmk))
        )
    ]
    for copy in small:
        copy.start()
    loads = []
    for h in range(nh):
        base = h * CHAN
        loads.append(
            pltpu.make_async_copy(
                wt.at[base + 2 * F : base + CHAN], w.at[h * E : (h + 1) * E], s_w
            )
        )
        loads.append(
            pltpu.make_async_copy(
                wt.at[base : base + 2 * F],
                w.at[nh * E + 2 * F * h : nh * E + 2 * F * (h + 1)],
                s_w,
            )
        )
    for copy in loads:
        copy.start()
    greeted = nx - 1 + ga - 1 + gb - 1 + 3
    pl.semaphore_wait(bar, jnp.where(x == nx - 1, greeted + nx, greeted))

    def chunk(c):
        return pl.ds(c * ch, ch)

    def own(way, c, first):
        return remote(
            tok.at[chunk(c)],
            g.at[x, chunk(c)],
            s_own.at[0 if first else 1],
            r_own.at[way, c % 2] if first else r_rest.at[way],
            head=right if way == 0 else left,
        )

    def forward(way, c):
        slot = left if way == 0 else right
        return remote(
            g.at[slot, chunk(c)],
            g.at[slot, chunk(c)],
            s_fwd,
            r_fwd,
            head=right if way == 0 else left,
        )

    def halo(j):
        return remote(tok.at[pl.ds(rows - 16, 16)], hal, s_hal, r_hal, seq=after, head=j)

    step0, step1, step2, step3, step4, step5, step6, step7 = weight_gather(
        nx, ny, nz, x, y, z, core, w, wf, sems
    )
    pltpu.make_async_copy(w, w, s_w).wait()
    step0()
    own(0, 0, True).start()
    own(1, 2, True).start()
    @pl.when(x == nx - 1)
    def _():
        for j in range(nx):
            halo(j).start()

    lane = lax.broadcasted_iota(jnp.int32, (BLK, BLK), 1)
    sub = lax.broadcasted_iota(jnp.int32, (BLK, BLK), 0)
    frow = lax.broadcasted_iota(jnp.int32, (FS, E), 0)

    for copy in small:
        copy.wait()

    for j in range(3):
        lines = [cv[j, h : h + 1, :] for h in range(nh)]
        for h in range(nh):
            taps[j : j + 1, h * E : (h + 1) * E] = lines[h][:, 2 * F :]
        taps[j : j + 1, nh * E :] = jnp.concatenate([v[:, : 2 * F] for v in lines], 1) * KAPPA

    def rows_of(a):
        return pl.ds(pl.multiple_of(a * piece, 16), piece)

    def first(e, k):
        a = (me_a + k) % ga
        return remote(
            loc.at[e, rows_of(a)], r1.at[e, me_a], s1.at[e], q1.at[e], seq=me_b * ga + a
        )

    def second(e, k):
        b = (me_b + k) % gb
        return remote(tot.at[e], r2.at[e, me_b], s2.at[e], q2.at[e], seq=b * ga + me_a)

    def third(e, k):
        a = (me_a + k) % ga
        return remote(
            out.at[e, a], res.at[e, rows_of(me_a)], s3.at[e], q3.at[e], seq=me_b * ga + a
        )

    def exchange_first(e):
        for k in range(1, ga):
            first(e, k).start()
        r1[e, me_a] = loc[e, rows_of(me_a), :]

    def exchange_second(e):
        arrived(r1.at[e, pl.ds(0, ga - 1)], q1.at[e])
        total = jnp.zeros((piece, E), f32)
        for a in range(ga):
            total = total + r1[e, a].astype(f32)
        tot[e] = total.astype(bf16)
        for k in range(1, gb):
            second(e, k).start()

    def exchange_third(e):
        arrived(r2.at[e, pl.ds(0, gb - 1)], q2.at[e])
        r2[e, me_b] = tot[e]
        total = jnp.zeros((piece, E), f32)
        for b in range(gb):
            ahead = b < me_b if e < 2 else b > me_b
            total = total + jnp.where(ahead, r2[e, b].astype(f32), 0.0)
        for step in range(ga):
            a = step if e < 2 else ga - 1 - step
            out[e, a] = total.astype(bf16)
            total = total + r1[e, a].astype(f32)
        for k in range(1, ga):
            third(e, k).start()
        res[e, rows_of(me_a), :] = out[e, me_a]

    def exchange_done(e):
        arrived(res.at[e, pl.ds(0, (ga - 1) * piece)], q3.at[e])

    def pack(e, h, whole):
        column = jnp.concatenate([whole[:, E:], jnp.zeros((2 * E - FS, E), f32)], 0)
        line = column.T[0:1, :]
        body = jnp.where(frow == NF, line[:, :E], jnp.where(frow == NF + 1, line[:, E:], whole[:, :E]))
        loc[e, h * FS : (h + 1) * FS, :] = body.astype(bf16)

    def pack_group(e):
        for j in range(gh):
            h = (e % 2) * gh + j
            whole = ub[h * nb]
            for b in range(1, nb):
                whole = whole + ub[h * nb + b]
            pack(e, j, whole)
        if gh * FS < loc.shape[1]:
            loc[e, gh * FS :, :] = jnp.zeros((loc.shape[1] - gh * FS, E), bf16)

    def unpack_group(e):
        for j in range(gh):
            body = res[e, j * FS : (j + 1) * FS, :].astype(f32)
            line = jnp.concatenate([body[NF : NF + 1, :], body[NF + 1 : NF + 2, :]], 1)
            column = jnp.broadcast_to(line, (E, 2 * E)).T[:FS, :]
            run[(e % 2) * gh + j] = jnp.concatenate([jnp.where(frow < NF, body, 0.0), column], 1)

    def factors(u, sel):
        high = u.astype(bf16)
        low = (u - high.astype(f32)).astype(bf16)
        stack = jnp.concatenate([high, low, jnp.ones((F, BLK), bf16)], 0)
        both = dot(sel[...], stack)
        return both[:FS], both[FS:]

    def block_at(b):
        return pl.ds(pl.multiple_of(b * BLK, BLK), BLK)

    def convolve(b):
        ext = p[pl.ds(pl.multiple_of(b * BLK, BLK), BLK + 16), :]
        conv = taps[0:1, :] * ext[16:] + taps[1:2, :] * ext[15:-1] + taps[2:3, :] * ext[14:-2]
        qkt[:, block_at(b)] = conv[:, nh * E :].T
        for h in range(nh):
            vaug[h * nb + b] = jnp.concatenate(
                [conv[:, h * E : (h + 1) * E].astype(bf16), jnp.ones((BLK, E), bf16)], 1
            )

    def featurize(b, group):
        for j in range(gh):
            h = group * gh + j
            i = h * nb + b
            at = block_at(b)
            first_q, second_q = factors(qkt[2 * F * h : 2 * F * h + F, at], selq)
            first_k, second_k = factors(qkt[2 * F * h + F : 2 * F * (h + 1), at], selk)
            q = (first_q * second_q).astype(bf16)
            k = (first_k * second_k).astype(bf16)
            fqt[i] = q
            fkt[i] = k
            fq[i] = q.T
            fk[i] = k.T
            ub[i] = dot(k, vaug[i])

    def project(slot):
        base = pl.multiple_of(slot * rows, rows)
        p[pl.ds(16 + base, rows), :] = dot(g[slot], w[...], NT)

    def turn(slot):
        base = pl.multiple_of(slot * rows, rows)

        def piece_of(i, carry):
            at = pl.ds(pl.multiple_of(i * 256, 256), 256)
            gt[at, pl.ds(base, rows)] = g[slot, :, at].T
            return carry

        lax.fori_loop(0, depth // 256, piece_of, 0)

    local_tok.wait()
    project(x)
    turn(x)
    step1()
    own(0, 1, True).start()
    own(1, 3, True).start()
    own(0, 2, False).start()
    own(1, 0, False).start()
    own(0, 3, False).start()
    own(1, 1, False).start()
    step2()
    for c in range(2):
        arrived(g.at[left, chunk(c)], r_own.at[0, c])
        forward(0, c).start()
        arrived(g.at[right, chunk(c + 2)], r_own.at[1, c])
        forward(1, c + 2).start()
    step3()
    arrived(hal, r_hal)
    head_rows = dot(hal[...], w[...], NT)
    p[0:16, :] = jnp.where(s == 0, 0.0, head_rows)

    def turn_halo(i, carry):
        at = pl.ds(pl.multiple_of(i * 256, 256), 256)
        tail_rows = jnp.concatenate([hal[:, at], jnp.zeros((E - 16, 256), bf16)], 0)
        gt[at, nb * BLK :] = tail_rows.T
        return carry

    lax.fori_loop(0, depth // 256, turn_halo, 0)
    arrived(g.at[left, pl.ds(0, 2 * ch)], r_rest.at[0])
    project(left)
    arrived(g.at[right, pl.ds(0, 2 * ch)], r_rest.at[1])
    project(right)
    step4()
    for b in (x, right):
        convolve(b)
        featurize(b, 0)
        featurize(b, 1)
    turn(left)
    turn(right)
    arrived(g.at[opp], r_fwd)
    project(opp)
    for b in (opp, left):
        convolve(b)
        featurize(b, 0)
    pack_group(0)
    exchange_first(0)
    for b in (opp, left):
        featurize(b, 1)
    pack_group(1)
    exchange_first(1)

    def inside(i):
        score = jnp.where(sub >= lane, dot(fq[i], fkt[i]), 0.0).astype(bf16)
        scot[i] = jnp.where(lane >= sub, dot(fk[i], fqt[i]), 0.0).astype(bf16)
        nin[i] = dot(score, vaug[i])

    fold = g.shape[2] // BLK

    def raw_at(i):
        return (i // fold, slice(None), slice(i % fold * BLK, (i % fold + 1) * BLK))

    def inside_raw(i):
        h, b = i // nb, i % nb
        cot = go_v[b * BLK : (b + 1) * BLK, h * E : (h + 1) * E]
        g[raw_at(i)] = dot(cot, vaug[i, :, :E], NT).astype(bf16)

    def quarter(n, body):
        for i in range(n * per // 2, (n + 1) * per // 2):
            body(i)

    turn(opp)
    local_go.wait()
    quarter(0, inside)
    exchange_second(0)
    quarter(1, inside)
    exchange_second(1)
    quarter(2, inside)
    exchange_third(0)
    exchange_third(1)
    quarter(3, inside)
    sent(g.at[opp], s_fwd)
    for n in range(4):
        quarter(n, inside_raw)

    ones = jnp.ones((2 * E, E), bf16)

    def attend(group):
        for b in range(nb):
            for j in range(gh):
                h = group * gh + j
                i = h * nb + b
                state = run[h]
                state_b = state.astype(bf16)
                run[h] = state + ub[i]
                both = dot(fq[i], state_b) + nin[i]
                num = both[:, :E]
                inv = 1.0 / both[:, E:]
                mean = num * inv
                at = (slice(b * BLK, (b + 1) * BLK), slice(h * E, (h + 1) * E))
                att_v[at] = mean.astype(bf16)
                scaled = go_v[at].astype(f32) * inv
                product = scaled * mean
                high = product.astype(bf16)
                low = (product - high.astype(f32)).astype(bf16)
                slope = dot(jnp.concatenate([high, low], 1), ones) * (-1.0 / E)
                ga_b = jnp.concatenate([scaled.astype(bf16), slope.astype(bf16)], 1)
                gna[i] = ga_b
                nin[i, :, E:] = inv
                st[i] = state_b
                ub[i] = dot(fqt[i], ga_b)
        pack_group(2 + group)

    def att_out(group):
        at = pl.ds(group * gh * E, gh * E)
        return pltpu.make_async_copy(att_v.at[:, at], att.at[:, at], s_att)

    for group in range(2):
        exchange_done(group)
        unpack_group(group)
        attend(group)
        exchange_first(2 + group)
        att_out(group).start()

    def feature_gradient(u, sel, gm, grad):
        one, two = factors(u, sel)
        stack = jnp.concatenate([(grad * two).astype(bf16), (grad * one).astype(bf16)], 0)
        return dot(gm[...], stack)

    def inside_back(i):
        h, b = i // nb, i % nb
        ga_b = gna[i]
        inv = nin[i, :, E:]
        slope = ga_b[:, E:].astype(f32) * float(E)
        scaled = g[raw_at(i)].astype(f32) * jnp.concatenate([inv, inv], 1)
        mix = scaled + jnp.concatenate([slope, slope], 1)
        mix = jnp.where(sub >= lane, mix, 0.0).astype(bf16)
        mixt = mix.T
        gfq = dot(st[i], ga_b, NT) + dot(fkt[i], mixt)
        at = (slice(h * 2 * F, h * 2 * F + F), slice(b * BLK, (b + 1) * BLK))
        gq = feature_gradient(qkt[at], selq, gmq, gfq)
        pfk[i] = dot(fqt[i], mix)
        qkt[at] = gq
        nin[i, :, :E] = dot(scot[i], ga_b[:, :E])

    step5()
    exchange_second(2)
    quarter(0, inside_back)
    quarter(1, inside_back)
    exchange_second(3)
    exchange_third(2)
    quarter(2, inside_back)
    quarter(3, inside_back)
    exchange_third(3)

    def value_gradient(group):
        for b in reversed(range(nb)):
            for j in range(gh):
                h = group * gh + j
                i = h * nb + b
                state = run[h]
                state_b = state.astype(bf16)
                st[i] = state_b
                run[h] = state + ub[i]
                rows_b = slice(b * BLK, (b + 1) * BLK)
                p[rows_b, h * E : (h + 1) * E] = dot(fk[i], state_b[:, :E]) + nin[i, :, :E]

    def key_gradient(b):
        rows_b = slice(b * BLK, (b + 1) * BLK)
        for h in range(nh):
            i = h * nb + b
            gfk = dot(st[i], vaug[i], NT) + pfk[i]
            at = (slice(2 * F * h + F, 2 * F * (h + 1)), rows_b)
            qkt[at] = feature_gradient(qkt[at], selk, gmk, gfk)
        p[rows_b, nh * E :] = qkt[:, rows_b].T

    total_rows = nb * BLK
    width = gp.shape[1]
    lanes = ((0, gh * E), (gh * E, nh * E), (nh * E, width))

    def spread(part):
        lo, up = lanes[part]
        one, two, three = taps[0:1, lo:up], taps[1:2, lo:up], taps[2:3, lo:up]
        p[total_rows:, lo:up] = jnp.zeros((16, up - lo), f32)
        for b in range(nb):
            ext = p[b * BLK : (b + 1) * BLK + 16, lo:up]
            grad = one * ext[:BLK] + two * ext[1 : BLK + 1] + three * ext[2 : BLK + 2]
            gp[b * BLK : (b + 1) * BLK, lo:up] = grad.astype(bf16)
        edge = jnp.concatenate([jnp.zeros((16, up - lo), f32), p[0:16, lo:up]], 0)
        edge = jnp.where(s == 0, 0.0, two * edge[1:17] + three * edge[2:18])
        gp[total_rows : total_rows + 16, lo:up] = edge.astype(bf16)
        gp[total_rows + 16 :, lo:up] = jnp.zeros((E - 16, up - lo), bf16)

    def rows_at(j):
        return pl.ds(pl.multiple_of(j * rows, rows), rows)

    def part_of(part):
        return pl.ds(lanes[part][0], lanes[part][1] - lanes[part][0])

    def back(part):
        return remote(
            gp.at[pl.ds(total_rows, 16), part_of(part)],
            hi.at[(x + 1) % nx, :, part_of(part)],
            sh.at[part],
            qh.at[part],
            seq=prev,
            head=nx - 1,
        )

    near = rows // 2

    def out_far(part, way):
        j = (x + 2) % nx
        src = pl.ds(pl.multiple_of(j * rows + way * near, near), near)
        return remote(
            gp.at[src, part_of(part)],
            relay.at[way, :, part_of(part)],
            sr1.at[part],
            qr1.at[part, way],
            head=right if way == 0 else left,
        )

    def on_far(part, way):
        lo, up = lanes[part]
        return remote(
            relay.at[way, :, part_of(part)],
            gin.at[pl.ds(way * near, near), pl.ds(2 * width + lo, up - lo)],
            sr2.at[part],
            qr2.at[part],
            head=right if way == 0 else left,
        )

    def pass_on(part):
        for way in range(2):
            arrived(relay.at[way, :, part_of(part)], qr1.at[part, way])
            on_far(part, way).start()

    def over(part, k):
        j = (x + k) % nx
        return remote(
            gp.at[rows_at(j), part_of(part)],
            gin.at[:, pl.ds((nx - k) * width + lanes[part][0], lanes[part][1] - lanes[part][0])],
            sx.at[part],
            qx.at[part],
            head=j,
        )

    def send_rows(part):
        if part < 2:
            out_far(part, 0).start()
            out_far(part, 1).start()
        else:
            over(part, 2).start()
        over(part, 1).start()
        over(part, 3).start()
        back(part).start()

    pieces = ny * nz
    height = gwb.shape[2]
    half = height // 2
    per_step = 1024 // (2 * height)
    low_half, high_half = pl.ds(0, half), pl.ds(half, half)

    def pair(part, j):
        at = part_of(part)
        return remote(
            gwb.at[j, 1 - core, :, at], rp.at[j, :, at], sp.at[part], qp.at[part], seq=sibling
        )

    def weight_part(part):
        lo, up = lanes[part]

        def weight_step(i, carry):
            at = pl.ds(pl.multiple_of(i * 1024, 1024), 1024)
            whole = dot(gt[at, :], gp[:, lo:up]).astype(bf16)
            whole = whole.reshape(per_step, 2, height, up - lo)
            for q in range(per_step):
                gwb[i * per_step + q, :, :, lo:up] = whole[q]
                pair(part, i * per_step + q).start()
            return carry

        lax.fori_loop(0, pieces // per_step, weight_step, 0)

    def go_2a(part, k):
        to, at = (z + k) % nz, part_of(part)
        return remote(
            t.at[:, to, low_half, at],
            r2a.at[k, :, :, at],
            s2a.at[part],
            q2a.at[part],
            seq=at_seq(y, to, core),
        )

    def go_2b(part, k):
        to, at = (y + k) % ny, part_of(part)
        return remote(
            t.at[to, :, high_half, at],
            r2b.at[k, :, :, at],
            s2b.at[part],
            q2b.at[part],
            seq=at_seq(to, z, core),
        )

    def go_3a(part, k):
        to, at = (y + k) % ny, part_of(part)
        return remote(
            va.at[to, :, at],
            r3a.at[k, :, at],
            s3a.at[part],
            q3a.at[part],
            seq=at_seq(to, z, core),
        )

    def go_3b(part, k):
        to, at = (z + k) % nz, part_of(part)
        return remote(
            vb.at[to, :, at],
            r3b.at[k, :, at],
            s3b.at[part],
            q3b.at[part],
            seq=at_seq(y, to, core),
        )

    def weight_second(part):
        lo, up = lanes[part]

        def pair_sum(j, carry):
            both = gwb[j, core, :, lo:up].astype(f32) + rp[j, :, lo:up].astype(f32)
            t[j // nz, j % nz, :, lo:up] = both.astype(bf16)
            return carry

        arrived(rp.at[:, :, part_of(part)], qp.at[part])
        lax.fori_loop(0, pieces, pair_sum, 0)
        for k in range(1, max(ny, nz)):
            if k < nz:
                go_2a(part, k).start()
            if k < ny:
                go_2b(part, k).start()

    def weight_third(part):
        lo, up = lanes[part]
        at = part_of(part)
        arrived(r2a.at[pl.ds(1, nz - 1), :, :, at], q2a.at[part])
        arrived(r2b.at[pl.ds(1, ny - 1), :, :, at], q2b.at[part])
        for i in range(ny):
            total = t[i, z, 0:half, lo:up].astype(f32)
            for k in range(1, nz):
                total = total + r2a[k, i, :, lo:up].astype(f32)
            va[i, :, lo:up] = total.astype(bf16)
        for i in range(nz):
            total = t[y, i, half:, lo:up].astype(f32)
            for k in range(1, ny):
                total = total + r2b[k, i, :, lo:up].astype(f32)
            vb[i, :, lo:up] = total.astype(bf16)
        for k in range(1, max(ny, nz)):
            if k < ny:
                go_3a(part, k).start()
            if k < nz:
                go_3b(part, k).start()

    exchange_done(2)
    unpack_group(2)
    value_gradient(0)
    spread(0)
    send_rows(0)
    weight_part(0)
    exchange_done(3)
    unpack_group(3)
    value_gradient(1)
    spread(1)
    send_rows(1)
    weight_second(0)
    for b in range(nb):
        key_gradient(b)
        if b == nb // 2:
            pass_on(0)
    spread(2)
    send_rows(2)
    weight_part(1)
    pass_on(1)
    weight_second(1)
    weight_part(2)
    weight_third(0)

    steps = depth // 256

    def load(i, slot):
        at = pl.ds(pl.multiple_of(i * 256, 256), 256)
        for j in range(nx):
            src = w.at[:, at] if j == 0 else wf.at[j - 1, :, at]
            dst = wbuf.at[slot, pl.ds(j * width, width)]
            pltpu.make_async_copy(src, dst, sw.at[slot]).start()

    def as_many(part, count):
        return gin.at[:, pl.ds(0, count * (lanes[part][1] - lanes[part][0]))]

    def gi_out(i):
        at = pl.ds(pl.multiple_of(i * 256, 256), 256)
        return pltpu.make_async_copy(gi_v.at[:, at], gi.at[:, at], s_gi)

    step6()
    load(0, 0)
    load(1, 1)
    weight_second(2)
    gin[:, :width] = gp[rows_at(x), :]
    for part in range(3):
        if part < 2:
            arrived(as_many(part, 1), qr2.at[part])
        arrived(as_many(part, 2 if part < 2 else 3), qx.at[part])

    @pl.when(x == nx - 1)
    def _():
        for part in range(3):
            arrived(hi.at[:, :, part_of(part)], qh.at[part])
        for k in range(nx):
            at = slice(k * width, (k + 1) * width)
            last = gin[rows - 16 :, at].astype(f32) + hi[k].astype(f32)
            gin[rows - 16 :, at] = last.astype(bf16)

    def input_step(i, carry):
        at = pl.ds(pl.multiple_of(i * 256, 256), 256)
        slot = i % 2
        pltpu.make_async_copy(wbuf.at[slot], wbuf.at[slot], sw.at[slot]).wait()
        gi_v[:, at] = dot(gin[...], wbuf[slot]).astype(bf16)
        gi_out(i).start()

        @pl.when(i + 2 < steps)
        def _():
            load(i + 2, slot)

        return carry

    lax.fori_loop(0, steps // 4, input_step, 0)
    weight_third(1)
    lax.fori_loop(steps // 4, 5 * steps // 8, input_step, 0)
    weight_third(2)
    lax.fori_loop(5 * steps // 8, steps, input_step, 0)

    for part in range(3):
        at = part_of(part)
        arrived(r3a.at[pl.ds(1, ny - 1), :, at], q3a.at[part])
        arrived(r3b.at[pl.ds(1, nz - 1), :, at], q3b.at[part])

    def put(at, total):
        for h in range(nh):
            narrow = total[:, nh * E + 2 * F * h : nh * E + 2 * F * (h + 1)]
            gw_v[at, h, :] = jnp.concatenate([narrow, total[:, h * E : (h + 1) * E]], 1)

    total = va[y].astype(f32)
    for k in range(1, ny):
        total = total + r3a[k].astype(f32)
    put(slice(0, half), total)
    total = vb[z].astype(f32)
    for k in range(1, nz):
        total = total + r3b[k].astype(f32)
    put(slice(half, height), total)
    gw_out = pltpu.make_async_copy(gw_v, gw, s_gw)
    gw_out.start()

    for part in range(3):
        at = part_of(part)
        back(part).wait_send()
        if part < 2:
            sent(as_many(part, 1), sr1.at[part])
            sent(as_many(part, 1), sr2.at[part])
        sent(as_many(part, 2 if part < 2 else 3), sx.at[part])
        sent(rp.at[:, :, at], sp.at[part])
        sent(r2a.at[pl.ds(1, nz - 1), :, :, at], s2a.at[part])
        sent(r2b.at[pl.ds(1, ny - 1), :, :, at], s2b.at[part])
        sent(r3a.at[pl.ds(1, ny - 1), :, at], s3a.at[part])
        sent(r3b.at[pl.ds(1, nz - 1), :, at], s3b.at[part])
    for e in range(4):
        sent(r1.at[e, pl.ds(0, ga - 1)], s1.at[e])
        sent(r2.at[e, pl.ds(0, gb - 1)], s2.at[e])
        sent(res.at[e, pl.ds(0, (ga - 1) * piece)], s3.at[e])
    sent(tok, s_own.at[0])
    sent(tok, s_own.at[1])

    @pl.when(x == nx - 1)
    def _():
        sent(tok.at[pl.ds(0, 16 * nx)], s_hal)

    step7()
    pltpu.make_async_copy(att_v, att, s_att).wait()
    pltpu.make_async_copy(gi_v, gi, s_gi).wait()
    gw_out.wait()


def hand_on_kernel(count, *refs):
    srcs, dsts, sems = refs[:count], refs[count : 2 * count], refs[2 * count]
    copies = [pltpu.make_async_copy(srcs[i], dsts[i], sems.at[i]) for i in range(count)]
    for copy in copies:
        copy.start()
    for copy in copies:
        copy.wait()


def hand_on(*arrays):
    hbm = pl.BlockSpec(memory_space=pl.ANY)
    count = len(arrays)
    return pl.pallas_call(
        functools.partial(hand_on_kernel, count),
        out_shape=tuple(jax.ShapeDtypeStruct(a.shape, a.dtype) for a in arrays),
        in_specs=[hbm] * count,
        out_specs=(hbm,) * count,
        scratch_shapes=[pltpu.SemaphoreType.DMA((count,))],
        compiler_params=pltpu.CompilerParams(vmem_limit_bytes=2**20),
    )(*arrays)


def local(nx, ny, nz, tokens, in_weight, conv_kernel, grad_out):
    depth, nh, _ = in_weight.shape
    wt = jnp.transpose(in_weight, (1, 2, 0)).reshape(nh * CHAN, depth)
    rows = tokens.shape[0]
    every = grad_out.shape[0]
    width = nh * CHAN
    nb = every // BLK
    n = nh * nb
    ga, gb, ns = 2 * nz, ny, 2 * ny * nz
    piece = -(-(nh // 2) * FS // (16 * ga)) * 16
    height = depth // ns
    half = height // 2
    hbm = pl.BlockSpec(memory_space=pl.ANY)
    dma = pltpu.SemaphoreType.DMA
    consts = [
        jnp.asarray(selection(True), bf16),
        jnp.asarray(selection(False), bf16),
        jnp.asarray(gradient_map(True), bf16),
        jnp.asarray(gradient_map(False), bf16),
    ]
    att, gi, gw, _ = pl.pallas_call(
        functools.partial(kernel, nx, ny, nz, nh),
        out_shape=(
            pltpu.VMEM((every, nh * E), bf16),
            pltpu.VMEM((rows, depth), bf16),
            pltpu.VMEM((height, nh, CHAN), f32),
            jax.ShapeDtypeStruct((nx - 1, width, depth), bf16),
        ),
        in_specs=[hbm] * 8,
        out_specs=(hbm, hbm, hbm, hbm),
        scratch_shapes=[
            pltpu.VMEM(conv_kernel.shape, f32),
            pltpu.VMEM((2 * FS, 3 * F), bf16),
            pltpu.VMEM((2 * FS, 3 * F), bf16),
            pltpu.VMEM((F, 2 * FS), bf16),
            pltpu.VMEM((F, 2 * FS), bf16),
            pltpu.VMEM((every, nh * E), bf16),
            pltpu.VMEM((every, nh * E), bf16),
            pltpu.VMEM((rows, depth), bf16),
            pltpu.VMEM((height, nh, CHAN), f32),
            pltpu.VMEM((width, depth), bf16),
            pltpu.VMEM((nx, rows, depth), bf16),
            pltpu.VMEM((depth, every + E), bf16),
            pltpu.VMEM((16 + every, width), f32),
            pltpu.VMEM((16, depth), bf16),
            pltpu.VMEM((8, width), f32),
            pltpu.VMEM((nh * 2 * F, every), f32),
            pltpu.VMEM((n, BLK, 2 * E), bf16),
            pltpu.VMEM((n, FS, BLK), bf16),
            pltpu.VMEM((n, FS, BLK), bf16),
            pltpu.VMEM((n, BLK, FS), bf16),
            pltpu.VMEM((n, BLK, FS), bf16),
            pltpu.VMEM((n, FS, 2 * E), f32),
            pltpu.VMEM((n, BLK, 2 * E), f32),
            pltpu.VMEM((n, BLK, BLK), bf16),
            pltpu.VMEM((n, BLK, 2 * E), bf16),
            pltpu.VMEM((nh, FS, 2 * E), f32),
            pltpu.VMEM((n, FS, 2 * E), bf16),
            pltpu.VMEM((n, FS, BLK), f32),
            pltpu.VMEM((every + E, width), bf16),
            pltpu.VMEM((4, ga * piece, E), bf16),
            pltpu.VMEM((4, ga, piece, E), bf16),
            pltpu.VMEM((4, piece, E), bf16),
            pltpu.VMEM((4, gb, piece, E), bf16),
            pltpu.VMEM((4, ga, piece, E), bf16),
            pltpu.VMEM((4, ga * piece, E), bf16),
            pltpu.VMEM((2, nx * width, 256), bf16),
            pltpu.VMEM((rows, nx * width), bf16),
            pltpu.VMEM((2, rows // 2, nh * E), bf16),
            pltpu.VMEM((nx, 16, width), bf16),
            pltpu.VMEM((ny * nz, 2, height, width), bf16),
            pltpu.VMEM((ny * nz, height, width), bf16),
            pltpu.VMEM((ny, nz, height, width), bf16),
            pltpu.VMEM((nz, ny, half, width), bf16),
            pltpu.VMEM((ny, nz, half, width), bf16),
            pltpu.VMEM((ny, half, width), bf16),
            pltpu.VMEM((nz, half, width), bf16),
            pltpu.VMEM((ny, half, width), bf16),
            pltpu.VMEM((nz, half, width), bf16),
            dma((2,)),
            dma((2, 2)),
            dma((2,)),
            dma(()),
            dma(()),
            dma(()),
            dma(()),
            dma(()),
            dma(()),
            dma((4,)),
            dma((4,)),
            dma((4,)),
            dma((4,)),
            dma((4,)),
            dma((4,)),
            dma((2,)),
            dma((2,)),
            dma((2, 2)),
            dma((2,)),
            dma((2,)),
            dma((3,)),
            dma((3,)),
            dma((3,)),
            dma((3,)),
            dma((3,)),
            dma((3,)),
            dma((3,)),
            dma((3,)),
            dma((3,)),
            dma((3,)),
            dma((3,)),
            dma((3,)),
            dma((3,)),
            dma((3,)),
            dma(()),
            dma(()),
            dma(()),
            dma(()),
            dma((5,)),
            dma(()),
            dma(()),
            dma(()),
            dma(()),
            dma(()),
            dma(()),
            dma(()),
            dma(()),
            dma((ny,)),
            dma((ny,)),
            dma((nz,)),
            dma((nz,)),
            dma(()),
            dma(()),
            dma(()),
            dma(()),
            dma((2,)),
            dma((2,)),
        ],
        compiler_params=pltpu.CompilerParams(
            collective_id=0, has_side_effects=True, vmem_limit_bytes=60 * 2**20
        ),
    )(tokens, wt, conv_kernel, grad_out, *consts)
    return hand_on(att, gi, gw)


def solution(mesh):
    nx, ns = mesh.shape["head"], mesh.shape["seq"]
    ny = math.isqrt(ns // 2)
    nz = ns // 2 // ny
    placed = (
        P(("seq", "head"), None),
        P(None, "head", None),
        P(None, "head", None),
        P("seq", "head"),
    )
    return jax.shard_map(
        functools.partial(local, nx, ny, nz),
        mesh=mesh,
        in_specs=placed,
        out_specs=(P("seq", "head"), P(("seq", "head"), None), P("seq", "head", None)),
        check_vma=False,
    )
```

```python
import functools
import math

import jax
import jax.numpy as jnp
import numpy as np
from jax import lax
from jax.experimental import pallas as pl
from jax.experimental.pallas import tpu as pltpu
from jax.sharding import PartitionSpec as P

F = 16
E = 128
BLK = 256
CHAN = 160
FS = 160
NF = 1 + F + F * (F + 1) // 2
KAPPA = 32.0 ** -0.25
f32 = jnp.float32
bf16 = jnp.bfloat16
NN = (((1,), (0,)), ((), ()))
NT = (((1,), (1,)), ((), ()))


def dot(a, b, dims=NN):
    return lax.dot_general(a, b, dims, preferred_element_type=f32)


def bf_parts(value, count):
    parts = []
    rest = np.float64(value)
    for _ in range(count):
        part = np.float64(np.asarray(rest, dtype=jnp.bfloat16))
        parts.append(part)
        rest = rest - part
    return parts


def selection(weighted):
    sel = np.zeros((2 * FS, 3 * F), np.float64)
    sel[0, 32] = 1.0
    sel[FS, 32] = 1.0
    for i in range(F):
        row = 1 + i
        sel[row, i] = sel[row, F + i] = 1.0
        for c, part in enumerate(bf_parts(0.5 / KAPPA, 3)):
            sel[FS + row, 32 + c] = part
    row = 1 + F
    for i in range(F):
        for j in range(i, F):
            first = 2.0 if (weighted and j > i) else 1.0
            sel[row, i] = sel[row, F + i] = first
            sel[FS + row, j] = sel[FS + row, F + j] = 1.0
            row += 1
    return sel


def gradient_map(weighted):
    sel = selection(weighted)
    return np.concatenate([sel[:FS, :F].T, sel[FS:, :F].T], 1)


def remote(src, dst, send, recv, **where):
    return pltpu.make_async_remote_copy(
        src_ref=src,
        dst_ref=dst,
        send_sem=send,
        recv_sem=recv,
        device_id=where,
        device_id_type=pl.DeviceIdType.MESH,
    )


def arrived(ref, sem):
    remote(ref, ref, sem, sem, seq=lax.axis_index("seq")).wait_recv()


def sent(ref, sem):
    remote(ref, ref, sem, sem, seq=lax.axis_index("seq")).wait_send()


def greet(sem, **where):
    pl.semaphore_signal(sem, inc=1, device_id=where, device_id_type=pl.DeviceIdType.MESH)


def weight_gather(nx, ny, nz, x, y, z, core, w, wf, sems):
    s1, q1, sr, qr, sa, qa, sb, qb, sc, qc, sd, qd, sf, qf, sg, qg, se, qe = sems
    chan, depth = w.shape
    half = chan // 2
    quarter = half // 2
    eighth = quarter // 2
    col = depth // (ny * nz)
    base = core * half
    rows_c = pl.ds(pl.multiple_of(base, 16), half)
    rows_a = pl.ds(pl.multiple_of(base, 16), quarter)
    rows_b = pl.ds(pl.multiple_of(base + quarter, 16), quarter)
    far = pl.ds(0, nx - 1)

    def piece_a(n):
        return pl.ds(pl.multiple_of(base + n * eighth, 16), eighth)

    def piece_b(n):
        return pl.ds(pl.multiple_of(base + quarter + n * eighth, 16), eighth)

    def cols(yy, zz):
        return pl.ds(pl.multiple_of((yy * nz + zz) * col, 128), col)

    def row_of(yy):
        return pl.ds(pl.multiple_of(yy * nz * col, 128), nz * col)

    def at_seq(yy, zz, cc):
        return (yy * nz + zz) * 2 + cc

    mine = cols(y, z)
    ring_y = (1, ny - 1) if ny > 2 else (1,)
    ring_z = (1, nz - 1) if nz > 2 else (1,)

    def spread_x(k):
        return remote(w.at[rows_c, mine], wf.at[nx - k - 1, rows_c, mine], s1, q1, head=(x + k) % nx)

    def spread_on(k):
        here = wf.at[nx - k - 1, rows_a if k == 1 else rows_b, mine]
        there = wf.at[nx // 2 - 1, rows_a if k == 1 else rows_b, mine]
        return remote(here, there, sr, qr, head=(x + k) % nx)

    def a_z(k):
        here = wf.at[far, rows_a, mine]
        return remote(here, here, sa, qa, seq=at_seq(y, (z + k) % nz, core))

    def b_y(k):
        here = wf.at[far, rows_b, mine]
        return remote(here, here, sb, qb, seq=at_seq((y + k) % ny, z, core))

    def a_y(k):
        here = wf.at[far, rows_a, row_of(y)]
        return remote(here, here, sc.at[k], qc.at[k], seq=at_seq((y + k) % ny, z, core))

    def b_z(k, yy):
        here = wf.at[far, rows_b, cols(yy, z)]
        return remote(here, here, sd.at[k], qd.at[k], seq=at_seq(y, (z + k) % nz, core))

    def a_y_on(k):
        here = wf.at[far, piece_a(0 if k == 1 else 1), row_of((y - k) % ny)]
        return remote(here, here, sf, qf, seq=at_seq((y + k) % ny, z, core))

    def b_z_on(k, yy):
        here = wf.at[far, piece_b(0 if k == 1 else 1), cols(yy, (z - k) % nz)]
        return remote(here, here, sg, qg, seq=at_seq(y, (z + k) % nz, core))

    def across(part):
        here = wf.at[far, rows_a if part == 0 else rows_b]
        return remote(here, here, se.at[part], qe.at[part], seq=at_seq(y, z, 1 - core))

    def lanes(rows, count):
        return wf.at[far, rows, pl.ds(0, count * col)]

    def step0():
        for k in (1, nx - 1):
            spread_x(k).start()

    def step1():
        arrived(wf.at[pl.ds(0, 2), rows_c, mine], q1)
        for k in (1, nx - 1):
            spread_on(k).start()

    def step2():
        arrived(wf.at[0, rows_c, mine], qr)
        for k in range(1, max(ny, nz)):
            if k < nz:
                a_z(k).start()
            if k < ny:
                b_y(k).start()

    def step3():
        arrived(lanes(rows_a, nz - 1), qa)
        for k in ring_y:
            a_y(k).start()
        arrived(lanes(rows_b, ny - 1), qb)
        for k in ring_z:
            for yy in range(ny):
                b_z(k, yy).start()

    def step4():
        for k in ring_y:
            arrived(lanes(rows_a, nz), qc.at[ny - k])
            if ny > 2:
                a_y_on(ny - k).start()
        for k in ring_z:
            arrived(lanes(rows_b, ny), qd.at[nz - k])
            if nz > 2:
                for yy in range(ny):
                    b_z_on(nz - k, yy).start()

    def step5():
        if ny > 2:
            arrived(lanes(rows_a, nz), qf)
        across(0).start()
        if nz > 2:
            arrived(lanes(rows_b, ny), qg)
        across(1).start()

    def step6():
        across(0).wait_recv()
        across(1).wait_recv()

    def step7():
        sent(wf.at[pl.ds(0, 2), rows_c, mine], s1)
        sent(wf.at[0, rows_c, mine], sr)
        sent(lanes(rows_a, nz - 1), sa)
        sent(lanes(rows_b, ny - 1), sb)
        for k in ring_y:
            sent(lanes(rows_a, nz), sc.at[k])
        for k in ring_z:
            sent(lanes(rows_b, ny), sd.at[k])
        if ny > 2:
            sent(lanes(rows_a, nz), sf)
        if nz > 2:
            sent(lanes(rows_b, ny), sg)
        across(0).wait_send()
        across(1).wait_send()

    return step0, step1, step2, step3, step4, step5, step6, step7


def kernel(
    nx, ny, nz, nh,
    tok, wt, cv_hbm, go, selq_hbm, selk_hbm, gmq_hbm, gmk_hbm,
    att, gi, gw, wf,
    cv, selq, selk, gmq, gmk, go_v, att_v, gi_v, gw_v, w, g, gt, p, hal, taps, qkt, vaug, fqt, fkt, fq, fk, ub, nin, scot, gna, run, st, pfk, gp,
    loc, r1, tot, r2, out, res,
    wbuf, gin, relay, hi, gwb, rp, t, r2a, r2b, va, vb, r3a, r3b,
    s_own, r_own, r_rest, s_fwd, r_fwd, s_hal, r_hal, s_w, s_tok,
    s1, q1, s2, q2, s3, q3,
    sw, sr1, qr1, sr2, qr2, sx, qx, sh, qh, sp, qp, s2a, q2a, s2b, q2b, s3a, q3a, s3b, q3b, s_att, s_gi, s_gw, s_go, s_const,
    *sems,
):
    x = lax.axis_index("head")
    s = lax.axis_index("seq")
    ns = 2 * ny * nz
    core, z, y = s % 2, (s // 2) % nz, s // (2 * nz)
    left, right, opp = (x + nx - 1) % nx, (x + 1) % nx, (x + 2) % nx
    prev, after = (s + ns - 1) % ns, (s + 1) % ns
    ga, gb = 2 * nz, ny
    me_a, me_b = s % ga, s // ga
    rows, depth = tok.shape
    nb = go.shape[0] // BLK
    ch = rows // 4
    piece = loc.shape[1] // ga
    gh = nh // 2
    per = gh * nb

    def at_seq(yy, zz, cc):
        return (yy * nz + zz) * 2 + cc

    sibling = at_seq(y, z, 1 - core)
    bar = pltpu.get_barrier_semaphore()
    for k in range(1, nx):
        greet(bar, head=(x + k) % nx)
    for k in range(1, ga):
        greet(bar, seq=me_b * ga + (me_a + k) % ga)
    for k in range(1, gb):
        greet(bar, seq=((me_b + k) % gb) * ga + me_a)
    greet(bar, seq=prev)
    greet(bar, seq=after)
    greet(bar, seq=prev, head=nx - 1)

    @pl.when(x == nx - 1)
    def _():
        for j in range(nx):
            greet(bar, seq=after, head=j)

    local_tok = pltpu.make_async_copy(tok, g.at[x], s_tok)
    local_tok.start()
    local_go = pltpu.make_async_copy(go, go_v, s_go)
    local_go.start()
    small = [
        pltpu.make_async_copy(src, dst, s_const.at[i])
        for i, (src, dst) in enumerate(
            ((cv_hbm, cv), (selq_hbm, selq), (selk_hbm, selk), (gmq_hbm, gmq), (gmk_hbm, gmk))
        )
    ]
    for copy in small:
        copy.start()
    loads = []
    for h in range(nh):
        base = h * CHAN
        loads.append(
            pltpu.make_async_copy(
                wt.at[base + 2 * F : base + CHAN], w.at[h * E : (h + 1) * E], s_w
            )
        )
        loads.append(
            pltpu.make_async_copy(
                wt.at[base : base + 2 * F],
                w.at[nh * E + 2 * F * h : nh * E + 2 * F * (h + 1)],
                s_w,
            )
        )
    for copy in loads:
        copy.start()
    greeted = nx - 1 + ga - 1 + gb - 1 + 3
    pl.semaphore_wait(bar, jnp.where(x == nx - 1, greeted + nx, greeted))

    def chunk(c):
        return pl.ds(c * ch, ch)

    def own(way, c, first):
        return remote(
            tok.at[chunk(c)],
            g.at[x, chunk(c)],
            s_own.at[0 if first else 1],
            r_own.at[way, c % 2] if first else r_rest.at[way],
            head=right if way == 0 else left,
        )

    def forward(way, c):
        slot = left if way == 0 else right
        return remote(
            g.at[slot, chunk(c)],
            g.at[slot, chunk(c)],
            s_fwd,
            r_fwd,
            head=right if way == 0 else left,
        )

    def halo(j):
        return remote(tok.at[pl.ds(rows - 16, 16)], hal, s_hal, r_hal, seq=after, head=j)

    step0, step1, step2, step3, step4, step5, step6, step7 = weight_gather(
        nx, ny, nz, x, y, z, core, w, wf, sems
    )
    pltpu.make_async_copy(w, w, s_w).wait()
    step0()
    own(0, 0, True).start()
    own(1, 2, True).start()
    @pl.when(x == nx - 1)
    def _():
        for j in range(nx):
            halo(j).start()

    lane = lax.broadcasted_iota(jnp.int32, (BLK, BLK), 1)
    sub = lax.broadcasted_iota(jnp.int32, (BLK, BLK), 0)
    frow = lax.broadcasted_iota(jnp.int32, (FS, E), 0)

    for copy in small:
        copy.wait()

    for j in range(3):
        lines = [cv[j, h : h + 1, :] for h in range(nh)]
        for h in range(nh):
            taps[j : j + 1, h * E : (h + 1) * E] = lines[h][:, 2 * F :]
        taps[j : j + 1, nh * E :] = jnp.concatenate([v[:, : 2 * F] for v in lines], 1) * KAPPA

    def rows_of(a):
        return pl.ds(pl.multiple_of(a * piece, 16), piece)

    def first(e, k):
        a = (me_a + k) % ga
        return remote(
            loc.at[e, rows_of(a)], r1.at[e, me_a], s1.at[e], q1.at[e], seq=me_b * ga + a
        )

    def second(e, k):
        b = (me_b + k) % gb
        return remote(tot.at[e], r2.at[e, me_b], s2.at[e], q2.at[e], seq=b * ga + me_a)

    def third(e, k):
        a = (me_a + k) % ga
        return remote(
            out.at[e, a], res.at[e, rows_of(me_a)], s3.at[e], q3.at[e], seq=me_b * ga + a
        )

    def exchange_first(e):
        for k in range(1, ga):
            first(e, k).start()
        r1[e, me_a] = loc[e, rows_of(me_a), :]

    def exchange_second(e):
        arrived(r1.at[e, pl.ds(0, ga - 1)], q1.at[e])
        total = jnp.zeros((piece, E), f32)
        for a in range(ga):
            total = total + r1[e, a].astype(f32)
        tot[e] = total.astype(bf16)
        for k in range(1, gb):
            second(e, k).start()

    def exchange_third(e):
        arrived(r2.at[e, pl.ds(0, gb - 1)], q2.at[e])
        r2[e, me_b] = tot[e]
        total = jnp.zeros((piece, E), f32)
        for b in range(gb):
            ahead = b < me_b if e < 2 else b > me_b
            total = total + jnp.where(ahead, r2[e, b].astype(f32), 0.0)
        for step in range(ga):
            a = step if e < 2 else ga - 1 - step
            out[e, a] = total.astype(bf16)
            total = total + r1[e, a].astype(f32)
        for k in range(1, ga):
            third(e, k).start()
        res[e, rows_of(me_a), :] = out[e, me_a]

    def exchange_done(e):
        arrived(res.at[e, pl.ds(0, (ga - 1) * piece)], q3.at[e])

    def pack(e, h, whole):
        column = jnp.concatenate([whole[:, E:], jnp.zeros((2 * E - FS, E), f32)], 0)
        line = column.T[0:1, :]
        body = jnp.where(frow == NF, line[:, :E], jnp.where(frow == NF + 1, line[:, E:], whole[:, :E]))
        loc[e, h * FS : (h + 1) * FS, :] = body.astype(bf16)

    def pack_group(e):
        for j in range(gh):
            h = (e % 2) * gh + j
            whole = ub[h * nb]
            for b in range(1, nb):
                whole = whole + ub[h * nb + b]
            pack(e, j, whole)
        if gh * FS < loc.shape[1]:
            loc[e, gh * FS :, :] = jnp.zeros((loc.shape[1] - gh * FS, E), bf16)

    def unpack_group(e):
        for j in range(gh):
            body = res[e, j * FS : (j + 1) * FS, :].astype(f32)
            line = jnp.concatenate([body[NF : NF + 1, :], body[NF + 1 : NF + 2, :]], 1)
            column = jnp.broadcast_to(line, (E, 2 * E)).T[:FS, :]
            run[(e % 2) * gh + j] = jnp.concatenate([jnp.where(frow < NF, body, 0.0), column], 1)

    def factors(u, sel):
        high = u.astype(bf16)
        low = (u - high.astype(f32)).astype(bf16)
        stack = jnp.concatenate([high, low, jnp.ones((F, BLK), bf16)], 0)
        both = dot(sel[...], stack)
        return both[:FS], both[FS:]

    def block_at(b):
        return pl.ds(pl.multiple_of(b * BLK, BLK), BLK)

    def convolve(b):
        ext = p[pl.ds(pl.multiple_of(b * BLK, BLK), BLK + 16), :]
        conv = taps[0:1, :] * ext[16:] + taps[1:2, :] * ext[15:-1] + taps[2:3, :] * ext[14:-2]
        qkt[:, block_at(b)] = conv[:, nh * E :].T
        for h in range(nh):
            vaug[h * nb + b] = jnp.concatenate(
                [conv[:, h * E : (h + 1) * E].astype(bf16), jnp.ones((BLK, E), bf16)], 1
            )

    def featurize(b, group):
        for j in range(gh):
            h = group * gh + j
            i = h * nb + b
            at = block_at(b)
            first_q, second_q = factors(qkt[2 * F * h : 2 * F * h + F, at], selq)
            first_k, second_k = factors(qkt[2 * F * h + F : 2 * F * (h + 1), at], selk)
            q = (first_q * second_q).astype(bf16)
            k = (first_k * second_k).astype(bf16)
            fqt[i] = q
            fkt[i] = k
            fq[i] = q.T
            fk[i] = k.T
            ub[i] = dot(k, vaug[i])

    def project(slot):
        base = pl.multiple_of(slot * rows, rows)
        p[pl.ds(16 + base, rows), :] = dot(g[slot], w[...], NT)

    def turn(slot):
        base = pl.multiple_of(slot * rows, rows)

        def piece_of(i, carry):
            at = pl.ds(pl.multiple_of(i * 256, 256), 256)
            gt[at, pl.ds(base, rows)] = g[slot, :, at].T
            return carry

        lax.fori_loop(0, depth // 256, piece_of, 0)

    local_tok.wait()
    project(x)
    turn(x)
    step1()
    own(0, 1, True).start()
    own(1, 3, True).start()
    own(0, 2, False).start()
    own(1, 0, False).start()
    own(0, 3, False).start()
    own(1, 1, False).start()
    step2()
    for c in range(2):
        arrived(g.at[left, chunk(c)], r_own.at[0, c])
        forward(0, c).start()
        arrived(g.at[right, chunk(c + 2)], r_own.at[1, c])
        forward(1, c + 2).start()
    step3()
    arrived(hal, r_hal)
    head_rows = dot(hal[...], w[...], NT)
    p[0:16, :] = jnp.where(s == 0, 0.0, head_rows)

    def turn_halo(i, carry):
        at = pl.ds(pl.multiple_of(i * 256, 256), 256)
        tail_rows = jnp.concatenate([hal[:, at], jnp.zeros((E - 16, 256), bf16)], 0)
        gt[at, nb * BLK :] = tail_rows.T
        return carry

    lax.fori_loop(0, depth // 256, turn_halo, 0)
    arrived(g.at[left, pl.ds(0, 2 * ch)], r_rest.at[0])
    project(left)
    arrived(g.at[right, pl.ds(0, 2 * ch)], r_rest.at[1])
    project(right)
    step4()
    for b in (x, right):
        convolve(b)
        featurize(b, 0)
        featurize(b, 1)
    turn(left)
    turn(right)
    arrived(g.at[opp], r_fwd)
    project(opp)
    for b in (opp, left):
        convolve(b)
        featurize(b, 0)
    pack_group(0)
    exchange_first(0)
    for b in (opp, left):
        featurize(b, 1)
    pack_group(1)
    exchange_first(1)

    def inside(i):
        score = jnp.where(sub >= lane, dot(fq[i], fkt[i]), 0.0).astype(bf16)
        scot[i] = jnp.where(lane >= sub, dot(fk[i], fqt[i]), 0.0).astype(bf16)
        nin[i] = dot(score, vaug[i])

    fold = g.shape[2] // BLK

    def raw_at(i):
        return (i // fold, slice(None), slice(i % fold * BLK, (i % fold + 1) * BLK))

    def inside_raw(i):
        h, b = i // nb, i % nb
        cot = go_v[b * BLK : (b + 1) * BLK, h * E : (h + 1) * E]
        g[raw_at(i)] = dot(cot, vaug[i, :, :E], NT).astype(bf16)

    def quarter(n, body):
        for i in range(n * per // 2, (n + 1) * per // 2):
            body(i)

    turn(opp)
    local_go.wait()
    quarter(0, inside)
    exchange_second(0)
    quarter(1, inside)
    exchange_second(1)
    quarter(2, inside)
    exchange_third(0)
    exchange_third(1)
    quarter(3, inside)
    sent(g.at[opp], s_fwd)
    for n in range(4):
        quarter(n, inside_raw)

    ones = jnp.ones((E, E), bf16)

    def attend(group):
        for b in range(nb):
            for j in range(gh):
                h = group * gh + j
                i = h * nb + b
                state = run[h]
                state_b = state.astype(bf16)
                run[h] = state + ub[i]
                both = dot(fq[i], state_b) + nin[i]
                num = both[:, :E]
                inv = 1.0 / both[:, E:]
                mean = num * inv
                at = (slice(b * BLK, (b + 1) * BLK), slice(h * E, (h + 1) * E))
                att_v[at] = mean.astype(bf16)
                scaled = go_v[at].astype(f32) * inv
                product = scaled * mean
                slope = dot(product.astype(bf16), ones) * (-1.0 / E)
                ga_b = jnp.concatenate([scaled.astype(bf16), slope.astype(bf16)], 1)
                gna[i] = ga_b
                nin[i, :, E:] = inv
                st[i] = state_b
                ub[i] = dot(fqt[i], ga_b)
        pack_group(2 + group)

    def att_out(group):
        at = pl.ds(group * gh * E, gh * E)
        return pltpu.make_async_copy(att_v.at[:, at], att.at[:, at], s_att)

    for group in range(2):
        exchange_done(group)
        unpack_group(group)
        attend(group)
        exchange_first(2 + group)
        att_out(group).start()

    def feature_gradient(u, sel, gm, grad):
        one, two = factors(u, sel)
        stack = jnp.concatenate([(grad * two).astype(bf16), (grad * one).astype(bf16)], 0)
        return dot(gm[...], stack)

    def inside_back(i):
        h, b = i // nb, i % nb
        ga_b = gna[i]
        inv = nin[i, :, E:]
        slope = ga_b[:, E:].astype(f32) * float(E)
        scaled = g[raw_at(i)].astype(f32) * jnp.concatenate([inv, inv], 1)
        mix = scaled + jnp.concatenate([slope, slope], 1)
        mix = jnp.where(sub >= lane, mix, 0.0).astype(bf16)
        mixt = mix.T
        gfq = dot(st[i], ga_b, NT) + dot(fkt[i], mixt)
        at = (slice(h * 2 * F, h * 2 * F + F), slice(b * BLK, (b + 1) * BLK))
        gq = feature_gradient(qkt[at], selq, gmq, gfq)
        pfk[i] = dot(fqt[i], mix)
        qkt[at] = gq
        nin[i, :, :E] = dot(scot[i], ga_b[:, :E])

    step5()
    exchange_second(2)
    quarter(0, inside_back)
    quarter(1, inside_back)
    exchange_second(3)
    exchange_third(2)
    quarter(2, inside_back)
    quarter(3, inside_back)
    exchange_third(3)

    def value_gradient(group):
        for b in reversed(range(nb)):
            for j in range(gh):
                h = group * gh + j
                i = h * nb + b
                state = run[h]
                state_b = state.astype(bf16)
                st[i] = state_b
                run[h] = state + ub[i]
                rows_b = slice(b * BLK, (b + 1) * BLK)
                p[rows_b, h * E : (h + 1) * E] = dot(fk[i], state_b[:, :E]) + nin[i, :, :E]

    def key_gradient(b):
        rows_b = slice(b * BLK, (b + 1) * BLK)
        for h in range(nh):
            i = h * nb + b
            gfk = dot(st[i], vaug[i], NT) + pfk[i]
            at = (slice(2 * F * h + F, 2 * F * (h + 1)), rows_b)
            qkt[at] = feature_gradient(qkt[at], selk, gmk, gfk)
        p[rows_b, nh * E :] = qkt[:, rows_b].T

    total_rows = nb * BLK
    width = gp.shape[1]
    lanes = ((0, gh * E), (gh * E, nh * E), (nh * E, width))

    def spread(part):
        lo, up = lanes[part]
        one, two, three = taps[0:1, lo:up], taps[1:2, lo:up], taps[2:3, lo:up]
        p[total_rows:, lo:up] = jnp.zeros((16, up - lo), f32)
        for b in range(nb):
            ext = p[b * BLK : (b + 1) * BLK + 16, lo:up]
            grad = one * ext[:BLK] + two * ext[1 : BLK + 1] + three * ext[2 : BLK + 2]
            gp[b * BLK : (b + 1) * BLK, lo:up] = grad.astype(bf16)
        edge = jnp.concatenate([jnp.zeros((16, up - lo), f32), p[0:16, lo:up]], 0)
        edge = jnp.where(s == 0, 0.0, two * edge[1:17] + three * edge[2:18])
        gp[total_rows : total_rows + 16, lo:up] = edge.astype(bf16)
        gp[total_rows + 16 :, lo:up] = jnp.zeros((E - 16, up - lo), bf16)

    def rows_at(j):
        return pl.ds(pl.multiple_of(j * rows, rows), rows)

    def part_of(part):
        return pl.ds(lanes[part][0], lanes[part][1] - lanes[part][0])

    def back(part):
        return remote(
            gp.at[pl.ds(total_rows, 16), part_of(part)],
            hi.at[(x + 1) % nx, :, part_of(part)],
            sh.at[part],
            qh.at[part],
            seq=prev,
            head=nx - 1,
        )

    near = rows // 2

    def out_far(part, way):
        j = (x + 2) % nx
        src = pl.ds(pl.multiple_of(j * rows + way * near, near), near)
        return remote(
            gp.at[src, part_of(part)],
            relay.at[way, :, part_of(part)],
            sr1.at[part],
            qr1.at[part, way],
            head=right if way == 0 else left,
        )

    def on_far(part, way):
        lo, up = lanes[part]
        return remote(
            relay.at[way, :, part_of(part)],
            gin.at[pl.ds(way * near, near), pl.ds(2 * width + lo, up - lo)],
            sr2.at[part],
            qr2.at[part],
            head=right if way == 0 else left,
        )

    def pass_on(part):
        for way in range(2):
            arrived(relay.at[way, :, part_of(part)], qr1.at[part, way])
            on_far(part, way).start()

    def over(part, k):
        j = (x + k) % nx
        return remote(
            gp.at[rows_at(j), part_of(part)],
            gin.at[:, pl.ds((nx - k) * width + lanes[part][0], lanes[part][1] - lanes[part][0])],
            sx.at[part],
            qx.at[part],
            head=j,
        )

    def send_rows(part):
        if part < 2:
            out_far(part, 0).start()
            out_far(part, 1).start()
        else:
            over(part, 2).start()
        over(part, 1).start()
        over(part, 3).start()
        back(part).start()

    pieces = ny * nz
    height = gwb.shape[2]
    half = height // 2
    per_step = 1024 // (2 * height)
    low_half, high_half = pl.ds(0, half), pl.ds(half, half)

    def pair(part, j):
        at = part_of(part)
        return remote(
            gwb.at[j, 1 - core, :, at], rp.at[j, :, at], sp.at[part], qp.at[part], seq=sibling
        )

    def weight_part(part):
        lo, up = lanes[part]

        def weight_step(i, carry):
            at = pl.ds(pl.multiple_of(i * 1024, 1024), 1024)
            whole = dot(gt[at, :], gp[:, lo:up]).astype(bf16)
            whole = whole.reshape(per_step, 2, height, up - lo)
            for q in range(per_step):
                gwb[i * per_step + q, :, :, lo:up] = whole[q]
                pair(part, i * per_step + q).start()
            return carry

        lax.fori_loop(0, pieces // per_step, weight_step, 0)

    def go_2a(part, k):
        to, at = (z + k) % nz, part_of(part)
        return remote(
            t.at[:, to, low_half, at],
            r2a.at[k, :, :, at],
            s2a.at[part],
            q2a.at[part],
            seq=at_seq(y, to, core),
        )

    def go_2b(part, k):
        to, at = (y + k) % ny, part_of(part)
        return remote(
            t.at[to, :, high_half, at],
            r2b.at[k, :, :, at],
            s2b.at[part],
            q2b.at[part],
            seq=at_seq(to, z, core),
        )

    def go_3a(part, k):
        to, at = (y + k) % ny, part_of(part)
        return remote(
            va.at[to, :, at],
            r3a.at[k, :, at],
            s3a.at[part],
            q3a.at[part],
            seq=at_seq(to, z, core),
        )

    def go_3b(part, k):
        to, at = (z + k) % nz, part_of(part)
        return remote(
            vb.at[to, :, at],
            r3b.at[k, :, at],
            s3b.at[part],
            q3b.at[part],
            seq=at_seq(y, to, core),
        )

    def weight_second(part):
        lo, up = lanes[part]

        def pair_sum(j, carry):
            both = gwb[j, core, :, lo:up].astype(f32) + rp[j, :, lo:up].astype(f32)
            t[j // nz, j % nz, :, lo:up] = both.astype(bf16)
            return carry

        arrived(rp.at[:, :, part_of(part)], qp.at[part])
        lax.fori_loop(0, pieces, pair_sum, 0)
        for k in range(1, max(ny, nz)):
            if k < nz:
                go_2a(part, k).start()
            if k < ny:
                go_2b(part, k).start()

    def weight_third(part):
        lo, up = lanes[part]
        at = part_of(part)
        arrived(r2a.at[pl.ds(1, nz - 1), :, :, at], q2a.at[part])
        arrived(r2b.at[pl.ds(1, ny - 1), :, :, at], q2b.at[part])
        for i in range(ny):
            total = t[i, z, 0:half, lo:up].astype(f32)
            for k in range(1, nz):
                total = total + r2a[k, i, :, lo:up].astype(f32)
            va[i, :, lo:up] = total.astype(bf16)
        for i in range(nz):
            total = t[y, i, half:, lo:up].astype(f32)
            for k in range(1, ny):
                total = total + r2b[k, i, :, lo:up].astype(f32)
            vb[i, :, lo:up] = total.astype(bf16)
        for k in range(1, max(ny, nz)):
            if k < ny:
                go_3a(part, k).start()
            if k < nz:
                go_3b(part, k).start()

    exchange_done(2)
    unpack_group(2)
    value_gradient(0)
    spread(0)
    send_rows(0)
    weight_part(0)
    exchange_done(3)
    unpack_group(3)
    value_gradient(1)
    spread(1)
    send_rows(1)
    weight_second(0)
    for b in range(nb):
        key_gradient(b)
        if b == nb // 2:
            pass_on(0)
    spread(2)
    send_rows(2)
    weight_part(1)
    pass_on(1)
    weight_second(1)
    weight_part(2)
    weight_third(0)

    steps = depth // 256
    slots = wbuf.shape[0]

    def load(i, slot):
        at = pl.ds(pl.multiple_of(i * 256, 256), 256)
        for j in range(nx - 1):
            dst = wbuf.at[slot, pl.ds(j * width, width)]
            pltpu.make_async_copy(wf.at[j, :, at], dst, sw.at[slot]).start()

    def as_many(part, count):
        return gin.at[:, pl.ds(0, count * (lanes[part][1] - lanes[part][0]))]

    def gi_out(i):
        at = pl.ds(pl.multiple_of(i * 256, 256), 256)
        return pltpu.make_async_copy(gi_v.at[:, at], gi.at[:, at], s_gi)

    step6()
    for slot in range(slots):
        load(slot, slot)
    weight_second(2)
    gin[:, :width] = gp[rows_at(x), :]
    for part in range(3):
        if part < 2:
            arrived(as_many(part, 1), qr2.at[part])
        arrived(as_many(part, 2 if part < 2 else 3), qx.at[part])

    @pl.when(x == nx - 1)
    def _():
        for part in range(3):
            arrived(hi.at[:, :, part_of(part)], qh.at[part])
        for k in range(nx):
            at = slice(k * width, (k + 1) * width)
            last = gin[rows - 16 :, at].astype(f32) + hi[k].astype(f32)
            gin[rows - 16 :, at] = last.astype(bf16)

    def input_step(i, carry):
        at = pl.ds(pl.multiple_of(i * 256, 256), 256)
        slot = i % slots
        total = dot(gin[:, :width], w[:, at])
        pltpu.make_async_copy(wbuf.at[slot], wbuf.at[slot], sw.at[slot]).wait()
        gi_v[:, at] = (total + dot(gin[:, width:], wbuf[slot])).astype(bf16)
        gi_out(i).start()

        @pl.when(i + slots < steps)
        def _():
            load(i + slots, slot)

        return carry

    lax.fori_loop(0, steps // 4, input_step, 0)
    weight_third(1)
    lax.fori_loop(steps // 4, 5 * steps // 8, input_step, 0)
    weight_third(2)
    lax.fori_loop(5 * steps // 8, steps, input_step, 0)

    for part in range(3):
        at = part_of(part)
        arrived(r3a.at[pl.ds(1, ny - 1), :, at], q3a.at[part])
        arrived(r3b.at[pl.ds(1, nz - 1), :, at], q3b.at[part])

    def put(at, total):
        for h in range(nh):
            narrow = total[:, nh * E + 2 * F * h : nh * E + 2 * F * (h + 1)]
            gw_v[at, h, :] = jnp.concatenate([narrow, total[:, h * E : (h + 1) * E]], 1)

    total = va[y].astype(f32)
    for k in range(1, ny):
        total = total + r3a[k].astype(f32)
    put(slice(0, half), total)
    total = vb[z].astype(f32)
    for k in range(1, nz):
        total = total + r3b[k].astype(f32)
    put(slice(half, height), total)
    gw_out = pltpu.make_async_copy(gw_v, gw, s_gw)
    gw_out.start()

    for part in range(3):
        at = part_of(part)
        back(part).wait_send()
        if part < 2:
            sent(as_many(part, 1), sr1.at[part])
            sent(as_many(part, 1), sr2.at[part])
        sent(as_many(part, 2 if part < 2 else 3), sx.at[part])
        sent(rp.at[:, :, at], sp.at[part])
        sent(r2a.at[pl.ds(1, nz - 1), :, :, at], s2a.at[part])
        sent(r2b.at[pl.ds(1, ny - 1), :, :, at], s2b.at[part])
        sent(r3a.at[pl.ds(1, ny - 1), :, at], s3a.at[part])
        sent(r3b.at[pl.ds(1, nz - 1), :, at], s3b.at[part])
    for e in range(4):
        sent(r1.at[e, pl.ds(0, ga - 1)], s1.at[e])
        sent(r2.at[e, pl.ds(0, gb - 1)], s2.at[e])
        sent(res.at[e, pl.ds(0, (ga - 1) * piece)], s3.at[e])
    sent(tok, s_own.at[0])
    sent(tok, s_own.at[1])

    @pl.when(x == nx - 1)
    def _():
        sent(tok.at[pl.ds(0, 16 * nx)], s_hal)

    step7()
    pltpu.make_async_copy(att_v, att, s_att).wait()
    pltpu.make_async_copy(gi_v, gi, s_gi).wait()
    gw_out.wait()


def hand_on_kernel(count, *refs):
    srcs, dsts, sems = refs[:count], refs[count : 2 * count], refs[2 * count]
    copies = [pltpu.make_async_copy(srcs[i], dsts[i], sems.at[i]) for i in range(count)]
    for copy in copies:
        copy.start()
    for copy in copies:
        copy.wait()


def hand_on(*arrays):
    hbm = pl.BlockSpec(memory_space=pl.ANY)
    count = len(arrays)
    return pl.pallas_call(
        functools.partial(hand_on_kernel, count),
        out_shape=tuple(jax.ShapeDtypeStruct(a.shape, a.dtype) for a in arrays),
        in_specs=[hbm] * count,
        out_specs=(hbm,) * count,
        scratch_shapes=[pltpu.SemaphoreType.DMA((count,))],
        compiler_params=pltpu.CompilerParams(vmem_limit_bytes=2**20),
    )(*arrays)


def local(nx, ny, nz, tokens, in_weight, conv_kernel, grad_out):
    depth, nh, _ = in_weight.shape
    wt = jnp.transpose(in_weight, (1, 2, 0)).reshape(nh * CHAN, depth)
    rows = tokens.shape[0]
    every = grad_out.shape[0]
    width = nh * CHAN
    nb = every // BLK
    n = nh * nb
    ga, gb, ns = 2 * nz, ny, 2 * ny * nz
    piece = -(-(nh // 2) * FS // (16 * ga)) * 16
    height = depth // ns
    half = height // 2
    hbm = pl.BlockSpec(memory_space=pl.ANY)
    dma = pltpu.SemaphoreType.DMA
    consts = [
        jnp.asarray(selection(True), bf16),
        jnp.asarray(selection(False), bf16),
        jnp.asarray(gradient_map(True), bf16),
        jnp.asarray(gradient_map(False), bf16),
    ]
    att, gi, gw, _ = pl.pallas_call(
        functools.partial(kernel, nx, ny, nz, nh),
        out_shape=(
            pltpu.VMEM((every, nh * E), bf16),
            pltpu.VMEM((rows, depth), bf16),
            pltpu.VMEM((height, nh, CHAN), f32),
            jax.ShapeDtypeStruct((nx - 1, width, depth), bf16),
        ),
        in_specs=[hbm] * 8,
        out_specs=(hbm, hbm, hbm, hbm),
        scratch_shapes=[
            pltpu.VMEM(conv_kernel.shape, f32),
            pltpu.VMEM((2 * FS, 3 * F), bf16),
            pltpu.VMEM((2 * FS, 3 * F), bf16),
            pltpu.VMEM((F, 2 * FS), bf16),
            pltpu.VMEM((F, 2 * FS), bf16),
            pltpu.VMEM((every, nh * E), bf16),
            pltpu.VMEM((every, nh * E), bf16),
            pltpu.VMEM((rows, depth), bf16),
            pltpu.VMEM((height, nh, CHAN), f32),
            pltpu.VMEM((width, depth), bf16),
            pltpu.VMEM((nx, rows, depth), bf16),
            pltpu.VMEM((depth, every + E), bf16),
            pltpu.VMEM((16 + every, width), f32),
            pltpu.VMEM((16, depth), bf16),
            pltpu.VMEM((8, width), f32),
            pltpu.VMEM((nh * 2 * F, every), f32),
            pltpu.VMEM((n, BLK, 2 * E), bf16),
            pltpu.VMEM((n, FS, BLK), bf16),
            pltpu.VMEM((n, FS, BLK), bf16),
            pltpu.VMEM((n, BLK, FS), bf16),
            pltpu.VMEM((n, BLK, FS), bf16),
            pltpu.VMEM((n, FS, 2 * E), f32),
            pltpu.VMEM((n, BLK, 2 * E), f32),
            pltpu.VMEM((n, BLK, BLK), bf16),
            pltpu.VMEM((n, BLK, 2 * E), bf16),
            pltpu.VMEM((nh, FS, 2 * E), f32),
            pltpu.VMEM((n, FS, 2 * E), bf16),
            pltpu.VMEM((n, FS, BLK), f32),
            pltpu.VMEM((every + E, width), bf16),
            pltpu.VMEM((4, ga * piece, E), bf16),
            pltpu.VMEM((4, ga, piece, E), bf16),
            pltpu.VMEM((4, piece, E), bf16),
            pltpu.VMEM((4, gb, piece, E), bf16),
            pltpu.VMEM((4, ga, piece, E), bf16),
            pltpu.VMEM((4, ga * piece, E), bf16),
            pltpu.VMEM((3, (nx - 1) * width, 256), bf16),
            pltpu.VMEM((rows, nx * width), bf16),
            pltpu.VMEM((2, rows // 2, nh * E), bf16),
            pltpu.VMEM((nx, 16, width), bf16),
            pltpu.VMEM((ny * nz, 2, height, width), bf16),
            pltpu.VMEM((ny * nz, height, width), bf16),
            pltpu.VMEM((ny, nz, height, width), bf16),
            pltpu.VMEM((nz, ny, half, width), bf16),
            pltpu.VMEM((ny, nz, half, width), bf16),
            pltpu.VMEM((ny, half, width), bf16),
            pltpu.VMEM((nz, half, width), bf16),
            pltpu.VMEM((ny, half, width), bf16),
            pltpu.VMEM((nz, half, width), bf16),
            dma((2,)),
            dma((2, 2)),
            dma((2,)),
            dma(()),
            dma(()),
            dma(()),
            dma(()),
            dma(()),
            dma(()),
            dma((4,)),
            dma((4,)),
            dma((4,)),
            dma((4,)),
            dma((4,)),
            dma((4,)),
            dma((3,)),
            dma((2,)),
            dma((2, 2)),
            dma((2,)),
            dma((2,)),
            dma((3,)),
            dma((3,)),
            dma((3,)),
            dma((3,)),
            dma((3,)),
            dma((3,)),
            dma((3,)),
            dma((3,)),
            dma((3,)),
            dma((3,)),
            dma((3,)),
            dma((3,)),
            dma((3,)),
            dma((3,)),
            dma(()),
            dma(()),
            dma(()),
            dma(()),
            dma((5,)),
            dma(()),
            dma(()),
            dma(()),
            dma(()),
            dma(()),
            dma(()),
            dma(()),
            dma(()),
            dma((ny,)),
            dma((ny,)),
            dma((nz,)),
            dma((nz,)),
            dma(()),
            dma(()),
            dma(()),
            dma(()),
            dma((2,)),
            dma((2,)),
        ],
        compiler_params=pltpu.CompilerParams(
            collective_id=0, has_side_effects=True, vmem_limit_bytes=60 * 2**20
        ),
    )(tokens, wt, conv_kernel, grad_out, *consts)
    return hand_on(att, gi, gw)


def solution(mesh):
    nx, ns = mesh.shape["head"], mesh.shape["seq"]
    ny = math.isqrt(ns // 2)
    nz = ns // 2 // ny
    placed = (
        P(("seq", "head"), None),
        P(None, "head", None),
        P(None, "head", None),
        P("seq", "head"),
    )
    return jax.shard_map(
        functools.partial(local, nx, ny, nz),
        mesh=mesh,
        in_specs=placed,
        out_specs=(P("seq", "head"), P(("seq", "head"), None), P("seq", "head", None)),
        check_vma=False,
    )
```

```python
import functools
import math

import jax
import jax.numpy as jnp
import numpy as np
from jax import lax
from jax.experimental import pallas as pl
from jax.experimental.pallas import tpu as pltpu
from jax.sharding import PartitionSpec as P

F = 16
E = 128
BLK = 256
CHAN = 160
FS = 160
NF = 1 + F + F * (F + 1) // 2
KAPPA = 32.0 ** -0.25
f32 = jnp.float32
bf16 = jnp.bfloat16
NN = (((1,), (0,)), ((), ()))
NT = (((1,), (1,)), ((), ()))


def dot(a, b, dims=NN):
    return lax.dot_general(a, b, dims, preferred_element_type=f32)


def bf_parts(value, count):
    parts = []
    rest = np.float64(value)
    for _ in range(count):
        part = np.float64(np.asarray(rest, dtype=jnp.bfloat16))
        parts.append(part)
        rest = rest - part
    return parts


def selection(weighted):
    sel = np.zeros((2 * FS, 3 * F), np.float64)
    sel[0, 32] = 1.0
    sel[FS, 32] = 1.0
    for i in range(F):
        row = 1 + i
        sel[row, i] = sel[row, F + i] = 1.0
        for c, part in enumerate(bf_parts(0.5 / KAPPA, 3)):
            sel[FS + row, 32 + c] = part
    row = 1 + F
    for i in range(F):
        for j in range(i, F):
            first = 2.0 if (weighted and j > i) else 1.0
            sel[row, i] = sel[row, F + i] = first
            sel[FS + row, j] = sel[FS + row, F + j] = 1.0
            row += 1
    return sel


def gradient_map(weighted):
    sel = selection(weighted)
    return np.concatenate([sel[:FS, :F].T, sel[FS:, :F].T], 1)


def remote(src, dst, send, recv, **where):
    return pltpu.make_async_remote_copy(
        src_ref=src,
        dst_ref=dst,
        send_sem=send,
        recv_sem=recv,
        device_id=where,
        device_id_type=pl.DeviceIdType.MESH,
    )


def arrived(ref, sem):
    remote(ref, ref, sem, sem, seq=lax.axis_index("seq")).wait_recv()


def sent(ref, sem):
    remote(ref, ref, sem, sem, seq=lax.axis_index("seq")).wait_send()


def greet(sem, **where):
    pl.semaphore_signal(sem, inc=1, device_id=where, device_id_type=pl.DeviceIdType.MESH)


def weight_gather(nx, ny, nz, x, y, z, core, w, wf, sems):
    s1, q1, sr, qr, sa, qa, sb, qb, sc, qc, sd, qd, sf, qf, sg, qg, se, qe = sems
    chan, depth = w.shape
    half = chan // 2
    quarter = half // 2
    eighth = quarter // 2
    col = depth // (ny * nz)
    base = core * half
    rows_c = pl.ds(pl.multiple_of(base, 16), half)
    rows_a = pl.ds(pl.multiple_of(base, 16), quarter)
    rows_b = pl.ds(pl.multiple_of(base + quarter, 16), quarter)
    far = pl.ds(0, nx - 1)

    def piece_a(n):
        return pl.ds(pl.multiple_of(base + n * eighth, 16), eighth)

    def piece_b(n):
        return pl.ds(pl.multiple_of(base + quarter + n * eighth, 16), eighth)

    def cols(yy, zz):
        return pl.ds(pl.multiple_of((yy * nz + zz) * col, 128), col)

    def row_of(yy):
        return pl.ds(pl.multiple_of(yy * nz * col, 128), nz * col)

    def at_seq(yy, zz, cc):
        return (yy * nz + zz) * 2 + cc

    mine = cols(y, z)
    ring_y = (1, ny - 1) if ny > 2 else (1,)
    ring_z = (1, nz - 1) if nz > 2 else (1,)

    def spread_x(k):
        return remote(w.at[rows_c, mine], wf.at[nx - k - 1, rows_c, mine], s1, q1, head=(x + k) % nx)

    def spread_on(k):
        here = wf.at[nx - k - 1, rows_a if k == 1 else rows_b, mine]
        there = wf.at[nx // 2 - 1, rows_a if k == 1 else rows_b, mine]
        return remote(here, there, sr, qr, head=(x + k) % nx)

    def a_z(k):
        here = wf.at[far, rows_a, mine]
        return remote(here, here, sa, qa, seq=at_seq(y, (z + k) % nz, core))

    def b_y(k):
        here = wf.at[far, rows_b, mine]
        return remote(here, here, sb, qb, seq=at_seq((y + k) % ny, z, core))

    def a_y(k):
        here = wf.at[far, rows_a, row_of(y)]
        return remote(here, here, sc.at[k], qc.at[k], seq=at_seq((y + k) % ny, z, core))

    def b_z(k, yy):
        here = wf.at[far, rows_b, cols(yy, z)]
        return remote(here, here, sd.at[k], qd.at[k], seq=at_seq(y, (z + k) % nz, core))

    def a_y_on(k):
        here = wf.at[far, piece_a(0 if k == 1 else 1), row_of((y - k) % ny)]
        return remote(here, here, sf, qf, seq=at_seq((y + k) % ny, z, core))

    def b_z_on(k, yy):
        here = wf.at[far, piece_b(0 if k == 1 else 1), cols(yy, (z - k) % nz)]
        return remote(here, here, sg, qg, seq=at_seq(y, (z + k) % nz, core))

    def across(part):
        here = wf.at[far, rows_a if part == 0 else rows_b]
        return remote(here, here, se.at[part], qe.at[part], seq=at_seq(y, z, 1 - core))

    def lanes(rows, count):
        return wf.at[far, rows, pl.ds(0, count * col)]

    def step0():
        for k in (1, nx - 1):
            spread_x(k).start()

    def step1():
        arrived(wf.at[pl.ds(0, 2), rows_c, mine], q1)
        for k in (1, nx - 1):
            spread_on(k).start()

    def step2():
        arrived(wf.at[0, rows_c, mine], qr)
        for k in range(1, max(ny, nz)):
            if k < nz:
                a_z(k).start()
            if k < ny:
                b_y(k).start()

    def step3():
        arrived(lanes(rows_a, nz - 1), qa)
        for k in ring_y:
            a_y(k).start()
        arrived(lanes(rows_b, ny - 1), qb)
        for k in ring_z:
            for yy in range(ny):
                b_z(k, yy).start()

    def step4():
        for k in ring_y:
            arrived(lanes(rows_a, nz), qc.at[ny - k])
            if ny > 2:
                a_y_on(ny - k).start()
        for k in ring_z:
            arrived(lanes(rows_b, ny), qd.at[nz - k])
            if nz > 2:
                for yy in range(ny):
                    b_z_on(nz - k, yy).start()

    def step5():
        if ny > 2:
            arrived(lanes(rows_a, nz), qf)
        across(0).start()
        if nz > 2:
            arrived(lanes(rows_b, ny), qg)
        across(1).start()

    def step6():
        across(0).wait_recv()
        across(1).wait_recv()

    def step7():
        sent(wf.at[pl.ds(0, 2), rows_c, mine], s1)
        sent(wf.at[0, rows_c, mine], sr)
        sent(lanes(rows_a, nz - 1), sa)
        sent(lanes(rows_b, ny - 1), sb)
        for k in ring_y:
            sent(lanes(rows_a, nz), sc.at[k])
        for k in ring_z:
            sent(lanes(rows_b, ny), sd.at[k])
        if ny > 2:
            sent(lanes(rows_a, nz), sf)
        if nz > 2:
            sent(lanes(rows_b, ny), sg)
        across(0).wait_send()
        across(1).wait_send()

    return step0, step1, step2, step3, step4, step5, step6, step7


def kernel(
    nx, ny, nz, nh,
    tok, wt, cv_hbm, go, selq_hbm, selk_hbm, gmq_hbm, gmk_hbm,
    att, gi, gw, wf,
    cv, selq, selk, gmq, gmk, go_v, att_v, gi_v, gw_v, w, g, gt, p, hal, taps, qkt, vaug, fqt, fkt, fq, fk, ub, nin, scot, gna, run, st, pfk, gp,
    loc, r1, tot, r2, out, res,
    wbuf, gin, relay, hi, gwb, rp, t, r2a, r2b, va, vb, r3a, r3b,
    s_own, r_own, r_rest, s_fwd, r_fwd, s_hal, r_hal, s_w, s_tok,
    s1, q1, s2, q2, s3, q3,
    sw, sr1, qr1, sr2, qr2, sx, qx, sh, qh, sp, qp, s2a, q2a, s2b, q2b, s3a, q3a, s3b, q3b, s_att, s_gi, s_gw, s_go, s_const,
    *sems,
):
    x = lax.axis_index("head")
    s = lax.axis_index("seq")
    ns = 2 * ny * nz
    core, z, y = s % 2, (s // 2) % nz, s // (2 * nz)
    left, right, opp = (x + nx - 1) % nx, (x + 1) % nx, (x + 2) % nx
    prev, after = (s + ns - 1) % ns, (s + 1) % ns
    ga, gb = 2 * nz, ny
    me_a, me_b = s % ga, s // ga
    rows, depth = tok.shape
    nb = go.shape[0] // BLK
    ch = rows // 4
    piece = loc.shape[1] // ga
    gh = nh // 2
    per = gh * nb

    def at_seq(yy, zz, cc):
        return (yy * nz + zz) * 2 + cc

    sibling = at_seq(y, z, 1 - core)
    bar = pltpu.get_barrier_semaphore()
    for k in range(1, nx):
        greet(bar, head=(x + k) % nx)
    for k in range(1, ga):
        greet(bar, seq=me_b * ga + (me_a + k) % ga)
    for k in range(1, gb):
        greet(bar, seq=((me_b + k) % gb) * ga + me_a)
    greet(bar, seq=prev)
    greet(bar, seq=after)
    greet(bar, seq=prev, head=nx - 1)

    @pl.when(x == nx - 1)
    def _():
        for j in range(nx):
            greet(bar, seq=after, head=j)

    local_tok = pltpu.make_async_copy(tok, g.at[x], s_tok)
    local_tok.start()
    local_go = pltpu.make_async_copy(go, go_v, s_go)
    local_go.start()
    small = [
        pltpu.make_async_copy(src, dst, s_const.at[i])
        for i, (src, dst) in enumerate(
            ((cv_hbm, cv), (selq_hbm, selq), (selk_hbm, selk), (gmq_hbm, gmq), (gmk_hbm, gmk))
        )
    ]
    for copy in small:
        copy.start()
    loads = []
    for h in range(nh):
        base = h * CHAN
        loads.append(
            pltpu.make_async_copy(
                wt.at[base + 2 * F : base + CHAN], w.at[h * E : (h + 1) * E], s_w
            )
        )
        loads.append(
            pltpu.make_async_copy(
                wt.at[base : base + 2 * F],
                w.at[nh * E + 2 * F * h : nh * E + 2 * F * (h + 1)],
                s_w,
            )
        )
    for copy in loads:
        copy.start()
    greeted = nx - 1 + ga - 1 + gb - 1 + 3
    pl.semaphore_wait(bar, jnp.where(x == nx - 1, greeted + nx, greeted))

    def chunk(c):
        return pl.ds(c * ch, ch)

    def own(way, c, first):
        return remote(
            tok.at[chunk(c)],
            g.at[x, chunk(c)],
            s_own.at[0 if first else 1],
            r_own.at[way, c % 2] if first else r_rest.at[way],
            head=right if way == 0 else left,
        )

    def forward(way, c):
        slot = left if way == 0 else right
        return remote(
            g.at[slot, chunk(c)],
            g.at[slot, chunk(c)],
            s_fwd,
            r_fwd,
            head=right if way == 0 else left,
        )

    def halo(j):
        return remote(tok.at[pl.ds(rows - 16, 16)], hal, s_hal, r_hal, seq=after, head=j)

    step0, step1, step2, step3, step4, step5, step6, step7 = weight_gather(
        nx, ny, nz, x, y, z, core, w, wf, sems
    )
    pltpu.make_async_copy(w, w, s_w).wait()
    step0()
    own(0, 0, True).start()
    own(1, 2, True).start()
    @pl.when(x == nx - 1)
    def _():
        for j in range(nx):
            halo(j).start()

    lane = lax.broadcasted_iota(jnp.int32, (BLK, BLK), 1)
    sub = lax.broadcasted_iota(jnp.int32, (BLK, BLK), 0)
    frow = lax.broadcasted_iota(jnp.int32, (FS, E), 0)

    for copy in small:
        copy.wait()

    for j in range(3):
        lines = [cv[j, h : h + 1, :] for h in range(nh)]
        for h in range(nh):
            taps[j : j + 1, h * E : (h + 1) * E] = lines[h][:, 2 * F :]
        taps[j : j + 1, nh * E :] = jnp.concatenate([v[:, : 2 * F] for v in lines], 1) * KAPPA

    def rows_of(a):
        return pl.ds(pl.multiple_of(a * piece, 16), piece)

    def first(e, k):
        a = (me_a + k) % ga
        return remote(
            loc.at[e, rows_of(a)], r1.at[e, me_a], s1.at[e], q1.at[e], seq=me_b * ga + a
        )

    def second(e, k):
        b = (me_b + k) % gb
        return remote(tot.at[e], r2.at[e, me_b], s2.at[e], q2.at[e], seq=b * ga + me_a)

    def third(e, k):
        a = (me_a + k) % ga
        return remote(
            out.at[e, a], res.at[e, rows_of(me_a)], s3.at[e], q3.at[e], seq=me_b * ga + a
        )

    def exchange_first(e):
        for k in range(1, ga):
            first(e, k).start()
        r1[e, me_a] = loc[e, rows_of(me_a), :]

    def exchange_second(e):
        arrived(r1.at[e, pl.ds(0, ga - 1)], q1.at[e])
        total = jnp.zeros((piece, E), f32)
        for a in range(ga):
            total = total + r1[e, a].astype(f32)
        tot[e] = total.astype(bf16)
        for k in range(1, gb):
            second(e, k).start()

    def exchange_third(e):
        arrived(r2.at[e, pl.ds(0, gb - 1)], q2.at[e])
        r2[e, me_b] = tot[e]
        total = jnp.zeros((piece, E), f32)
        for b in range(gb):
            ahead = b < me_b if e < 2 else b > me_b
            total = total + jnp.where(ahead, r2[e, b].astype(f32), 0.0)
        for step in range(ga):
            a = step if e < 2 else ga - 1 - step
            out[e, a] = total.astype(bf16)
            total = total + r1[e, a].astype(f32)
        for k in range(1, ga):
            third(e, k).start()
        res[e, rows_of(me_a), :] = out[e, me_a]

    def exchange_done(e):
        arrived(res.at[e, pl.ds(0, (ga - 1) * piece)], q3.at[e])

    def pack(e, h, whole):
        column = jnp.concatenate([whole[:, E:], jnp.zeros((2 * E - FS, E), f32)], 0)
        line = column.T[0:1, :]
        body = jnp.where(frow == NF, line[:, :E], jnp.where(frow == NF + 1, line[:, E:], whole[:, :E]))
        loc[e, h * FS : (h + 1) * FS, :] = body.astype(bf16)

    def pack_group(e):
        for j in range(gh):
            h = (e % 2) * gh + j
            whole = ub[h * nb]
            for b in range(1, nb):
                whole = whole + ub[h * nb + b]
            pack(e, j, whole)
        if gh * FS < loc.shape[1]:
            loc[e, gh * FS :, :] = jnp.zeros((loc.shape[1] - gh * FS, E), bf16)

    def unpack_group(e):
        for j in range(gh):
            body = res[e, j * FS : (j + 1) * FS, :].astype(f32)
            line = jnp.concatenate([body[NF : NF + 1, :], body[NF + 1 : NF + 2, :]], 1)
            column = jnp.broadcast_to(line, (E, 2 * E)).T[:FS, :]
            run[(e % 2) * gh + j] = jnp.concatenate([jnp.where(frow < NF, body, 0.0), column], 1)

    def factors(u, sel):
        high = u.astype(bf16)
        low = (u - high.astype(f32)).astype(bf16)
        stack = jnp.concatenate([high, low, jnp.ones((F, BLK), bf16)], 0)
        both = dot(sel[...], stack)
        return both[:FS], both[FS:]

    def block_at(b):
        return pl.ds(pl.multiple_of(b * BLK, BLK), BLK)

    def convolve(b):
        ext = p[pl.ds(pl.multiple_of(b * BLK, BLK), BLK + 16), :]
        conv = taps[0:1, :] * ext[16:] + taps[1:2, :] * ext[15:-1] + taps[2:3, :] * ext[14:-2]
        qkt[:, block_at(b)] = conv[:, nh * E :].T
        for h in range(nh):
            vaug[h * nb + b] = jnp.concatenate(
                [conv[:, h * E : (h + 1) * E].astype(bf16), jnp.ones((BLK, E), bf16)], 1
            )

    def featurize(b, group):
        for j in range(gh):
            h = group * gh + j
            i = h * nb + b
            at = block_at(b)
            first_q, second_q = factors(qkt[2 * F * h : 2 * F * h + F, at], selq)
            first_k, second_k = factors(qkt[2 * F * h + F : 2 * F * (h + 1), at], selk)
            q = (first_q * second_q).astype(bf16)
            k = (first_k * second_k).astype(bf16)
            fqt[i] = q
            fkt[i] = k
            fq[i] = q.T
            fk[i] = k.T
            ub[i] = dot(k, vaug[i])

    def project(slot):
        base = pl.multiple_of(slot * rows, rows)
        p[pl.ds(16 + base, rows), :] = dot(g[slot], w[...], NT)

    def turn(slot):
        base = pl.multiple_of(slot * rows, rows)

        def piece_of(i, carry):
            at = pl.ds(pl.multiple_of(i * 256, 256), 256)
            gt[at, pl.ds(base, rows)] = g[slot, :, at].T
            return carry

        lax.fori_loop(0, depth // 256, piece_of, 0)

    local_tok.wait()
    project(x)
    turn(x)
    step1()
    own(0, 1, True).start()
    own(1, 3, True).start()
    own(0, 2, False).start()
    own(1, 0, False).start()
    own(0, 3, False).start()
    own(1, 1, False).start()
    step2()
    for c in range(2):
        arrived(g.at[left, chunk(c)], r_own.at[0, c])
        forward(0, c).start()
        arrived(g.at[right, chunk(c + 2)], r_own.at[1, c])
        forward(1, c + 2).start()
    step3()
    arrived(hal, r_hal)
    head_rows = dot(hal[...], w[...], NT)
    p[0:16, :] = jnp.where(s == 0, 0.0, head_rows)

    def turn_halo(i, carry):
        at = pl.ds(pl.multiple_of(i * 256, 256), 256)
        tail_rows = jnp.concatenate([hal[:, at], jnp.zeros((E - 16, 256), bf16)], 0)
        gt[at, nb * BLK :] = tail_rows.T
        return carry

    lax.fori_loop(0, depth // 256, turn_halo, 0)
    arrived(g.at[left, pl.ds(0, 2 * ch)], r_rest.at[0])
    project(left)
    arrived(g.at[right, pl.ds(0, 2 * ch)], r_rest.at[1])
    project(right)
    step4()
    for b in (x, right):
        convolve(b)
        featurize(b, 0)
        featurize(b, 1)
    turn(left)
    turn(right)
    arrived(g.at[opp], r_fwd)
    project(opp)
    for b in (opp, left):
        convolve(b)
        featurize(b, 0)
    pack_group(0)
    exchange_first(0)
    for b in (opp, left):
        featurize(b, 1)
    pack_group(1)
    exchange_first(1)

    def inside(i):
        score = jnp.where(sub >= lane, dot(fq[i], fkt[i]), 0.0).astype(bf16)
        scot[i] = jnp.where(lane >= sub, dot(fk[i], fqt[i]), 0.0).astype(bf16)
        nin[i] = dot(score, vaug[i])

    fold = g.shape[2] // BLK

    def raw_at(i):
        return (i // fold, slice(None), slice(i % fold * BLK, (i % fold + 1) * BLK))

    def inside_raw(i):
        h, b = i // nb, i % nb
        cot = go_v[b * BLK : (b + 1) * BLK, h * E : (h + 1) * E]
        g[raw_at(i)] = dot(cot, vaug[i, :, :E], NT).astype(bf16)

    def quarter(n, body):
        for i in range(n * per // 2, (n + 1) * per // 2):
            body(i)

    turn(opp)
    local_go.wait()
    quarter(0, inside)
    exchange_second(0)
    quarter(1, inside)
    exchange_second(1)
    quarter(2, inside)
    exchange_third(0)
    exchange_third(1)
    quarter(3, inside)
    sent(g.at[opp], s_fwd)
    for n in range(4):
        quarter(n, inside_raw)

    ones = jnp.ones((E, E), bf16)

    def attend(group):
        for b in range(nb):
            for j in range(gh):
                h = group * gh + j
                i = h * nb + b
                state = run[h]
                state_b = state.astype(bf16)
                run[h] = state + ub[i]
                both = dot(fq[i], state_b) + nin[i]
                num = both[:, :E]
                inv = 1.0 / both[:, E:]
                mean = num * inv
                at = (slice(b * BLK, (b + 1) * BLK), slice(h * E, (h + 1) * E))
                att_v[at] = mean.astype(bf16)
                scaled = go_v[at].astype(f32) * inv
                product = scaled * mean
                slope = dot(product.astype(bf16), ones) * (-1.0 / E)
                ga_b = jnp.concatenate([scaled.astype(bf16), slope.astype(bf16)], 1)
                gna[i] = ga_b
                nin[i, :, E:] = inv
                st[i] = state_b
                ub[i] = dot(fqt[i], ga_b)
        pack_group(2 + group)

    def att_out(group):
        at = pl.ds(group * gh * E, gh * E)
        return pltpu.make_async_copy(att_v.at[:, at], att.at[:, at], s_att)

    for group in range(2):
        exchange_done(group)
        unpack_group(group)
        attend(group)
        exchange_first(2 + group)
        att_out(group).start()

    def feature_gradient(u, sel, gm, grad):
        one, two = factors(u, sel)
        stack = jnp.concatenate([(grad * two).astype(bf16), (grad * one).astype(bf16)], 0)
        return dot(gm[...], stack)

    def inside_back(i):
        h, b = i // nb, i % nb
        ga_b = gna[i]
        inv = nin[i, :, E:]
        slope = ga_b[:, E:].astype(f32) * float(E)
        scaled = g[raw_at(i)].astype(f32) * jnp.concatenate([inv, inv], 1)
        mix = scaled + jnp.concatenate([slope, slope], 1)
        mix = jnp.where(sub >= lane, mix, 0.0).astype(bf16)
        mixt = mix.T
        gfq = dot(st[i], ga_b, NT) + dot(fkt[i], mixt)
        at = (slice(h * 2 * F, h * 2 * F + F), slice(b * BLK, (b + 1) * BLK))
        gq = feature_gradient(qkt[at], selq, gmq, gfq)
        pfk[i] = dot(fqt[i], mix)
        qkt[at] = gq
        nin[i, :, :E] = dot(scot[i], ga_b[:, :E])

    step5()
    exchange_second(2)
    quarter(0, inside_back)
    quarter(1, inside_back)
    exchange_second(3)
    exchange_third(2)
    quarter(2, inside_back)
    quarter(3, inside_back)
    exchange_third(3)

    def value_gradient(group):
        for b in reversed(range(nb)):
            for j in range(gh):
                h = group * gh + j
                i = h * nb + b
                state = run[h]
                state_b = state.astype(bf16)
                st[i] = state_b
                run[h] = state + ub[i]
                rows_b = slice(b * BLK, (b + 1) * BLK)
                p[rows_b, h * E : (h + 1) * E] = dot(fk[i], state_b[:, :E]) + nin[i, :, :E]

    def key_gradient(b):
        rows_b = slice(b * BLK, (b + 1) * BLK)
        for h in range(nh):
            i = h * nb + b
            gfk = dot(st[i], vaug[i], NT) + pfk[i]
            at = (slice(2 * F * h + F, 2 * F * (h + 1)), rows_b)
            qkt[at] = feature_gradient(qkt[at], selk, gmk, gfk)
        p[rows_b, nh * E :] = qkt[:, rows_b].T

    total_rows = nb * BLK
    width = gp.shape[1]
    lanes = ((0, gh * E), (gh * E, nh * E), (nh * E, width))

    def spread(part):
        lo, up = lanes[part]
        one, two, three = taps[0:1, lo:up], taps[1:2, lo:up], taps[2:3, lo:up]
        p[total_rows:, lo:up] = jnp.zeros((16, up - lo), f32)
        for b in range(nb):
            ext = p[b * BLK : (b + 1) * BLK + 16, lo:up]
            grad = one * ext[:BLK] + two * ext[1 : BLK + 1] + three * ext[2 : BLK + 2]
            gp[b * BLK : (b + 1) * BLK, lo:up] = grad.astype(bf16)
        edge = jnp.concatenate([jnp.zeros((16, up - lo), f32), p[0:16, lo:up]], 0)
        edge = jnp.where(s == 0, 0.0, two * edge[1:17] + three * edge[2:18])
        gp[total_rows : total_rows + 16, lo:up] = edge.astype(bf16)
        gp[total_rows + 16 :, lo:up] = jnp.zeros((E - 16, up - lo), bf16)

    def rows_at(j):
        return pl.ds(pl.multiple_of(j * rows, rows), rows)

    def part_of(part):
        return pl.ds(lanes[part][0], lanes[part][1] - lanes[part][0])

    def back(part):
        return remote(
            gp.at[pl.ds(total_rows, 16), part_of(part)],
            hi.at[(x + 1) % nx, :, part_of(part)],
            sh.at[part],
            qh.at[part],
            seq=prev,
            head=nx - 1,
        )

    near = rows // 2

    def out_far(part, way):
        j = (x + 2) % nx
        src = pl.ds(pl.multiple_of(j * rows + way * near, near), near)
        return remote(
            gp.at[src, part_of(part)],
            relay.at[way, :, part_of(part)],
            sr1.at[part],
            qr1.at[part, way],
            head=right if way == 0 else left,
        )

    def on_far(part, way):
        lo, up = lanes[part]
        return remote(
            relay.at[way, :, part_of(part)],
            gin.at[pl.ds(way * near, near), pl.ds(2 * width + lo, up - lo)],
            sr2.at[part],
            qr2.at[part],
            head=right if way == 0 else left,
        )

    def pass_on(part):
        for way in range(2):
            arrived(relay.at[way, :, part_of(part)], qr1.at[part, way])
            on_far(part, way).start()

    def over(part, k):
        j = (x + k) % nx
        return remote(
            gp.at[rows_at(j), part_of(part)],
            gin.at[:, pl.ds((nx - k) * width + lanes[part][0], lanes[part][1] - lanes[part][0])],
            sx.at[part],
            qx.at[part],
            head=j,
        )

    def send_rows(part):
        if part < 2:
            out_far(part, 0).start()
            out_far(part, 1).start()
        else:
            over(part, 2).start()
        over(part, 1).start()
        over(part, 3).start()
        back(part).start()

    pieces = ny * nz
    height = gwb.shape[2]
    half = height // 2
    per_step = 1024 // (2 * height)
    low_half, high_half = pl.ds(0, half), pl.ds(half, half)

    def pair(part, j):
        at = part_of(part)
        return remote(
            gwb.at[j, 1 - core, :, at], rp.at[j, :, at], sp.at[part], qp.at[part], seq=sibling
        )

    def weight_part(part):
        lo, up = lanes[part]

        def weight_step(i, carry):
            at = pl.ds(pl.multiple_of(i * 1024, 1024), 1024)
            whole = dot(gt[at, :], gp[:, lo:up]).astype(bf16)
            whole = whole.reshape(per_step, 2, height, up - lo)
            for q in range(per_step):
                gwb[i * per_step + q, :, :, lo:up] = whole[q]
                pair(part, i * per_step + q).start()
            return carry

        lax.fori_loop(0, pieces // per_step, weight_step, 0)

    def go_2a(part, k):
        to, at = (z + k) % nz, part_of(part)
        return remote(
            t.at[:, to, low_half, at],
            r2a.at[k, :, :, at],
            s2a.at[part],
            q2a.at[part],
            seq=at_seq(y, to, core),
        )

    def go_2b(part, k):
        to, at = (y + k) % ny, part_of(part)
        return remote(
            t.at[to, :, high_half, at],
            r2b.at[k, :, :, at],
            s2b.at[part],
            q2b.at[part],
            seq=at_seq(to, z, core),
        )

    def go_3a(part, k):
        to, at = (y + k) % ny, part_of(part)
        return remote(
            va.at[to, :, at],
            r3a.at[k, :, at],
            s3a.at[part],
            q3a.at[part],
            seq=at_seq(to, z, core),
        )

    def go_3b(part, k):
        to, at = (z + k) % nz, part_of(part)
        return remote(
            vb.at[to, :, at],
            r3b.at[k, :, at],
            s3b.at[part],
            q3b.at[part],
            seq=at_seq(y, to, core),
        )

    def weight_second(part):
        lo, up = lanes[part]

        def pair_sum(j, carry):
            both = gwb[j, core, :, lo:up].astype(f32) + rp[j, :, lo:up].astype(f32)
            t[j // nz, j % nz, :, lo:up] = both.astype(bf16)
            return carry

        arrived(rp.at[:, :, part_of(part)], qp.at[part])
        lax.fori_loop(0, pieces, pair_sum, 0)
        for k in range(1, max(ny, nz)):
            if k < nz:
                go_2a(part, k).start()
            if k < ny:
                go_2b(part, k).start()

    def weight_third(part):
        lo, up = lanes[part]
        at = part_of(part)
        arrived(r2a.at[pl.ds(1, nz - 1), :, :, at], q2a.at[part])
        arrived(r2b.at[pl.ds(1, ny - 1), :, :, at], q2b.at[part])
        for i in range(ny):
            total = t[i, z, 0:half, lo:up].astype(f32)
            for k in range(1, nz):
                total = total + r2a[k, i, :, lo:up].astype(f32)
            va[i, :, lo:up] = total.astype(bf16)
        for i in range(nz):
            total = t[y, i, half:, lo:up].astype(f32)
            for k in range(1, ny):
                total = total + r2b[k, i, :, lo:up].astype(f32)
            vb[i, :, lo:up] = total.astype(bf16)
        for k in range(1, max(ny, nz)):
            if k < ny:
                go_3a(part, k).start()
            if k < nz:
                go_3b(part, k).start()

    exchange_done(2)
    unpack_group(2)
    value_gradient(0)
    spread(0)
    send_rows(0)
    weight_part(0)
    exchange_done(3)
    unpack_group(3)
    value_gradient(1)
    spread(1)
    send_rows(1)
    weight_second(0)
    for b in range(nb):
        key_gradient(b)
        if b == nb // 2:
            pass_on(0)
    spread(2)
    send_rows(2)
    weight_part(1)
    pass_on(1)
    weight_second(1)
    weight_part(2)
    weight_third(0)

    steps = depth // 256
    slots = wbuf.shape[0]

    def load(i, slot):
        at = pl.ds(pl.multiple_of(i * 256, 256), 256)
        for j in range(nx - 1):
            dst = wbuf.at[slot, pl.ds(j * width, width)]
            pltpu.make_async_copy(wf.at[j, :, at], dst, sw.at[slot]).start()

    def as_many(part, count):
        return gin.at[:, pl.ds(0, count * (lanes[part][1] - lanes[part][0]))]

    def gi_out(i):
        at = pl.ds(pl.multiple_of(i * 256, 256), 256)
        return pltpu.make_async_copy(gi_v.at[:, at], gi.at[:, at], s_gi)

    step6()
    for slot in range(slots):
        load(slot, slot)
    weight_second(2)
    gin[:, :width] = gp[rows_at(x), :]
    for part in range(3):
        if part < 2:
            arrived(as_many(part, 1), qr2.at[part])
        arrived(as_many(part, 2 if part < 2 else 3), qx.at[part])

    @pl.when(x == nx - 1)
    def _():
        for part in range(3):
            arrived(hi.at[:, :, part_of(part)], qh.at[part])
        for k in range(nx):
            at = slice(k * width, (k + 1) * width)
            last = gin[rows - 16 :, at].astype(f32) + hi[k].astype(f32)
            gin[rows - 16 :, at] = last.astype(bf16)

    def input_step(i, carry):
        at = pl.ds(pl.multiple_of(i * 256, 256), 256)
        slot = i % slots
        total = dot(gin[:, :width], w[:, at])
        pltpu.make_async_copy(wbuf.at[slot], wbuf.at[slot], sw.at[slot]).wait()
        gi_v[:, at] = (total + dot(gin[:, width:], wbuf[slot])).astype(bf16)
        gi_out(i).start()

        @pl.when(i + slots < steps)
        def _():
            load(i + slots, slot)

        return carry

    lax.fori_loop(0, steps // 4, input_step, 0)
    weight_third(1)
    lax.fori_loop(steps // 4, 5 * steps // 8, input_step, 0)
    weight_third(2)
    lax.fori_loop(5 * steps // 8, steps, input_step, 0)

    for part in range(3):
        at = part_of(part)
        arrived(r3a.at[pl.ds(1, ny - 1), :, at], q3a.at[part])
        arrived(r3b.at[pl.ds(1, nz - 1), :, at], q3b.at[part])

    def put(at, total):
        for h in range(nh):
            narrow = total[:, nh * E + 2 * F * h : nh * E + 2 * F * (h + 1)]
            gw_v[at, h, :] = jnp.concatenate([narrow, total[:, h * E : (h + 1) * E]], 1)

    total = va[y].astype(f32)
    for k in range(1, ny):
        total = total + r3a[k].astype(f32)
    put(slice(0, half), total)
    total = vb[z].astype(f32)
    for k in range(1, nz):
        total = total + r3b[k].astype(f32)
    put(slice(half, height), total)
    gw_out = pltpu.make_async_copy(gw_v, gw, s_gw)
    gw_out.start()

    for part in range(3):
        at = part_of(part)
        back(part).wait_send()
        if part < 2:
            sent(as_many(part, 1), sr1.at[part])
            sent(as_many(part, 1), sr2.at[part])
        sent(as_many(part, 2 if part < 2 else 3), sx.at[part])
        sent(rp.at[:, :, at], sp.at[part])
        sent(r2a.at[pl.ds(1, nz - 1), :, :, at], s2a.at[part])
        sent(r2b.at[pl.ds(1, ny - 1), :, :, at], s2b.at[part])
        sent(r3a.at[pl.ds(1, ny - 1), :, at], s3a.at[part])
        sent(r3b.at[pl.ds(1, nz - 1), :, at], s3b.at[part])
    for e in range(4):
        sent(r1.at[e, pl.ds(0, ga - 1)], s1.at[e])
        sent(r2.at[e, pl.ds(0, gb - 1)], s2.at[e])
        sent(res.at[e, pl.ds(0, (ga - 1) * piece)], s3.at[e])
    sent(tok, s_own.at[0])
    sent(tok, s_own.at[1])

    @pl.when(x == nx - 1)
    def _():
        sent(tok.at[pl.ds(0, 16 * nx)], s_hal)

    step7()
    pltpu.make_async_copy(att_v, att, s_att).wait()
    pltpu.make_async_copy(gi_v, gi, s_gi).wait()
    gw_out.wait()


def hand_on_kernel(count, *refs):
    srcs, dsts, sems = refs[:count], refs[count : 2 * count], refs[2 * count]
    copies = [pltpu.make_async_copy(srcs[i], dsts[i], sems.at[i]) for i in range(count)]
    for copy in copies:
        copy.start()
    for copy in copies:
        copy.wait()


def hand_on(*arrays):
    hbm = pl.BlockSpec(memory_space=pl.ANY)
    count = len(arrays)
    return pl.pallas_call(
        functools.partial(hand_on_kernel, count),
        out_shape=tuple(jax.ShapeDtypeStruct(a.shape, a.dtype) for a in arrays),
        in_specs=[hbm] * count,
        out_specs=(hbm,) * count,
        scratch_shapes=[pltpu.SemaphoreType.DMA((count,))],
        compiler_params=pltpu.CompilerParams(vmem_limit_bytes=2**20),
    )(*arrays)


def local(nx, ny, nz, tokens, in_weight, conv_kernel, grad_out):
    depth, nh, _ = in_weight.shape
    wt = jnp.transpose(in_weight, (1, 2, 0)).reshape(nh * CHAN, depth)
    rows = tokens.shape[0]
    every = grad_out.shape[0]
    width = nh * CHAN
    nb = every // BLK
    n = nh * nb
    ga, gb, ns = 2 * nz, ny, 2 * ny * nz
    piece = -(-(nh // 2) * FS // (16 * ga)) * 16
    height = depth // ns
    half = height // 2
    hbm = pl.BlockSpec(memory_space=pl.ANY)
    dma = pltpu.SemaphoreType.DMA
    consts = [
        jnp.asarray(selection(True), bf16),
        jnp.asarray(selection(False), bf16),
        jnp.asarray(gradient_map(True), bf16),
        jnp.asarray(gradient_map(False), bf16),
    ]
    att, gi, gw, _ = pl.pallas_call(
        functools.partial(kernel, nx, ny, nz, nh),
        out_shape=(
            pltpu.VMEM((every, nh * E), bf16),
            pltpu.VMEM((rows, depth), bf16),
            pltpu.VMEM((height, nh, CHAN), f32),
            jax.ShapeDtypeStruct((nx - 1, width, depth), bf16),
        ),
        in_specs=[hbm] * 8,
        out_specs=(hbm, hbm, hbm, hbm),
        scratch_shapes=[
            pltpu.VMEM(conv_kernel.shape, f32),
            pltpu.VMEM((2 * FS, 3 * F), bf16),
            pltpu.VMEM((2 * FS, 3 * F), bf16),
            pltpu.VMEM((F, 2 * FS), bf16),
            pltpu.VMEM((F, 2 * FS), bf16),
            pltpu.VMEM((every, nh * E), bf16),
            pltpu.VMEM((every, nh * E), bf16),
            pltpu.VMEM((rows, depth), bf16),
            pltpu.VMEM((height, nh, CHAN), f32),
            pltpu.VMEM((width, depth), bf16),
            pltpu.VMEM((nx, rows, depth), bf16),
            pltpu.VMEM((depth, every + E), bf16),
            pltpu.VMEM((16 + every, width), f32),
            pltpu.VMEM((16, depth), bf16),
            pltpu.VMEM((8, width), f32),
            pltpu.VMEM((nh * 2 * F, every), f32),
            pltpu.VMEM((n, BLK, 2 * E), bf16),
            pltpu.VMEM((n, FS, BLK), bf16),
            pltpu.VMEM((n, FS, BLK), bf16),
            pltpu.VMEM((n, BLK, FS), bf16),
            pltpu.VMEM((n, BLK, FS), bf16),
            pltpu.VMEM((n, FS, 2 * E), f32),
            pltpu.VMEM((n, BLK, 2 * E), f32),
            pltpu.VMEM((n, BLK, BLK), bf16),
            pltpu.VMEM((n, BLK, 2 * E), bf16),
            pltpu.VMEM((nh, FS, 2 * E), f32),
            pltpu.VMEM((n, FS, 2 * E), bf16),
            pltpu.VMEM((n, FS, BLK), f32),
            pltpu.VMEM((every + E, width), bf16),
            pltpu.VMEM((4, ga * piece, E), bf16),
            pltpu.VMEM((4, ga, piece, E), bf16),
            pltpu.VMEM((4, piece, E), bf16),
            pltpu.VMEM((4, gb, piece, E), bf16),
            pltpu.VMEM((4, ga, piece, E), bf16),
            pltpu.VMEM((4, ga * piece, E), bf16),
            pltpu.VMEM((4, (nx - 1) * width, 256), bf16),
            pltpu.VMEM((rows, nx * width), bf16),
            pltpu.VMEM((2, rows // 2, nh * E), bf16),
            pltpu.VMEM((nx, 16, width), bf16),
            pltpu.VMEM((ny * nz, 2, height, width), bf16),
            pltpu.VMEM((ny * nz, height, width), bf16),
            pltpu.VMEM((ny, nz, height, width), bf16),
            pltpu.VMEM((nz, ny, half, width), bf16),
            pltpu.VMEM((ny, nz, half, width), bf16),
            pltpu.VMEM((ny, half, width), bf16),
            pltpu.VMEM((nz, half, width), bf16),
            pltpu.VMEM((ny, half, width), bf16),
            pltpu.VMEM((nz, half, width), bf16),
            dma((2,)),
            dma((2, 2)),
            dma((2,)),
            dma(()),
            dma(()),
            dma(()),
            dma(()),
            dma(()),
            dma(()),
            dma((4,)),
            dma((4,)),
            dma((4,)),
            dma((4,)),
            dma((4,)),
            dma((4,)),
            dma((4,)),
            dma((2,)),
            dma((2, 2)),
            dma((2,)),
            dma((2,)),
            dma((3,)),
            dma((3,)),
            dma((3,)),
            dma((3,)),
            dma((3,)),
            dma((3,)),
            dma((3,)),
            dma((3,)),
            dma((3,)),
            dma((3,)),
            dma((3,)),
            dma((3,)),
            dma((3,)),
            dma((3,)),
            dma(()),
            dma(()),
            dma(()),
            dma(()),
            dma((5,)),
            dma(()),
            dma(()),
            dma(()),
            dma(()),
            dma(()),
            dma(()),
            dma(()),
            dma(()),
            dma((ny,)),
            dma((ny,)),
            dma((nz,)),
            dma((nz,)),
            dma(()),
            dma(()),
            dma(()),
            dma(()),
            dma((2,)),
            dma((2,)),
        ],
        compiler_params=pltpu.CompilerParams(
            collective_id=0, has_side_effects=True, vmem_limit_bytes=60 * 2**20
        ),
    )(tokens, wt, conv_kernel, grad_out, *consts)
    return hand_on(att, gi, gw)


def solution(mesh):
    nx, ns = mesh.shape["head"], mesh.shape["seq"]
    ny = math.isqrt(ns // 2)
    nz = ns // 2 // ny
    placed = (
        P(("seq", "head"), None),
        P(None, "head", None),
        P(None, "head", None),
        P("seq", "head"),
    )
    return jax.shard_map(
        functools.partial(local, nx, ny, nz),
        mesh=mesh,
        in_specs=placed,
        out_specs=(P("seq", "head"), P(("seq", "head"), None), P("seq", "head", None)),
        check_vma=False,
    )
```
